128 devices in a mesh: dp: 32 (over x_lo, z, y), mp: 4 (over x_hi, core).
Axes of the slice: x: 4 (x_hi: 2, x_lo: 2; x = x_hi * 2 + x_lo), y: 4, z: 4, core: 2. Of those that a mesh axis runs over, the one named last changes fastest.
Arguments:
- tokens: bfloat16 [16384, 2048], P(('dp', 'mp')), may hold values from -6 to 6
- cotangent: bfloat16 [16384, 2048], P(('dp', 'mp')), may hold values from -7.5 to 7.5
- doc_lengths: int32 [32, 4], P('dp'), may hold values from 1 to 385, 512 in all within a row
- row_owner: int32 [32], replicated, may hold values from 0 to 31, each once
- norm_params: float32 [2, 2048], replicated, may hold values from -1.2 to 1.75, as said below
- norm_moment1: float32 [2, 2048], replicated
- norm_moment2: float32 [2, 2048], replicated, as said below
- qkv_weight: float32 [2048, 6144], P('dp', 'mp'), may hold values from -0.125 to 0.125
- out_weight: float32 [2048, 2048], P('dp', 'mp')
- gate_weight: float32 [2048, 5632], P('dp', 'mp'), may hold values from -0.125 to 0.125
- up_weight: float32 [2048, 5632], P('dp', 'mp'), may hold values from -0.125 to 0.125
- down_weight: float32 [2048, 5632], P('dp', 'mp')
- qkv_moment1: float32 [2048, 6144], P('dp', 'mp')
- out_moment1: float32 [2048, 2048], P('dp', 'mp')
- gate_moment1: float32 [2048, 5632], P('dp', 'mp')
- up_moment1: float32 [2048, 5632], P('dp', 'mp')
- down_moment1: float32 [2048, 5632], P('dp', 'mp')
- qkv_moment2: float32 [2048, 6144], P('dp', 'mp'), as said below
- out_moment2: float32 [2048, 2048], P('dp', 'mp'), as said below
- gate_moment2: float32 [2048, 5632], P('dp', 'mp'), as said below
- up_moment2: float32 [2048, 5632], P('dp', 'mp'), as said below
- down_moment2: float32 [2048, 5632], P('dp', 'mp'), as said below
- qkv_basis: float32 [48, 128, 128], P('mp'), may hold values from -0.5 to 0.5
- out_basis: float32 [16, 128, 128], P('mp'), may hold values from -0.5 to 0.5
- gate_basis: float32 [44, 128, 128], P('mp'), may hold values from -0.5 to 0.5
- up_basis: float32 [44, 128, 128], P('mp'), may hold values from -0.5 to 0.5
- down_basis: float32 [44, 128, 128], P('mp'), may hold values from -0.5 to 0.5
Outputs:
- out: bfloat16 [16384, 2048], P(('dp', 'mp'))
- input_grad: bfloat16 [16384, 2048], P(('dp', 'mp'))
- grad_norm: float32 [], replicated
- norm_grads: float32 [2, 2048], replicated
- norm_moment1_new: float32 [2, 2048], replicated
- norm_moment2_new: float32 [2, 2048], replicated
- norm_params_new: float32 [2, 2048], replicated
- qkv_grad: float32 [2048, 6144], P('dp', 'mp')
- out_grad: float32 [2048, 2048], P('dp', 'mp')
- gate_grad: float32 [2048, 5632], P('dp', 'mp')
- up_grad: float32 [2048, 5632], P('dp', 'mp')
- down_grad: float32 [2048, 5632], P('dp', 'mp')
- qkv_moment1_new: float32 [2048, 6144], P('dp', 'mp')
- out_moment1_new: float32 [2048, 2048], P('dp', 'mp')
- gate_moment1_new: float32 [2048, 5632], P('dp', 'mp')
- up_moment1_new: float32 [2048, 5632], P('dp', 'mp')
- down_moment1_new: float32 [2048, 5632], P('dp', 'mp')
- qkv_moment2_new: float32 [2048, 6144], P('dp', 'mp')
- out_moment2_new: float32 [2048, 2048], P('dp', 'mp')
- gate_moment2_new: float32 [2048, 5632], P('dp', 'mp')
- up_moment2_new: float32 [2048, 5632], P('dp', 'mp')
- down_moment2_new: float32 [2048, 5632], P('dp', 'mp')
- qkv_new: float32 [2048, 6144], P('dp', 'mp')
- out_new: float32 [2048, 2048], P('dp', 'mp')
- gate_new: float32 [2048, 5632], P('dp', 'mp')
- up_new: float32 [2048, 5632], P('dp', 'mp')
- down_new: float32 [2048, 5632], P('dp', 'mp')
The draws below stay inside these ranges and needn't reach their ends.
Inputs may be any that keep to these rules, and one draw needn't show every extreme that they name: `doc_lengths`: one document of each sequence has exactly 385 tokens. `row_owner`: each value once. `norm_params`: gains positive. `norm_moment2`: positive. `qkv_moment2`: positive. `out_moment2`: positive. `gate_moment2`: positive. `up_moment2`: positive. `down_moment2`: positive.
All inputs are finite; a program needn't handle non-finite values.
Results may differ from the reference program's by a relative error of at most 0.005.
The reference program's roundings to bfloat16 on the way count: a program that leaves them out, or rounds other values in their place, can miss the bound.
Values may be sent and summed in bfloat16 or wider, within the bound.
A program may use at most 256 MiB of HBM per device.

```python
import math
import jax
import jax.numpy as jnp
import numpy as np
from jax import lax

D = 2048
HEADS = 32
HEAD_DIM = 64
ROT = 16
FF = 5632
LEN = 512
DOCS = 4
BASIS = 128
STEP = 5
TOKENS = 16384
N_DP = 32


def rising(count, start):
    return start + jnp.arange(count, dtype=jnp.float32) / count


def grad_scale(factor):
    return factor / (3.0 * D * D + 0.4 * D * FF) ** 0.5


def first_moment(key, shape, factor):
    sign_key, size_key = jax.random.split(key)
    signs = jnp.where(jax.random.bernoulli(sign_key, 0.5, shape), 1.0, -1.0)
    sizes = jnp.exp(jax.random.uniform(size_key, shape, jnp.float32, jnp.log(0.5), jnp.log(2.0)))
    return signs * sizes * grad_scale(factor)


def second_moment(key, shape, factor):
    sizes = jnp.exp(jax.random.uniform(key, shape, jnp.float32, 0.0, jnp.log(4.0)))
    return sizes * grad_scale(factor) ** 2


def draw_cotangent(key, part):
    key = jax.random.fold_in(key, 1)
    base = jnp.clip(jax.random.normal(key, (TOKENS, D), jnp.float32), -5.0, 5.0)
    return (base * rising(D, 0.5)[None, :]).astype(jnp.bfloat16)


def draw_norm_params(key, part):
    key = jax.random.fold_in(key, 2)
    gain_key, bias_key = jax.random.split(key)
    gains = rising(D, 0.5) * jax.random.uniform(gain_key, (D,), jnp.float32, 0.85, 1.15)
    biases = 0.3 * jnp.clip(jax.random.normal(bias_key, (D,), jnp.float32), -4.0, 4.0)
    return jnp.stack([gains, biases])


def draw_norm_moment1(key, part):
    key = jax.random.fold_in(key, 3)
    return first_moment(key, (2, D), 2.0)


def draw_norm_moment2(key, part):
    key = jax.random.fold_in(key, 4)
    return second_moment(key, (2, D), 2.0)


def draw_out_weight(key, part):
    key = jax.random.fold_in(key, 5)
    base = jnp.clip(jax.random.normal(key, (D, D), jnp.float32), -5.0, 5.0)
    return base * rising(D, 0.5)[None, :] / (D // 16) ** 0.5


def draw_down_weight(key, part):
    key = jax.random.fold_in(key, 6)
    base = jnp.clip(jax.random.normal(key, (D, FF), jnp.float32), -5.0, 5.0)
    return base * rising(FF, 0.5)[None, :] / FF ** 0.5


def draw_qkv_moment1(key, part):
    key = jax.random.fold_in(key, 11)
    return first_moment(key, (D, 3 * D), 1.0)


def draw_out_moment1(key, part):
    key = jax.random.fold_in(key, 12)
    return first_moment(key, (D, D), 0.3)


def draw_gate_moment1(key, part):
    key = jax.random.fold_in(key, 13)
    return first_moment(key, (D, FF), 0.4)


def draw_up_moment1(key, part):
    key = jax.random.fold_in(key, 14)
    return first_moment(key, (D, FF), 0.4)


def draw_down_moment1(key, part):
    key = jax.random.fold_in(key, 15)
    return first_moment(key, (D, FF), 0.4)


def draw_qkv_moment2(key, part):
    key = jax.random.fold_in(key, 21)
    return second_moment(key, (D, 3 * D), 1.0)


def draw_out_moment2(key, part):
    key = jax.random.fold_in(key, 22)
    return second_moment(key, (D, D), 0.3)


def draw_gate_moment2(key, part):
    key = jax.random.fold_in(key, 23)
    return second_moment(key, (D, FF), 0.4)


def draw_up_moment2(key, part):
    key = jax.random.fold_in(key, 24)
    return second_moment(key, (D, FF), 0.4)


def draw_down_moment2(key, part):
    key = jax.random.fold_in(key, 25)
    return second_moment(key, (D, FF), 0.4)


def block_levels(own_key, extent, shards, smallest, top_value):
    level = 1.0
    for axis_at, shards_of in shards:
        heights = jax.random.uniform(jax.random.fold_in(jax.random.fold_in(own_key, 6), axis_at), (shards_of,), jnp.float32, smallest / len(shards), top_value / len(shards))
        level = level * jnp.repeat(jnp.exp(heights), extent[axis_at] // shards_of).reshape((-1,) + (1,) * (len(extent) - 1 - axis_at))
    return level


def split_up(count, total, limit, slope):
    loads = [(1 << 20) // math.isqrt(rank ** slope) + 1 for rank in range(2, count + 1)]
    rest, given = total - limit - (count - 1), [1] * (count - 1)
    while rest > 0:
        candidates = [i for i in range(count - 1) if given[i] < limit]
        pool, budget = sum([loads[i] for i in candidates]), rest
        for i in candidates:
            addition = min(limit - given[i], max(1, budget * loads[i] // pool), rest)
            given[i] = given[i] + addition
            rest = rest - addition
    return np.array([limit] + given)


def ragged_sizes(own_key, count, total, limit, lean):
    if count == 2:
        one = jax.random.randint(own_key, (), max(1, total - limit), min(limit, total - 1) + 1)
        return jnp.stack([one, total - one])
    sizes = jnp.asarray(split_up(count, total, limit, lean), jnp.int32)
    twos = (count - 1) // 2
    giver, sink = sizes[1:1 + 2 * twos:2], sizes[2:2 + 2 * twos:2]
    room = jnp.minimum(giver - 1, limit - sink)
    shifted = jax.random.randint(jax.random.fold_in(own_key, 1), (twos,), 0, 1 << 20) % (room + 1)
    sizes = sizes.at[1:1 + 2 * twos:2].set(giver - shifted).at[2:2 + 2 * twos:2].set(sink + shifted)
    return sizes[jax.random.permutation(jax.random.fold_in(own_key, 2), count)]


def bell_draw(rng, dims, width, reach, cuts=(), held_as=jnp.bfloat16):
    entries = jax.random.normal(rng, dims, jnp.float32) * width
    if len(cuts) > 0:
        entries = block_levels(rng, dims, cuts, -0.22, 0.18) * entries
    return jnp.clip(entries, min=-reach, max=reach).astype(held_as)


def setup_inputs(seed: int = 0) -> dict:
    streams_of = jax.random.split(jax.random.key(seed), 28)
    tokens = bell_draw(streams_of[0], (TOKENS, D), 1.0, 6.0, ((0, 128),))
    cotangent = draw_cotangent(jax.random.fold_in(streams_of[27], 71), 0)
    doc_lengths = jax.vmap(lambda own: ragged_sizes(own, DOCS, LEN, 3 * LEN // 4 + 1, 0))(jax.random.split(streams_of[2], N_DP)).reshape((N_DP, DOCS)).astype(jnp.int32)
    row_owner = jax.random.permutation(streams_of[3], N_DP).astype(jnp.int32)
    norm_params = draw_norm_params(jax.random.fold_in(streams_of[27], 71), 0)
    norm_moment1 = draw_norm_moment1(jax.random.fold_in(streams_of[27], 71), 0)
    norm_moment2 = draw_norm_moment2(jax.random.fold_in(streams_of[27], 71), 0)
    qkv_weight = bell_draw(streams_of[7], (D, 3 * D), D ** -0.5, 0.125, ((0, 32), (1, 4)), jnp.float32)
    out_weight = draw_out_weight(jax.random.fold_in(streams_of[27], 71), 0)
    gate_weight = bell_draw(streams_of[9], (D, FF), D ** -0.5, 0.125, ((0, 32), (1, 4)), jnp.float32)
    up_weight = bell_draw(streams_of[10], (D, FF), D ** -0.5, 0.125, ((0, 32), (1, 4)), jnp.float32)
    down_weight = draw_down_weight(jax.random.fold_in(streams_of[27], 71), 0)
    qkv_moment1 = draw_qkv_moment1(jax.random.fold_in(streams_of[27], 71), 0)
    out_moment1 = draw_out_moment1(jax.random.fold_in(streams_of[27], 71), 0)
    gate_moment1 = draw_gate_moment1(jax.random.fold_in(streams_of[27], 71), 0)
    up_moment1 = draw_up_moment1(jax.random.fold_in(streams_of[27], 71), 0)
    down_moment1 = draw_down_moment1(jax.random.fold_in(streams_of[27], 71), 0)
    qkv_moment2 = draw_qkv_moment2(jax.random.fold_in(streams_of[27], 71), 0)
    out_moment2 = draw_out_moment2(jax.random.fold_in(streams_of[27], 71), 0)
    gate_moment2 = draw_gate_moment2(jax.random.fold_in(streams_of[27], 71), 0)
    up_moment2 = draw_up_moment2(jax.random.fold_in(streams_of[27], 71), 0)
    down_moment2 = draw_down_moment2(jax.random.fold_in(streams_of[27], 71), 0)
    qkv_basis = bell_draw(streams_of[22], (3 * D // BASIS, BASIS, BASIS), BASIS ** -0.5, 0.5, ((0, 4),), jnp.float32)
    out_basis = bell_draw(streams_of[23], (D // BASIS, BASIS, BASIS), BASIS ** -0.5, 0.5, ((0, 4),), jnp.float32)
    gate_basis = bell_draw(streams_of[24], (FF // BASIS, BASIS, BASIS), BASIS ** -0.5, 0.5, ((0, 4),), jnp.float32)
    up_basis = bell_draw(streams_of[25], (FF // BASIS, BASIS, BASIS), BASIS ** -0.5, 0.5, ((0, 4),), jnp.float32)
    down_basis = bell_draw(streams_of[26], (FF // BASIS, BASIS, BASIS), BASIS ** -0.5, 0.5, ((0, 4),), jnp.float32)
    return {"tokens": tokens, "cotangent": cotangent, "doc_lengths": doc_lengths, "row_owner": row_owner, "norm_params": norm_params, "norm_moment1": norm_moment1, "norm_moment2": norm_moment2, "qkv_weight": qkv_weight, "out_weight": out_weight, "gate_weight": gate_weight, "up_weight": up_weight, "down_weight": down_weight, "qkv_moment1": qkv_moment1, "out_moment1": out_moment1, "gate_moment1": gate_moment1, "up_moment1": up_moment1, "down_moment1": down_moment1, "qkv_moment2": qkv_moment2, "out_moment2": out_moment2, "gate_moment2": gate_moment2, "up_moment2": up_moment2, "down_moment2": down_moment2, "qkv_basis": qkv_basis, "out_basis": out_basis, "gate_basis": gate_basis, "up_basis": up_basis, "down_basis": down_basis}


@jax.custom_vjp
def lower_precision(v):
    return lax.optimization_barrier(v.astype(jnp.bfloat16)).astype(jnp.float32)

@jax.custom_vjp
def low_back(v):
    return v

def low_keep(v):
    return (lower_precision(v), None)

def low_pass(kept, grad):
    return (grad,)

def back_keep(v):
    return (v, None)

def back_low(kept, grad):
    return (lower_precision(grad),)
lower_precision.defvjp(low_keep, low_pass)
low_back.defvjp(back_keep, back_low)
NORM_EPSILON = 1e-05
BETA_ONE = 0.5
BETA_TWO = 0.5
ADAM_EPS = 1e-08
WEIGHT_DECAY = 0.01
RATE_LIST = (0.02, 0.1, 0.02, 0.02, 0.015)
NORM_RATE = 0.2
CLIP_LIMIT = 1.0
MASK_FILL = -1e+30
PRECISE = lax.Precision.HIGHEST

def dense(left, right):
    return jnp.dot(left, right, precision=PRECISE, preferred_element_type=jnp.float32)

def doc_layout(lengths, total):
    ends = jnp.cumsum(lengths).astype(jnp.int32)
    index = jnp.arange(total, dtype=jnp.int32)
    passed = (index[:, None] >= ends[None, :]).astype(jnp.int32)
    doc_ids = lax.optimization_barrier(jnp.sum(passed, 1)).astype(jnp.int32)
    starts = lax.optimization_barrier(jnp.sum(passed * lengths[None, :], 1)).astype(jnp.int32)
    return (doc_ids, index - starts, index)

def turn_angles(positions):
    half = ROT // 2
    freq = 10000.0 ** (-2.0 * jnp.arange(half, dtype=jnp.float32) / ROT)
    angle = positions.astype(jnp.float32)[:, None] * freq[None, :]
    return (jnp.cos(angle)[:, None, :], jnp.sin(angle)[:, None, :])

def rotate(field, cosine, sine):
    half = ROT // 2
    lead_half = field[..., :half]
    tail_half = field[..., half:ROT]
    return jnp.concatenate([lead_half * cosine - tail_half * sine, tail_half * cosine + lead_half * sine, field[..., ROT:]], -1)

def true_rows(weight, order):
    return weight.reshape(N_DP, -1, weight.shape[1])[order].reshape(weight.shape)

def soap_update(weight, grad, first, second, basis, rate):
    rows, cols = grad.shape
    blocks = basis.shape[0]
    turned = jnp.einsum('rbi,bij->rbj', grad.reshape(rows, blocks, -1), basis, precision=PRECISE).reshape(rows, cols)
    first_new = BETA_ONE * first + (1.0 - BETA_ONE) * turned
    second_new = BETA_TWO * second + (1.0 - BETA_TWO) * turned * turned
    ratio = first_new / (1.0 - BETA_ONE ** STEP) / (jnp.sqrt(second_new / (1.0 - BETA_TWO ** STEP)) + ADAM_EPS)
    back = jnp.einsum('rbj,bij->rbi', ratio.reshape(rows, blocks, -1), basis, precision=PRECISE).reshape(rows, cols)
    return (first_new, second_new, weight - rate * (back + WEIGHT_DECAY * weight))

def adam_plain(param, grad, first, second, rate):
    first_new = BETA_ONE * first + (1.0 - BETA_ONE) * grad
    second_new = BETA_TWO * second + (1.0 - BETA_TWO) * grad * grad
    ratio = first_new / (1.0 - BETA_ONE ** STEP) / (jnp.sqrt(second_new / (1.0 - BETA_TWO ** STEP)) + ADAM_EPS)
    return (first_new, second_new, param - rate * ratio)

def layer(rows, norm_gain, norm_shift, w_qkv, w_out, w_gate, w_up, w_down, doc_ids, positions, index):
    row_mean = lax.optimization_barrier(jnp.mean(rows, -1, keepdims=True))
    centered_input = rows - row_mean
    row_variance = lax.optimization_barrier(jnp.mean(centered_input * centered_input, -1, keepdims=True))
    standardized_input = centered_input * lax.rsqrt(row_variance + NORM_EPSILON)
    normed_output = lower_precision(standardized_input * norm_gain + norm_shift)
    qkv = low_back(dense(normed_output, w_qkv)).reshape(LEN, HEADS, 3, HEAD_DIM)
    cosine, sine = turn_angles(positions)
    scale = 1.0 / math.sqrt(HEAD_DIM)
    queries = lower_precision(rotate(qkv[:, :, 0], cosine, sine) * scale)
    key_rows = lower_precision(rotate(qkv[:, :, 1], cosine, sine))
    value_rows = lower_precision(qkv[:, :, 2])
    scores = low_back(jnp.einsum('qhd,khd->hqk', queries, key_rows, precision=PRECISE))
    allowed = (doc_ids[:, None] == doc_ids[None, :]) & (index[:, None] >= index[None, :])
    scores = jnp.where(allowed[None], scores, MASK_FILL)
    attn_probs = lower_precision(jax.nn.softmax(scores, -1))
    attn = jnp.einsum('hqk,khd->qhd', attn_probs, value_rows, precision=PRECISE).reshape(LEN, D)
    attn = lower_precision(low_back(attn))
    gate_pre = low_back(dense(normed_output, w_gate))
    up_pre = low_back(dense(normed_output, w_up))
    hidden = lower_precision(jax.nn.silu(gate_pre) * up_pre)
    branch = dense(attn, w_out.T) + dense(hidden, w_down.T)
    return rows + branch

def reference(tokens, cotangent, doc_lengths, row_owner, norm_params, norm_moment1, norm_moment2, qkv_weight, out_weight, gate_weight, up_weight, down_weight, qkv_moment1, out_moment1, gate_moment1, up_moment1, down_moment1, qkv_moment2, out_moment2, gate_moment2, up_moment2, down_moment2, qkv_basis, out_basis, gate_basis, up_basis, down_basis):
    masters = (qkv_weight, out_weight, gate_weight, up_weight, down_weight)
    copies = tuple((lower_precision(true_rows(weight, row_owner)) for weight in masters))
    inputs = tokens.astype(jnp.float32).reshape(N_DP, LEN, D)
    grads_in = cotangent.astype(jnp.float32).reshape(N_DP, LEN, D)

    def one_sequence(totals, packed):
        seq_rows, seq_grad, lengths = packed
        doc_ids, positions, index = doc_layout(lengths, LEN)

        def forward(rows, norm_gain, norm_shift, w_qkv, w_out, w_gate, w_up, w_down):
            return layer(rows, norm_gain, norm_shift, w_qkv, w_out, w_gate, w_up, w_down, doc_ids, positions, index)
        result, pull = jax.vjp(forward, seq_rows, norm_params[0], norm_params[1], *copies)
        grads = pull(seq_grad)
        totals = tuple((total + grad for total, grad in zip(totals, grads[1:])))
        return (totals, (result, grads[0]))
    start = tuple((jnp.zeros_like(item) for item in (norm_params[0], norm_params[1]) + copies))
    totals, (results, input_grads) = lax.scan(one_sequence, start, (inputs, grads_in, doc_lengths))
    out = results.reshape(TOKENS, D).astype(jnp.bfloat16)
    input_grad = input_grads.reshape(TOKENS, D).astype(jnp.bfloat16)
    norm_raw = jnp.stack([totals[0], totals[1]])
    inverse = jnp.argsort(row_owner).astype(jnp.int32)
    stored = [true_rows(grad, inverse) for grad in totals[2:]]
    square = jnp.sum(norm_raw * norm_raw)
    for grad in stored:
        square = square + jnp.sum(grad * grad)
    grad_norm = jnp.sqrt(square)
    clip = jnp.minimum(1.0, CLIP_LIMIT / grad_norm)
    norm_grads = clip * norm_raw
    norm_first, norm_second, norm_new = adam_plain(norm_params, norm_grads, norm_moment1, norm_moment2, NORM_RATE)
    firsts = (qkv_moment1, out_moment1, gate_moment1, up_moment1, down_moment1)
    seconds = (qkv_moment2, out_moment2, gate_moment2, up_moment2, down_moment2)
    bases = (qkv_basis, out_basis, gate_basis, up_basis, down_basis)
    clipped = [clip * grad for grad in stored]
    updates = [soap_update(masters[i], clipped[i], firsts[i], seconds[i], bases[i], RATE_LIST[i]) for i in range(5)]
    return (out, input_grad, grad_norm, norm_grads, norm_first, norm_second, norm_new, clipped[0], clipped[1], clipped[2], clipped[3], clipped[4], updates[0][0], updates[1][0], updates[2][0], updates[3][0], updates[4][0], updates[0][1], updates[1][1], updates[2][1], updates[3][1], updates[4][1], updates[0][2], updates[1][2], updates[2][2], updates[3][2], updates[4][2])
```

```python
import math

import jax
import jax.numpy as jnp
from jax import lax
from jax.experimental import pallas as pl
from jax.experimental.pallas import tpu as pltpu
from jax.sharding import PartitionSpec as P

MESH = pl.DeviceIdType.MESH
BF = jnp.bfloat16
F32 = jnp.float32

HEAD_DIM = 64
ROT = 16
STEP = 5

NORM_EPSILON = 1e-05
BETA_ONE = 0.5
BETA_TWO = 0.5
ADAM_EPS = 1e-08
WEIGHT_DECAY = 0.01
RATE_LIST = (0.02, 0.1, 0.02, 0.02, 0.015)
NORM_RATE = 0.2
CLIP_LIMIT = 1.0
MASK_FILL = -1e30
PRECISE = lax.Precision.HIGHEST
ROWS_DIMS = (((0,), (0,)), ((), ()))
COLS_DIMS = (((1,), (1,)), ((), ()))

D = 2048
LEN = 512
ROWS = 64
TOK = 128
GROUP = 1024
HEADS = 4
CA = 2176
CB = 1024
CHUNKS = ((0, 0, 512), (0, 512, 512), (0, 1024, 512), (0, 1536, 640), (1, 0, 512), (1, 512, 512))


def place():
    dp = lax.axis_index("dp")
    mp = lax.axis_index("mp")
    return (mp // 2) * 2 + dp // 16, dp % 4, (dp // 4) % 4, mp % 2


def device(x, y, z, c):
    return ((x % 2) * 16 + z * 4 + y, (x // 2) * 2 + c)


def near(me, name):
    x, y, z, c = me
    return {
        "y+": lambda: device(x, (y + 1) % 4, z, c),
        "y-": lambda: device(x, (y + 3) % 4, z, c),
        "z+": lambda: device(x, y, (z + 1) % 4, c),
        "z-": lambda: device(x, y, (z + 3) % 4, c),
        "x+": lambda: device((x + 1) % 4, y, z, c),
        "x-": lambda: device((x + 3) % 4, y, z, c),
        "c": lambda: device(x, y, z, 1 - c),
        "p": lambda: device((x // 2) * 2 + 1 - x % 2, y, z, c),
    }[name]()


NEIGHBOURS = ("y+", "y-", "z+", "z-", "x+", "x-", "c")


def greet(me):
    barrier = pltpu.get_barrier_semaphore()
    for name in NEIGHBOURS:
        pl.semaphore_signal(barrier, inc=1, device_id=near(me, name), device_id_type=MESH)
    pl.semaphore_wait(barrier, len(NEIGHBOURS))


class Wires:
    def __init__(self, me, send, recv):
        self.me, self.send, self.recv = me, send, recv
        self.count = 0
        self.open = []

    def push(self, src, dst, name, at=None):
        if at is None:
            at = self.count
            self.count += 1
        copy = pltpu.make_async_remote_copy(
            src, dst, self.send.at[at], self.recv.at[at], device_id=near(self.me, name), device_id_type=MESH
        )
        copy.start()
        self.open.append(copy)
        return copy

    def take(self, number):
        at = self.count
        self.count += number
        return at

    def close(self):
        for copy in self.open:
            copy.wait_send()


def gather_kernel(own_a, own_b, tok, doc, wall_a, wall_b, toks, docs, send, recv, keep):
    me = x, y, z, c = place()
    xlo, xhi = x % 2, x // 2
    wires = Wires(me, send, recv)
    pairs = ((own_a, wall_a), (own_b, wall_b))
    locals_ = []

    def local(src, dst):
        copy = pltpu.make_async_copy(src, dst, keep.at[len(locals_)])
        copy.start()
        locals_.append(copy)

    greet(me)
    four = ("y+", "y-", "z+", "z-")
    first = wires.take(16)

    def own_at(i, half, d):
        return first + i * 8 + half * 4 + d

    for i, (own, wall) in enumerate(pairs):
        for d, name in enumerate(four):
            wires.push(own.at[xlo], wall.at[xlo, z, y], name, own_at(i, xlo, d))
    swaps = [wires.push(own.at[1 - xlo], wall.at[xlo, z, y], "p") for own, wall in pairs]
    doc_swap = wires.push(doc, docs.at[xlo], "p")
    local(doc, docs.at[xlo])
    for own, wall in pairs:
        local(own.at[xlo], wall.at[xlo, z, y])
    tok_x = {}
    tok_c = []
    for k in range(2):
        for name in ("x+", "x-"):
            tok_x[k, name] = wires.push(tok.at[k], toks.at[k, xlo, xhi, c], name)
        tok_c.append(wires.push(tok.at[k], toks.at[k, xlo, xhi, c], "c"))
        local(tok.at[k], toks.at[k, xlo, xhi, c])
    for i, (own, wall) in enumerate(pairs):
        swaps[i].wait_recv()
        for d, name in enumerate(four):
            mine = wall.at[1 - xlo, z, y]
            wires.push(mine, mine, name, own_at(i, 1 - xlo, d))

    axes = (("y+", "y-", "z+", "z-"), ("z+", "z-", "y+", "y-"))

    def block(wall, half, a, b):
        return wall.at[0, b, a] if half == 0 else wall.at[1, a, b]

    def spots(half):
        return (y, z) if half == 0 else (z, y)

    def wait_own(i, half, name):
        wall = pairs[i][1]
        mine = wall.at[half, z, y]
        at = own_at(i, half, four.index(name))
        pltpu.make_async_remote_copy(
            mine, mine, send.at[at], recv.at[at], device_id=near(me, name), device_id_type=MESH
        ).wait_recv()

    lo, hi = pl.ds(0, ROWS // 2), pl.ds(ROWS // 2, ROWS // 2)
    forwards, seconds = {}, {}
    for i, (own, wall) in enumerate(pairs):
        for half in range(2):
            a, b = spots(half)
            f_up, f_down, s_up, s_down = axes[half]
            wait_own(i, half, f_up)
            got = block(wall, half, (a + 3) % 4, b)
            forwards[i, half, 0] = wires.push(got.at[lo], got.at[lo], f_up)
            wait_own(i, half, f_down)
            other = block(wall, half, (a + 1) % 4, b)
            forwards[i, half, 1] = wires.push(other.at[hi], other.at[hi], f_down)
            for j, item in ((1, got), (2, other)):
                seconds[i, half, j, 0] = wires.push(item, item, s_up)
                seconds[i, half, j, 1] = wires.push(item, item, s_down)
    tok_f = {}
    for k in range(2):
        for n, name in enumerate(("x+", "x-")):
            tok_x[k, name].wait_recv()
            sx = (x + 3) % 4 if n == 0 else (x + 1) % 4
            got = toks.at[k, sx % 2, sx // 2, c]
            part = got.at[pl.ds(n * (TOK // 2), TOK // 2)]
            tok_f[k, n] = wires.push(part, part, name)
            tok_c.append(wires.push(got, got, "c"))
    for i, (own, wall) in enumerate(pairs):
        for half in range(2):
            a, b = spots(half)
            f_up, f_down, s_up, s_down = axes[half]
            forwards[i, half, 0].wait_recv()
            forwards[i, half, 1].wait_recv()
            item = block(wall, half, (a + 2) % 4, b)
            seconds[i, half, 3, 0] = wires.push(item, item, s_up)
            seconds[i, half, 3, 1] = wires.push(item, item, s_down)
    lasts = []
    for j, step in enumerate((0, 3, 1, 2)):
        for i, (own, wall) in enumerate(pairs):
            for half in range(2):
                a, b = spots(half)
                f_up, f_down, s_up, s_down = axes[half]
                spot = (a + step) % 4
                for n, name in ((0, s_up), (1, s_down)):
                    if j == 0:
                        wait_own(i, half, name)
                    else:
                        seconds[i, half, j, n].wait_recv()
                    got = block(wall, half, spot, (b + 3) % 4 if n == 0 else (b + 1) % 4)
                    part = got.at[lo if n == 0 else hi]
                    lasts.append(wires.push(part, part, name))
        if j == 1:
            for k in range(2):
                tok_f[k, 0].wait_recv()
                tok_f[k, 1].wait_recv()
                sx = (x + 2) % 4
                got = toks.at[k, sx % 2, sx // 2, c]
                tok_c.append(wires.push(got, got, "c"))
    for copy in lasts:
        copy.wait_recv()
    for copy in tok_c:
        copy.wait_recv()
    doc_swap.wait_recv()
    wires.close()
    for copy in locals_:
        copy.wait()


def gather_all(own_a, own_b, tok, doc):
    any_ = pl.BlockSpec(memory_space=pl.ANY)
    return pl.pallas_call(
        gather_kernel,
        out_shape=(
            jax.ShapeDtypeStruct((2, 4, 4, ROWS, CA), BF),
            jax.ShapeDtypeStruct((2, 4, 4, ROWS, CB), BF),
            jax.ShapeDtypeStruct((2, 2, 2, 2, TOK, D), BF),
            jax.ShapeDtypeStruct((2, 8, 128), F32),
        ),
        in_specs=[any_] * 4,
        out_specs=(any_,) * 4,
        scratch_shapes=[
            pltpu.SemaphoreType.DMA((160,)),
            pltpu.SemaphoreType.DMA((160,)),
            pltpu.SemaphoreType.DMA((8,)),
        ],
        compiler_params=pltpu.CompilerParams(collective_id=0, has_side_effects=True),
    )(own_a, own_b, tok, doc)


def add_rows(dst, src, rows, cols):
    def step(g, carry):
        at = pl.ds(pl.multiple_of(g * 16, 16), 16)
        dst[at, cols] = (dst[at, cols].astype(F32) + src[at, cols].astype(F32)).astype(dst.dtype)
        return carry

    lax.fori_loop(0, rows // 16, step, 0)


def scatter_kernel(
    part_a, part_b, branch, grad_a, grad_b, tok_out,
    o1_a, o1_b, o3_a, o3_b, r1_a, r1_b, r2_a, r2_b, t1_a, t1_b, t2_a, t2_b, sum_a, sum_b,
    own, core, x1, x2, send, recv, keep,
):
    me = x, y, z, c = place()
    xlo = x % 2
    wires = Wires(me, send, recv)
    parts, grads = (part_a, part_b), (grad_a, grad_b)
    o1, o3, r1, r2 = (o1_a, o1_b), (o3_a, o3_b), (r1_a, r1_b), (r2_a, r2_b)
    t1, t2, sums = (t1_a, t1_b), (t2_a, t2_b), (sum_a, sum_b)
    kept = []
    late = []

    def local(src, dst):
        copy = pltpu.make_async_copy(src, dst, keep.at[len(kept)])
        copy.start()
        kept.append(copy)
        return copy

    greet(me)
    axes = (("z+", "z-", "y+", "y-"), ("y+", "y-", "z+", "z-"))

    def spots(half):
        return (z, y) if half == 0 else (y, z)

    def piece(half, chunk, spot, start, size):
        i, c0, cn = chunk
        cols = pl.ds(c0, cn)
        if half == 0:
            return parts[i].at[0, spot, pl.ds(start, size), :, cols]
        return parts[i].at[1, pl.ds(start, size), spot, :, cols]

    state = {}

    def tokens_start():
        for k in range(2):
            state["c", k] = wires.push(branch.at[k, :, :, 1 - c], core.at[k], "c")
            state["l", k] = local(branch.at[k, :, :, c], own.at[k])

    def stage0(n, half):
        chunk = i, c0, cn = CHUNKS[n]
        p, q = spots(half)
        up, down = axes[half][:2]
        cols = pl.ds(c0, cn)
        state["a", n, half, 0] = wires.push(
            piece(half, chunk, (p + 2) % 4, 0, 2), r1[i].at[half, 0, :, :, cols], up
        )
        state["a", n, half, 1] = wires.push(
            piece(half, chunk, (p + 2) % 4, 2, 2), r1[i].at[half, 1, :, :, cols], down
        )
        state["o", n, half, 0] = local(piece(half, chunk, (p + 1) % 4, 0, 2), o1[i].at[half, 0, :, :, cols])
        state["o", n, half, 1] = local(piece(half, chunk, (p + 3) % 4, 2, 2), o1[i].at[half, 1, :, :, cols])
        state["b", n, half, 0] = wires.push(
            piece(half, chunk, (p + 1) % 4, 2, 2), r2[i].at[half, 0, pl.ds(2, 2), :, cols], up
        )
        state["b", n, half, 1] = wires.push(
            piece(half, chunk, (p + 3) % 4, 0, 2), r2[i].at[half, 1, pl.ds(0, 2), :, cols], down
        )
        state["o3", n, half] = local(piece(half, chunk, p, 0, 4), o3[i].at[half, :, :, cols])

    def stage1(n, half):
        i, c0, cn = CHUNKS[n]
        cols = pl.ds(c0, cn)
        for d in range(2):
            state["a", n, half, d].wait_recv()
            state["o", n, half, d].wait()
            for m in range(2):
                add_rows(o1[i].at[half, d, m], r1[i].at[half, d, m], ROWS, cols)
            state["s", n, half, d] = wires.push(
                o1[i].at[half, d, :, :, cols], r2[i].at[half, d, pl.ds(2 * d, 2), :, cols], axes[half][d]
            )

    def stage2(n, half):
        i, c0, cn = CHUNKS[n]
        cols = pl.ds(c0, cn)
        p, q = spots(half)
        up, down = axes[half][2:]
        for d in range(2):
            state["b", n, half, d].wait_recv()
            state["s", n, half, d].wait_recv()
        state["o3", n, half].wait()

        def step(g, carry):
            at = pl.ds(pl.multiple_of((g % 4) * 16, 16), 16)
            m = g // 4
            total = (
                o3[i][half, m, at, cols].astype(F32)
                + r2[i][half, 0, m, at, cols].astype(F32)
                + r2[i][half, 1, m, at, cols].astype(F32)
            )
            o3[i][half, m, at, cols] = total.astype(BF)
            return carry

        lax.fori_loop(0, 16, step, 0)
        far = o3[i].at[half, (q + 2) % 4]
        lo, hi = pl.ds(0, ROWS // 2), pl.ds(ROWS // 2, ROWS // 2)
        state["t", n, half, 0] = wires.push(far.at[lo, cols], t1[i].at[half, 0, :, cols], up)
        state["t", n, half, 1] = wires.push(far.at[hi, cols], t1[i].at[half, 1, :, cols], down)
        state["u", n, half, 0] = wires.push(
            o3[i].at[half, (q + 1) % 4, hi, cols], t2[i].at[half, 0, hi, cols], up
        )
        state["u", n, half, 1] = wires.push(
            o3[i].at[half, (q + 3) % 4, lo, cols], t2[i].at[half, 1, lo, cols], down
        )

    def stage3(n, half):
        i, c0, cn = CHUNKS[n]
        cols = pl.ds(c0, cn)
        p, q = spots(half)
        for d in range(2):
            state["t", n, half, d].wait_recv()
            rows = pl.ds(d * (ROWS // 2), ROWS // 2)
            spot = (q + 1) % 4 if d == 0 else (q + 3) % 4
            mine = o3[i].at[half, spot, rows]
            add_rows(mine, t1[i].at[half, d], ROWS // 2, cols)
            state["v", n, half, d] = wires.push(
                mine.at[:, cols], t2[i].at[half, d, rows, cols], axes[half][2 + d]
            )

    def stage4(n, half):
        i, c0, cn = CHUNKS[n]
        cols = pl.ds(c0, cn)
        p, q = spots(half)
        for d in range(2):
            state["u", n, half, d].wait_recv()
            state["v", n, half, d].wait_recv()

        def step(g, carry):
            at = pl.ds(pl.multiple_of(g * 16, 16), 16)
            total = (
                o3[i][half, q, at, cols].astype(F32)
                + t2[i][half, 0, at, cols].astype(F32)
                + t2[i][half, 1, at, cols].astype(F32)
            )
            sums[i][half, at, cols] = total
            return carry

        lax.fori_loop(0, ROWS // 16, step, 0)

    def stage5(n):
        i, c0, cn = CHUNKS[n]
        cols = pl.ds(c0, cn)
        state["g", n] = wires.push(sums[i].at[1 - xlo, :, cols], grads[i].at[xlo, :, cols], "p")
        late.append(local(sums[i].at[xlo, :, cols], grads[i].at[xlo, :, cols]))

    half_tok = TOK // 2

    def tokens1(k):
        state["c", k].wait_recv()
        state["l", k].wait()

        def step(g, carry):
            at = pl.ds(pl.multiple_of((g % 8) * 16, 16), 16)
            s = g // 8
            own[k, s // 2, s % 2, at, :] = (
                own[k, s // 2, s % 2, at, :].astype(F32) + core[k, s // 2, s % 2, at, :].astype(F32)
            ).astype(BF)
            return carry

        lax.fori_loop(0, 32, step, 0)

        def spot(s, d, far):
            rows = pl.ds((d if far else 1 - d) * half_tok, half_tok)
            return own.at[k, s % 2, s // 2, rows]

        for d, name in enumerate(("x+", "x-")):
            state["x1", k, d] = wires.push(spot((x + 2) % 4, d, True), x1.at[k, d], name)
        for d, name in enumerate(("x+", "x-")):
            to = (x + 1) % 4 if d == 0 else (x + 3) % 4
            rows = pl.ds((1 - d) * half_tok, half_tok)
            state["x2", k, d] = wires.push(spot(to, d, False), x2.at[k, d, rows], name)

    def tokens2(k):
        for d, name in enumerate(("x+", "x-")):
            state["x1", k, d].wait_recv()
            to = (x + 1) % 4 if d == 0 else (x + 3) % 4
            rows = pl.ds(d * half_tok, half_tok)
            mine = own.at[k, to % 2, to // 2, rows]
            add_rows(mine, x1.at[k, d], half_tok, pl.ds(0, D))
            state["x3", k, d] = wires.push(mine, x2.at[k, d, rows], name)

    def tokens3(k):
        for d in range(2):
            state["x2", k, d].wait_recv()
            state["x3", k, d].wait_recv()

        def step(g, carry):
            at = pl.ds(pl.multiple_of(g * 16, 16), 16)
            tok_out[k, at, :] = (
                own[k, xlo, x // 2, at, :].astype(F32)
                + x2[k, 0, at, :].astype(F32)
                + x2[k, 1, at, :].astype(F32)
            )
            return carry

        lax.fori_loop(0, TOK // 16, step, 0)

    tokens_start()
    stages = (stage1, stage2, stage3, stage4)
    total = len(CHUNKS)
    for t in range(-1, total + 5):
        if t + 1 < total:
            for half in range(2):
                stage0(t + 1, half)
        for s, stage in enumerate(stages):
            n = t - s
            if 0 <= n < total:
                for half in range(2):
                    stage(n, half)
        if 0 <= t - 3 < total:
            stage5(t - 3)
        if t in (0, 1):
            tokens1(t)
        if t in (2, 3):
            tokens2(t - 2)
        if t in (4, 5):
            tokens3(t - 4)
    for n in range(total):
        state["g", n].wait_recv()
    wires.close()
    for copy in late:
        copy.wait()


def scatter_all(part_a, part_b, branch):
    any_ = pl.BlockSpec(memory_space=pl.ANY)
    vmem = pl.BlockSpec(memory_space=pltpu.VMEM)

    def both(*shape, dtype=BF):
        return [pltpu.VMEM(shape + (CA,), dtype), pltpu.VMEM(shape + (CB,), dtype)]

    return pl.pallas_call(
        scatter_kernel,
        out_shape=(
            jax.ShapeDtypeStruct((2, ROWS, CA), F32),
            jax.ShapeDtypeStruct((2, ROWS, CB), F32),
            jax.ShapeDtypeStruct((2, TOK, D), F32),
        ),
        in_specs=[any_] * 3,
        out_specs=(any_, any_, vmem),
        scratch_shapes=[
            *both(2, 2, 2, ROWS),
            *both(2, 4, ROWS),
            *both(2, 2, 2, ROWS),
            *both(2, 2, 4, ROWS),
            *both(2, 2, ROWS // 2),
            *both(2, 2, ROWS),
            *both(2, ROWS, dtype=F32),
            pltpu.VMEM((2, 2, 2, TOK, D), BF),
            pltpu.VMEM((2, 2, 2, TOK, D), BF),
            pltpu.VMEM((2, 2, TOK // 2, D), BF),
            pltpu.VMEM((2, 2, TOK, D), BF),
            pltpu.SemaphoreType.DMA((192,)),
            pltpu.SemaphoreType.DMA((192,)),
            pltpu.SemaphoreType.DMA((64,)),
        ],
        compiler_params=pltpu.CompilerParams(
            collective_id=1, has_side_effects=True, vmem_limit_bytes=56 * 2**20
        ),
    )(part_a, part_b, branch)


def total_kernel(item, out, first, second, send1, recv1, send2, recv2):
    x, y, z, c = place()
    here, there = z * 4 + y, x * 2 + c

    def plane(k):
        at = (here + k) % 16
        return device(x, at % 4, at // 4, c)

    def line(k):
        at = (there + k) % 8
        return device(at // 2, y, z, at % 2)

    barrier = pltpu.get_barrier_semaphore()
    for k in range(1, 16):
        pl.semaphore_signal(barrier, inc=1, device_id=plane(k), device_id_type=MESH)
    for k in range(1, 8):
        pl.semaphore_signal(barrier, inc=1, device_id=line(k), device_id_type=MESH)
    first[here] = item[...]
    pl.semaphore_wait(barrier, 22)
    copies = []
    for k in range(1, 16):
        copies.append(
            pltpu.make_async_remote_copy(
                first.at[here], first.at[here], send1.at[k], recv1.at[k], device_id=plane(k), device_id_type=MESH
            )
        )
        copies[-1].start()
    for copy in copies:
        copy.wait_recv()
    total = first[0]
    for k in range(1, 16):
        total = total + first[k]
    second[there] = total
    others = []
    for k in range(1, 8):
        others.append(
            pltpu.make_async_remote_copy(
                second.at[there], second.at[there], send2.at[k], recv2.at[k], device_id=line(k), device_id_type=MESH
            )
        )
        others[-1].start()
    for copy in others:
        copy.wait_recv()
    total = second[0]
    for k in range(1, 8):
        total = total + second[k]
    out[...] = total
    for copy in copies + others:
        copy.wait_send()


def total_all(item):
    vmem = pl.BlockSpec(memory_space=pltpu.VMEM)
    return pl.pallas_call(
        total_kernel,
        out_shape=jax.ShapeDtypeStruct(item.shape, F32),
        in_specs=[vmem],
        out_specs=vmem,
        scratch_shapes=[
            pltpu.VMEM((16,) + item.shape, F32),
            pltpu.VMEM((8,) + item.shape, F32),
            pltpu.SemaphoreType.DMA((16,)),
            pltpu.SemaphoreType.DMA((16,)),
            pltpu.SemaphoreType.DMA((8,)),
            pltpu.SemaphoreType.DMA((8,)),
        ],
        compiler_params=pltpu.CompilerParams(collective_id=2, has_side_effects=True),
    )(item)


def doc_layout(lengths, total):
    ends = jnp.cumsum(lengths)
    index = jnp.arange(total, dtype=jnp.int32)
    passed = (index[:, None] >= ends[None, :]).astype(jnp.int32)
    doc_ids = jnp.sum(passed, 1)
    starts = jnp.sum(passed * lengths[None, :], 1)
    return (doc_ids, index - starts, index)


def turn_angles(positions):
    half = ROT // 2
    freq = 10000.0 ** (-2.0 * jnp.arange(half, dtype=F32) / ROT)
    angle = positions.astype(F32)[..., None] * freq
    return (jnp.cos(angle)[:, :, None, :], jnp.sin(angle)[:, :, None, :])


def rotate(field, cosine, sine):
    half = ROT // 2
    lead_half = field[..., :half]
    tail_half = field[..., half:ROT]
    return jnp.concatenate(
        [
            lead_half * cosine - tail_half * sine,
            tail_half * cosine + lead_half * sine,
            field[..., ROT:],
        ],
        -1,
    )


def soap_update(weight, grad, first, second, basis, rate):
    rows, cols = grad.shape
    blocks = basis.shape[0]
    turned = jnp.einsum(
        "rbi,bij->rbj", grad.reshape(rows, blocks, -1), basis, precision=PRECISE
    ).reshape(rows, cols)
    first_new = BETA_ONE * first + (1.0 - BETA_ONE) * turned
    second_new = BETA_TWO * second + (1.0 - BETA_TWO) * turned * turned
    ratio = (
        first_new
        / (1.0 - BETA_ONE**STEP)
        / (jnp.sqrt(second_new / (1.0 - BETA_TWO**STEP)) + ADAM_EPS)
    )
    back = jnp.einsum(
        "rbj,bij->rbi", ratio.reshape(rows, blocks, -1), basis, precision=PRECISE
    ).reshape(rows, cols)
    return (first_new, second_new, weight - rate * (back + WEIGHT_DECAY * weight))


def adam_plain(param, grad, first, second, rate):
    first_new = BETA_ONE * first + (1.0 - BETA_ONE) * grad
    second_new = BETA_TWO * second + (1.0 - BETA_TWO) * grad * grad
    ratio = (
        first_new
        / (1.0 - BETA_ONE**STEP)
        / (jnp.sqrt(second_new / (1.0 - BETA_TWO**STEP)) + ADAM_EPS)
    )
    return (first_new, second_new, param - rate * ratio)


def split_columns(qkv, out, gate, up, down):
    zeros = jnp.zeros((ROWS, 64), qkv.dtype)
    a = jnp.stack(
        [
            jnp.concatenate(
                [qkv[:, :768], gate[:, :640], up[:, :640], gate[:, 640:704], up[:, 640:704]], 1
            ),
            jnp.concatenate(
                [qkv[:, 768:], gate[:, 768:], up[:, 768:], gate[:, 704:768], up[:, 704:768]], 1
            ),
        ]
    )
    b = jnp.stack(
        [
            jnp.concatenate([out[:, :256], down[:, :640], down[:, 640:704], zeros], 1),
            jnp.concatenate([out[:, 256:], down[:, 768:], down[:, 704:768], zeros], 1),
        ]
    )
    return a, b


def join_columns(a, b):
    def joined(item, start, rest):
        return jnp.concatenate(
            [
                item[0, :, start : start + 640],
                item[0, :, rest : rest + 64],
                item[1, :, rest : rest + 64],
                item[1, :, start : start + 640],
            ],
            1,
        )

    qkv = jnp.concatenate([a[0, :, :768], a[1, :, :768]], 1)
    out = jnp.concatenate([b[0, :, :256], b[1, :, :256]], 1)
    return (qkv, out, joined(a, 768, 2048), joined(a, 1408, 2112), joined(b, 256, 896))


def attention(qkv_pre, d_attn_of, lengths):
    docs, positions, index = jax.vmap(lambda one: doc_layout(one, LEN))(lengths)
    cosine, sine = turn_angles(positions)
    scale = 1.0 / math.sqrt(HEAD_DIM)
    queries = (rotate(qkv_pre[:, :, :, 0], cosine, sine) * scale).astype(BF)
    keys = rotate(qkv_pre[:, :, :, 1], cosine, sine).astype(BF)
    values = qkv_pre[:, :, :, 2].astype(BF)
    allowed = (docs[:, :, None] == docs[:, None, :]) & (index[:, :, None] >= index[:, None, :])
    allowed = allowed[:, None]
    scores = jnp.einsum("sqhd,skhd->shqk", queries, keys, preferred_element_type=F32)
    scores = jnp.where(allowed, scores, MASK_FILL)
    peak = jnp.max(scores, -1, keepdims=True)
    expo = jnp.exp(scores - peak)
    probs = expo / jnp.sum(expo, -1, keepdims=True)
    probs_low = probs.astype(BF)
    attn = jnp.einsum("shqk,skhd->sqhd", probs_low, values, preferred_element_type=F32)
    attn = attn.reshape(GROUP, HEADS * HEAD_DIM).astype(BF)
    d_attn = d_attn_of.reshape(2, LEN, HEADS, HEAD_DIM)
    d_prob = jnp.einsum("sqhd,skhd->shqk", d_attn, values, preferred_element_type=F32)
    delta = jnp.sum(probs * d_prob, -1, keepdims=True)
    d_score = (probs * (d_prob - delta)).astype(BF)
    d_query = jnp.einsum("shqk,skhd->sqhd", d_score, keys, preferred_element_type=F32) * scale
    d_key = jnp.einsum("shqk,sqhd->skhd", d_score, queries, preferred_element_type=F32)
    d_value = jnp.einsum("shqk,sqhd->skhd", probs_low, d_attn, preferred_element_type=F32)
    d_qkv = jnp.stack([rotate(d_query, cosine, -sine), rotate(d_key, cosine, -sine), d_value], 3)
    return attn, d_qkv.reshape(GROUP, HEADS * 3 * HEAD_DIM).astype(BF)


def body(
    tokens,
    cotangent,
    doc_lengths,
    row_owner,
    norm_params,
    norm_moment1,
    norm_moment2,
    qkv_weight,
    out_weight,
    gate_weight,
    up_weight,
    down_weight,
    qkv_moment1,
    out_moment1,
    gate_moment1,
    up_moment1,
    down_moment1,
    qkv_moment2,
    out_moment2,
    gate_moment2,
    up_moment2,
    down_moment2,
    qkv_basis,
    out_basis,
    gate_basis,
    up_basis,
    down_basis,
):
    stored_at = (row_owner[:, None] * ROWS + jnp.arange(ROWS, dtype=jnp.int32)[None, :]).reshape(D)
    turn = (stored_at[:, None] == jnp.arange(D, dtype=jnp.int32)[None, :]).astype(BF)
    pair = jnp.dot(jnp.concatenate([tokens, cotangent], 0), turn, preferred_element_type=F32)
    inputs = pair[:TOK]
    grad_in = pair[TOK:]
    inverse = jnp.argsort(row_owner)
    params_stored = norm_params.reshape(2, 32, ROWS)[:, inverse].reshape(2, D)
    norm_gain = params_stored[0]
    norm_shift = params_stored[1]
    row_mean = jnp.mean(inputs, -1, keepdims=True)
    centered_input = inputs - row_mean
    row_variance = jnp.mean(centered_input * centered_input, -1, keepdims=True)
    inverse_deviation = lax.rsqrt(row_variance + NORM_EPSILON)
    standardized_input = centered_input * inverse_deviation
    normed_output = (standardized_input * norm_gain + norm_shift).astype(BF)

    own_a, own_b = split_columns(
        *[item.astype(BF) for item in (qkv_weight, out_weight, gate_weight, up_weight, down_weight)]
    )
    doc_item = jnp.zeros((8, 128), F32).at[0, :4].set(doc_lengths[0].astype(F32))
    wall_a, wall_b, toks, docs = gather_all(
        own_a, own_b, jnp.stack([normed_output, grad_in.astype(BF)]), doc_item
    )
    wall_a = wall_a.reshape(D, CA)
    wall_b = wall_b.reshape(D, CB)
    normed_all = toks[0].reshape(GROUP, D)
    grad_all = toks[1].reshape(GROUP, D)
    lengths = docs[:, 0, :4].astype(jnp.int32)

    pre_a = jnp.dot(normed_all, wall_a, preferred_element_type=F32)
    pre_b = jnp.dot(grad_all, wall_b, preferred_element_type=F32)
    attn, d_qkv = attention(
        pre_a[:, :768].reshape(2, LEN, HEADS, 3, HEAD_DIM), pre_b[:, :256].astype(BF), lengths
    )

    def units(gate, up, d_hidden):
        sigma = jax.nn.sigmoid(gate)
        hidden = (gate * sigma * up).astype(BF)
        d_gate = (d_hidden * up * sigma * (1.0 + gate * (1.0 - sigma))).astype(BF)
        d_up = (d_hidden * gate * sigma).astype(BF)
        return hidden, d_gate, d_up

    hidden0, d_gate0, d_up0 = units(pre_a[:, 768:1408], pre_a[:, 1408:2048], pre_b[:, 256:896])
    hidden1, d_gate1, d_up1 = units(pre_a[:, 2048:2112], pre_a[:, 2112:2176], pre_b[:, 896:960])
    made = jnp.concatenate([attn, hidden0, hidden1, jnp.zeros((GROUP, 64), BF)], 1)
    back = jnp.concatenate([d_qkv, d_gate0, d_up0, d_gate1, d_up1], 1)
    branch = lax.dot_general(made, wall_b, COLS_DIMS, preferred_element_type=F32).astype(BF)
    d_normed = lax.dot_general(back, wall_a, COLS_DIMS, preferred_element_type=F32).astype(BF)
    part_a = lax.dot_general(normed_all, back, ROWS_DIMS, preferred_element_type=F32).astype(BF)
    part_b = lax.dot_general(grad_all, made, ROWS_DIMS, preferred_element_type=F32).astype(BF)
    grad_a, grad_b, tok_sums = scatter_all(
        part_a.reshape(2, 4, 4, ROWS, CA),
        part_b.reshape(2, 4, 4, ROWS, CB),
        jnp.stack([branch, d_normed]).reshape(2, 2, 2, 2, TOK, D),
    )

    out = (inputs + tok_sums[0]).astype(BF)
    normed_cotangent = tok_sums[1]
    standardized_cotangent = normed_cotangent * norm_gain
    input_grad = (
        grad_in
        + inverse_deviation
        * (
            standardized_cotangent
            - jnp.mean(standardized_cotangent, -1, keepdims=True)
            - standardized_input
            * jnp.mean(standardized_cotangent * standardized_input, -1, keepdims=True)
        )
    ).astype(BF)
    pair_out = lax.dot_general(
        jnp.concatenate([out, input_grad], 0), turn, COLS_DIMS, preferred_element_type=F32
    ).astype(BF)

    norm_partial = jnp.stack(
        [jnp.sum(normed_cotangent * standardized_input, 0), jnp.sum(normed_cotangent, 0)]
    )
    squares = jnp.sum((grad_a * grad_a).reshape(-1, 128), 0) + jnp.sum((grad_b * grad_b).reshape(-1, 128), 0)
    item = jnp.concatenate(
        [norm_partial.reshape(8, 512), jnp.zeros((8, 128), F32).at[0].set(squares)], 1
    )
    totals = total_all(item)
    norm_raw = totals[:, :512].reshape(2, 32, ROWS)[:, row_owner].reshape(2, D)
    grad_norm = jnp.sqrt(jnp.sum(totals[:, 512:]) + jnp.sum(norm_raw * norm_raw))
    clip = jnp.minimum(1.0, CLIP_LIMIT / grad_norm)
    norm_grads = clip * norm_raw
    norm_first, norm_second, norm_new = adam_plain(
        norm_params, norm_grads, norm_moment1, norm_moment2, NORM_RATE
    )
    masters = (qkv_weight, out_weight, gate_weight, up_weight, down_weight)
    firsts = (qkv_moment1, out_moment1, gate_moment1, up_moment1, down_moment1)
    seconds = (qkv_moment2, out_moment2, gate_moment2, up_moment2, down_moment2)
    bases = (qkv_basis, out_basis, gate_basis, up_basis, down_basis)
    clipped = [clip * grad for grad in join_columns(grad_a, grad_b)]
    updates = [
        soap_update(masters[i], clipped[i], firsts[i], seconds[i], bases[i], RATE_LIST[i])
        for i in range(5)
    ]
    return (
        pair_out[:TOK],
        pair_out[TOK:],
        grad_norm,
        norm_grads,
        norm_first,
        norm_second,
        norm_new,
        *clipped,
        *[item[0] for item in updates],
        *[item[1] for item in updates],
        *[item[2] for item in updates],
    )


def solution(mesh):
    tok, weight, whole = P(("dp", "mp"), None), P("dp", "mp"), P()
    in_specs = (tok, tok, P("dp", None)) + (whole,) * 4 + (weight,) * 15 + (P("mp", None, None),) * 5
    out_specs = (tok, tok) + (whole,) * 5 + (weight,) * 20
    return jax.shard_map(body, mesh=mesh, in_specs=in_specs, out_specs=out_specs, check_vma=False)
```

```python
import jax
import jax.numpy as jnp
from jax import lax
from jax.experimental import pallas as pl
from jax.experimental.pallas import tpu as pltpu
from jax.sharding import PartitionSpec as P

MESH = pl.DeviceIdType.MESH
BF = jnp.bfloat16
F32 = jnp.float32

HEAD_DIM = 64
ROT = 16
STEP = 5

NORM_EPSILON = 1e-05
BETA_ONE = 0.5
BETA_TWO = 0.5
ADAM_EPS = 1e-08
WEIGHT_DECAY = 0.01
RATE_LIST = (0.02, 0.1, 0.02, 0.02, 0.015)
NORM_RATE = 0.2
CLIP_LIMIT = 1.0
MASK_FILL = -1e30
ROWS_DIMS = (((0,), (0,)), ((), ()))
COLS_DIMS = (((1,), (1,)), ((), ()))

D = 2048
LEN = 512
ROWS = 64
TOK = 128
GROUP = 1024
HEADS = 4
CA = 2176
CB = 1024
CHUNKS = ((1, 0, 512), (1, 512, 512), (0, 0, 512), (0, 512, 512), (0, 1024, 512), (0, 1536, 640))


def place():
    dp = lax.axis_index("dp")
    mp = lax.axis_index("mp")
    return (mp // 2) * 2 + dp // 16, dp % 4, (dp // 4) % 4, mp % 2


def device(x, y, z, c):
    return ((x % 2) * 16 + z * 4 + y, (x // 2) * 2 + c)


def near(me, name):
    x, y, z, c = me
    return {
        "y+": lambda: device(x, (y + 1) % 4, z, c),
        "y-": lambda: device(x, (y + 3) % 4, z, c),
        "z+": lambda: device(x, y, (z + 1) % 4, c),
        "z-": lambda: device(x, y, (z + 3) % 4, c),
        "x+": lambda: device((x + 1) % 4, y, z, c),
        "x-": lambda: device((x + 3) % 4, y, z, c),
        "c": lambda: device(x, y, z, 1 - c),
        "p": lambda: device((x // 2) * 2 + 1 - x % 2, y, z, c),
    }[name]()


NEIGHBOURS = ("y+", "y-", "z+", "z-", "x+", "x-", "c")


def greet(me):
    barrier = pltpu.get_barrier_semaphore()
    for name in NEIGHBOURS:
        pl.semaphore_signal(barrier, inc=1, device_id=near(me, name), device_id_type=MESH)
    pl.semaphore_wait(barrier, len(NEIGHBOURS))


class Wires:
    def __init__(self, me, send, recv):
        self.me, self.send, self.recv = me, send, recv
        self.count = 0
        self.open = []

    def push(self, src, dst, to, at=None):
        if at is None:
            at = self.count
            self.count += 1
        if isinstance(to, str):
            to = near(self.me, to)
        copy = pltpu.make_async_remote_copy(
            src, dst, self.send.at[at], self.recv.at[at], device_id=to, device_id_type=MESH
        )
        copy.start()
        self.open.append(copy)
        return copy

    def take(self, number):
        at = self.count
        self.count += number
        return at

    def close(self):
        for copy in self.open:
            copy.wait_send()


def gather_kernel(own_a, own_b, tok, doc, wall_a, wall_b, toks, docs, send, recv, keep):
    me = x, y, z, c = place()
    xlo, xhi = x % 2, x // 2
    wires = Wires(me, send, recv)
    pairs = ((own_a, wall_a), (own_b, wall_b))
    locals_ = []

    def local(src, dst):
        copy = pltpu.make_async_copy(src, dst, keep.at[len(locals_)])
        copy.start()
        locals_.append(copy)

    greet(me)
    four = ("y+", "y-", "z+", "z-")
    first = wires.take(16)

    def own_at(i, half, d):
        return first + i * 8 + half * 4 + d

    for i, (own, wall) in enumerate(pairs):
        for d, name in enumerate(four):
            wires.push(own.at[xlo], wall.at[xlo, z, y], name, own_at(i, xlo, d))
    swaps = [wires.push(own.at[1 - xlo], wall.at[xlo, z, y], "p") for own, wall in pairs]
    doc_swap = wires.push(doc, docs.at[xlo], "p")
    local(doc, docs.at[xlo])
    for own, wall in pairs:
        local(own.at[xlo], wall.at[xlo, z, y])
    tok_x = {}
    tok_c = []
    for k in range(2):
        for name in ("x+", "x-"):
            tok_x[k, name] = wires.push(tok.at[k], toks.at[k, xlo, xhi, c], name)
        tok_c.append(wires.push(tok.at[k], toks.at[k, xlo, xhi, c], "c"))
        local(tok.at[k], toks.at[k, xlo, xhi, c])
    for i, (own, wall) in enumerate(pairs):
        swaps[i].wait_recv()
        for d, name in enumerate(four):
            mine = wall.at[1 - xlo, z, y]
            wires.push(mine, mine, name, own_at(i, 1 - xlo, d))

    axes = (("y+", "y-", "z+", "z-"), ("z+", "z-", "y+", "y-"))

    def block(wall, half, a, b):
        return wall.at[0, b, a] if half == 0 else wall.at[1, a, b]

    def spots(half):
        return (y, z) if half == 0 else (z, y)

    def wait_own(i, half, name):
        wall = pairs[i][1]
        mine = wall.at[half, z, y]
        at = own_at(i, half, four.index(name))
        pltpu.make_async_remote_copy(
            mine, mine, send.at[at], recv.at[at], device_id=near(me, name), device_id_type=MESH
        ).wait_recv()

    lo, hi = pl.ds(0, ROWS // 2), pl.ds(ROWS // 2, ROWS // 2)
    forwards, seconds = {}, {}
    for i, (own, wall) in enumerate(pairs):
        for half in range(2):
            a, b = spots(half)
            f_up, f_down, s_up, s_down = axes[half]
            wait_own(i, half, f_up)
            got = block(wall, half, (a + 3) % 4, b)
            forwards[i, half, 0] = wires.push(got.at[lo], got.at[lo], f_up)
            wait_own(i, half, f_down)
            other = block(wall, half, (a + 1) % 4, b)
            forwards[i, half, 1] = wires.push(other.at[hi], other.at[hi], f_down)
            for j, item in ((1, got), (2, other)):
                seconds[i, half, j, 0] = wires.push(item, item, s_up)
                seconds[i, half, j, 1] = wires.push(item, item, s_down)
    tok_f = {}
    for k in range(2):
        for n, name in enumerate(("x+", "x-")):
            tok_x[k, name].wait_recv()
            sx = (x + 3) % 4 if n == 0 else (x + 1) % 4
            got = toks.at[k, sx % 2, sx // 2, c]
            part = got.at[pl.ds(n * (TOK // 2), TOK // 2)]
            tok_f[k, n] = wires.push(part, part, name)
            tok_c.append(wires.push(got, got, "c"))
    for i, (own, wall) in enumerate(pairs):
        for half in range(2):
            a, b = spots(half)
            f_up, f_down, s_up, s_down = axes[half]
            forwards[i, half, 0].wait_recv()
            forwards[i, half, 1].wait_recv()
            item = block(wall, half, (a + 2) % 4, b)
            seconds[i, half, 3, 0] = wires.push(item, item, s_up)
            seconds[i, half, 3, 1] = wires.push(item, item, s_down)
    lasts = []
    for j, step in enumerate((0, 3, 1, 2)):
        for i, (own, wall) in enumerate(pairs):
            for half in range(2):
                a, b = spots(half)
                f_up, f_down, s_up, s_down = axes[half]
                spot = (a + step) % 4
                for n, name in ((0, s_up), (1, s_down)):
                    if j == 0:
                        wait_own(i, half, name)
                    else:
                        seconds[i, half, j, n].wait_recv()
                    got = block(wall, half, spot, (b + 3) % 4 if n == 0 else (b + 1) % 4)
                    part = got.at[lo if n == 0 else hi]
                    lasts.append(wires.push(part, part, name))
        if j == 1:
            for k in range(2):
                tok_f[k, 0].wait_recv()
                tok_f[k, 1].wait_recv()
                sx = (x + 2) % 4
                got = toks.at[k, sx % 2, sx // 2, c]
                tok_c.append(wires.push(got, got, "c"))
    for copy in lasts:
        copy.wait_recv()
    for copy in tok_c:
        copy.wait_recv()
    doc_swap.wait_recv()
    wires.close()
    for copy in locals_:
        copy.wait()


def gather_all(own_a, own_b, tok, doc):
    any_ = pl.BlockSpec(memory_space=pl.ANY)
    return pl.pallas_call(
        gather_kernel,
        out_shape=(
            jax.ShapeDtypeStruct((2, 4, 4, ROWS, CA), BF),
            jax.ShapeDtypeStruct((2, 4, 4, ROWS, CB), BF),
            jax.ShapeDtypeStruct((2, 2, 2, 2, TOK, D), BF),
            jax.ShapeDtypeStruct((2, 8, 128), F32),
        ),
        in_specs=[any_] * 4,
        out_specs=(any_,) * 4,
        scratch_shapes=[
            pltpu.SemaphoreType.DMA((160,)),
            pltpu.SemaphoreType.DMA((160,)),
            pltpu.SemaphoreType.DMA((8,)),
        ],
        compiler_params=pltpu.CompilerParams(collective_id=0, has_side_effects=True),
    )(own_a, own_b, tok, doc)


def add_rows(dst, src, rows, cols):
    def step(g, carry):
        at = pl.ds(pl.multiple_of(g * 16, 16), 16)
        dst[at, cols] = (dst[at, cols].astype(F32) + src[at, cols].astype(F32)).astype(dst.dtype)
        return carry

    lax.fori_loop(0, rows // 16, step, 0)


def peers(me):
    x, y, z, c = me
    here, there = z * 4 + y, x * 2 + c
    plane, line = [], []
    for k in range(1, 16):
        at = (here + k) % 16
        plane.append(device(x, at % 4, at // 4, c))
    for k in range(1, 8):
        at = (there + k) % 8
        line.append(device(at // 2, y, z, at % 2))
    return here, there, plane, line


FEATS = 256


def scatter_kernel(
    made, back, toks, wall_a, wall_b, tokens, cotangent, gains,
    grad_a, grad_b, tok_out, norm_out, square_out,
    v_act, v_made, v_back, v_wall_a, v_wall_b, part_a, part_b, stage,
    r1_a, r1_b, r2_a, r2_b, t1_a, t1_b, t2_a, t2_b, sum_a, sum_b,
    own, core, x1, x2, norm1, norm2, square1, square2,
    send, recv, keep, load,
):
    me = x, y, z, c = place()
    xlo = x % 2
    wires = Wires(me, send, recv)
    parts, grads = (part_a, part_b), (grad_a, grad_b)
    r1, r2 = (r1_a, r1_b), (r2_a, r2_b)
    t1, t2, sums = (t1_a, t1_b), (t2_a, t2_b), (sum_a, sum_b)
    late = []
    here, there, plane, line = peers(me)

    def fetch(src, dst, sem):
        for side in range(2):
            for g in range(4):
                at = g * 256 + (c if side == 0 else 1 - c) * TOK
                pltpu.make_async_copy(
                    src.at[pl.ds(at, TOK)], dst.at[pl.ds(side * 512 + g * TOK, TOK)], load.at[sem]
                ).start()

    def fetched(dst, sem):
        pltpu.make_async_copy(dst, dst, load.at[sem]).wait()

    def wall_copy(i, f):
        wall, buf = ((wall_a, v_wall_a), (wall_b, v_wall_b))[i]
        return pltpu.make_async_copy(
            wall.at[pl.ds(f * FEATS, FEATS)], buf.at[f % 2], load.at[4 + 2 * i + f % 2]
        )

    fetch(toks.at[1], v_act, 0)
    fetch(made, v_made, 1)
    fetch(back, v_back, 2)
    for i in (1, 0):
        for f in range(2):
            wall_copy(i, f).start()

    barrier = pltpu.get_barrier_semaphore()
    for to in plane + line:
        pl.semaphore_signal(barrier, inc=1, device_id=to, device_id_type=MESH)
    pl.semaphore_wait(barrier, 22)
    axes = (("z+", "z-", "y+", "y-"), ("y+", "y-", "z+", "z-"))

    def spots(half):
        return (z, y) if half == 0 else (y, z)

    def piece(half, chunk, spot, start, size):
        i, c0, cn = chunk
        cols = pl.ds(c0, cn)
        if half == 0:
            return parts[i].at[0, spot, pl.ds(start, size), :, cols]
        return parts[i].at[1, pl.ds(start, size), spot, :, cols]

    state = {}

    def product(n):
        i, c0, cn = CHUNKS[n]
        right = (v_back, v_made)[i]

        def step(f, carry):
            feats = pl.ds(pl.multiple_of(f * FEATS, FEATS), FEATS)
            got = lax.dot_general(
                v_act[:, feats], right[:, pl.ds(c0, cn)], ROWS_DIMS, preferred_element_type=F32
            )
            parts[i][f // 4, f % 4, :, :, pl.ds(c0, cn)] = got.astype(BF).reshape(4, ROWS, cn)
            return carry

        lax.fori_loop(0, D // FEATS, step, 0)

    def branch(k, blocks):
        i = 1 - k
        left, buf = (v_back, v_made)[i], (v_wall_a, v_wall_b)[i]
        for f in blocks:
            wall_copy(i, f).wait()
            feats = pl.ds(f * FEATS, FEATS)
            for side in range(2):
                got = lax.dot_general(
                    left[pl.ds(side * 512, 512), :], buf[f % 2], COLS_DIMS, preferred_element_type=F32
                )
                got = got.astype(BF).reshape(2, 2, TOK, FEATS)
                if side == 0:
                    own[k, :, :, :, feats] = got
                else:
                    stage[:, :, :, feats] = got
            if f + 2 < D // FEATS:
                wall_copy(i, f + 2).start()

    def cross(k):
        state["c", k] = wires.push(stage, core.at[k], "c")

    def stage0(n, half):
        chunk = i, c0, cn = CHUNKS[n]
        p, q = spots(half)
        up, down = axes[half][:2]
        cols = pl.ds(c0, cn)
        state["a", n, half, 0] = wires.push(
            piece(half, chunk, (p + 2) % 4, 0, 2), r1[i].at[half, 0, :, :, cols], up
        )
        state["a", n, half, 1] = wires.push(
            piece(half, chunk, (p + 2) % 4, 2, 2), r1[i].at[half, 1, :, :, cols], down
        )
        state["b", n, half, 0] = wires.push(
            piece(half, chunk, (p + 1) % 4, 2, 2), r2[i].at[half, 0, pl.ds(2, 2), :, cols], up
        )
        state["b", n, half, 1] = wires.push(
            piece(half, chunk, (p + 3) % 4, 0, 2), r2[i].at[half, 1, pl.ds(0, 2), :, cols], down
        )

    def stage1(n, half):
        chunk = i, c0, cn = CHUNKS[n]
        cols = pl.ds(c0, cn)
        p, q = spots(half)
        for d in range(2):
            state["a", n, half, d].wait_recv()
            spot = (p + 1) % 4 if d == 0 else (p + 3) % 4
            for m in range(2):
                block = 2 * d + m
                mine = parts[i].at[0, spot, block] if half == 0 else parts[i].at[1, block, spot]
                add_rows(mine, r1[i].at[half, d, m], ROWS, cols)
            state["s", n, half, d] = wires.push(
                piece(half, chunk, spot, 2 * d, 2), r2[i].at[half, d, pl.ds(2 * d, 2), :, cols], axes[half][d]
            )

    def kept(i, half, p, q):
        return parts[i].at[0, p, q] if half == 0 else parts[i].at[1, q, p]

    def stage2(n, half):
        i, c0, cn = CHUNKS[n]
        cols = pl.ds(c0, cn)
        p, q = spots(half)
        up, down = axes[half][2:]
        for d in range(2):
            state["b", n, half, d].wait_recv()
            state["s", n, half, d].wait_recv()

        def step(g, carry):
            at = pl.ds(pl.multiple_of((g % 4) * 16, 16), 16)
            m = g // 4
            mine = kept(i, half, p, m)
            total = (
                mine[at, cols].astype(F32)
                + r2[i][half, 0, m, at, cols].astype(F32)
                + r2[i][half, 1, m, at, cols].astype(F32)
            )
            mine[at, cols] = total.astype(BF)
            return carry

        lax.fori_loop(0, 16, step, 0)
        lo, hi = pl.ds(0, ROWS // 2), pl.ds(ROWS // 2, ROWS // 2)
        far = kept(i, half, p, (q + 2) % 4)
        state["t", n, half, 0] = wires.push(far.at[lo, cols], t1[i].at[half, 0, :, cols], up)
        state["t", n, half, 1] = wires.push(far.at[hi, cols], t1[i].at[half, 1, :, cols], down)
        state["u", n, half, 0] = wires.push(
            kept(i, half, p, (q + 1) % 4).at[hi, cols], t2[i].at[half, 0, hi, cols], up
        )
        state["u", n, half, 1] = wires.push(
            kept(i, half, p, (q + 3) % 4).at[lo, cols], t2[i].at[half, 1, lo, cols], down
        )

    def stage3(n, half):
        i, c0, cn = CHUNKS[n]
        cols = pl.ds(c0, cn)
        p, q = spots(half)
        for d in range(2):
            state["t", n, half, d].wait_recv()
            rows = pl.ds(d * (ROWS // 2), ROWS // 2)
            mine = kept(i, half, p, (q + 1) % 4 if d == 0 else (q + 3) % 4).at[rows]
            add_rows(mine, t1[i].at[half, d], ROWS // 2, cols)
            state["v", n, half, d] = wires.push(
                mine.at[:, cols], t2[i].at[half, d, rows, cols], axes[half][2 + d]
            )

    def stage4(n, half):
        i, c0, cn = CHUNKS[n]
        cols = pl.ds(c0, cn)
        p, q = spots(half)
        for d in range(2):
            state["u", n, half, d].wait_recv()
            state["v", n, half, d].wait_recv()
        mine = kept(i, half, p, q)

        def step(g, carry):
            at = pl.ds(pl.multiple_of(g * 16, 16), 16)
            total = (
                mine[at, cols].astype(F32)
                + t2[i][half, 0, at, cols].astype(F32)
                + t2[i][half, 1, at, cols].astype(F32)
            )
            sums[i][half, at, cols] = total
            squares = total * total
            for m in range(cn // 128):
                part = squares[:, m * 128 : m * 128 + 128]
                carry = carry + part[:8] + part[8:]
            return carry

        return lax.fori_loop(0, ROWS // 16, step, jnp.zeros((8, 128), F32))

    def stage5(n):
        i, c0, cn = CHUNKS[n]
        cols = pl.ds(c0, cn)
        state["g", n] = wires.push(sums[i].at[1 - xlo, :, cols], grads[i].at[xlo, :, cols], "p")
        copy = pltpu.make_async_copy(sums[i].at[xlo, :, cols], grads[i].at[xlo, :, cols], keep.at[n])
        copy.start()
        late.append(copy)

    half_tok = TOK // 2

    def tokens1(k):
        state["c", k].wait_recv()

        def step(g, carry):
            at = pl.ds(pl.multiple_of((g % 8) * 16, 16), 16)
            s = g // 8
            own[k, s // 2, s % 2, at, :] = (
                own[k, s // 2, s % 2, at, :].astype(F32) + core[k, s // 2, s % 2, at, :].astype(F32)
            ).astype(BF)
            return carry

        lax.fori_loop(0, 32, step, 0)

        def spot(s, d, far):
            rows = pl.ds((d if far else 1 - d) * half_tok, half_tok)
            return own.at[k, s % 2, s // 2, rows]

        for d, name in enumerate(("x+", "x-")):
            state["x1", k, d] = wires.push(spot((x + 2) % 4, d, True), x1.at[k, d], name)
        for d, name in enumerate(("x+", "x-")):
            to = (x + 1) % 4 if d == 0 else (x + 3) % 4
            rows = pl.ds((1 - d) * half_tok, half_tok)
            state["x2", k, d] = wires.push(spot(to, d, False), x2.at[k, d, rows], name)

    def tokens2(k):
        for d, name in enumerate(("x+", "x-")):
            state["x1", k, d].wait_recv()
            to = (x + 1) % 4 if d == 0 else (x + 3) % 4
            rows = pl.ds(d * half_tok, half_tok)
            mine = own.at[k, to % 2, to // 2, rows]
            add_rows(mine, x1.at[k, d], half_tok, pl.ds(0, D))
            state["x3", k, d] = wires.push(mine, x2.at[k, d, rows], name)

    def tokens3(k):
        for d in range(2):
            state["x2", k, d].wait_recv()
            state["x3", k, d].wait_recv()

        def total(at):
            return (
                own[k, xlo, x // 2, at, :].astype(F32)
                + x2[k, 0, at, :].astype(F32)
                + x2[k, 1, at, :].astype(F32)
            )

        def result(g, carry):
            at = pl.ds(pl.multiple_of(g * 16, 16), 16)
            tok_out[0, at, :] = (tokens[at, :].astype(F32) + total(at)).astype(BF)
            return carry

        def gradient(g, carry):
            at = pl.ds(pl.multiple_of(g * 16, 16), 16)
            inputs = tokens[at, :].astype(F32)
            centered = inputs - jnp.mean(inputs, -1, keepdims=True)
            variance = jnp.mean(centered * centered, -1, keepdims=True)
            deviation = lax.rsqrt(variance + NORM_EPSILON)
            standard = centered * deviation
            d_normed = total(at)
            d_standard = d_normed * gains[0:1, :]
            tok_out[1, at, :] = (
                cotangent[at, :].astype(F32)
                + deviation
                * (
                    d_standard
                    - jnp.mean(d_standard, -1, keepdims=True)
                    - standard * jnp.mean(d_standard * standard, -1, keepdims=True)
                )
            ).astype(BF)
            return (
                carry[0] + jnp.sum(d_normed * standard, 0, keepdims=True),
                carry[1] + jnp.sum(d_normed, 0, keepdims=True),
            )

        if k == 0:
            lax.fori_loop(0, TOK // 16, result, 0)
        else:
            zero = jnp.zeros((1, D), F32)
            gain_sum, shift_sum = lax.fori_loop(0, TOK // 16, gradient, (zero, zero))
            norm1[here, 0:1, :] = gain_sum
            norm1[here, 1:2, :] = shift_sum

    def small1(slots):
        return [wires.push(slots.at[here], slots.at[here], to) for to in plane]

    def small2(copies, slots, after):
        for copy in copies:
            copy.wait_recv()
        total = slots[0]
        for k in range(1, 16):
            total = total + slots[k]
        after[there] = total
        return [wires.push(after.at[there], after.at[there], to) for to in line]

    def small3(copies, after):
        for copy in copies:
            copy.wait_recv()
        total = after[0]
        for k in range(1, 8):
            total = total + after[k]
        return total

    def both(step, n):
        for half in range(2):
            step(n, half)

    squares = [jnp.zeros((8, 128), F32)]

    def last(n):
        for half in range(2):
            squares[0] = squares[0] + stage4(n, half)
        stage5(n)

    fetched(v_act, 0)
    fetched(v_made, 1)
    product(0)
    both(stage0, 0)
    product(1)
    both(stage0, 1)
    fetch(toks.at[0], v_act, 0)
    branch(0, range(8))
    cross(0)
    fetched(v_act, 0)
    fetched(v_back, 2)
    product(2)
    both(stage0, 2)
    both(stage1, 0)
    product(3)
    both(stage0, 3)
    both(stage1, 1)
    tokens1(0)
    product(4)
    both(stage0, 4)
    both(stage2, 0)
    product(5)
    both(stage0, 5)
    both(stage1, 2)
    state["c", 0].wait_send()
    wires.open = [copy for copy in wires.open if copy is not state["c", 0]]
    branch(1, range(4))
    both(stage2, 1)
    tokens2(0)
    both(stage3, 0)
    branch(1, range(4, 8))
    cross(1)
    both(stage1, 3)
    both(stage2, 2)
    both(stage3, 1)
    last(0)
    tokens1(1)
    both(stage1, 4)
    both(stage2, 3)
    both(stage3, 2)
    tokens3(0)
    last(1)
    both(stage1, 5)
    tokens2(1)
    both(stage2, 4)
    both(stage3, 3)
    last(2)
    tokens3(1)
    norm_copies = small1(norm1)
    both(stage2, 5)
    both(stage3, 4)
    last(3)
    norm_copies = small2(norm_copies, norm1, norm2)
    both(stage3, 5)
    last(4)
    last(5)
    square1[here] = squares[0]
    square_copies = small1(square1)
    norm_out[...] = small3(norm_copies, norm2)
    square_copies = small2(square_copies, square1, square2)
    square_out[...] = small3(square_copies, square2)
    for n in range(len(CHUNKS)):
        state["g", n].wait_recv()
    wires.close()
    for copy in late:
        copy.wait()


def scatter_all(made, back, toks, wall_a, wall_b, tokens, cotangent, gains):
    any_ = pl.BlockSpec(memory_space=pl.ANY)
    vmem = pl.BlockSpec(memory_space=pltpu.VMEM)

    def both(*shape, dtype=BF):
        return [pltpu.VMEM(shape + (CA,), dtype), pltpu.VMEM(shape + (CB,), dtype)]

    return pl.pallas_call(
        scatter_kernel,
        out_shape=(
            jax.ShapeDtypeStruct((2, ROWS, CA), F32),
            jax.ShapeDtypeStruct((2, ROWS, CB), F32),
            jax.ShapeDtypeStruct((2, TOK, D), BF),
            jax.ShapeDtypeStruct((2, D), F32),
            jax.ShapeDtypeStruct((8, 128), F32),
        ),
        in_specs=[any_] * 5 + [vmem] * 3,
        out_specs=(any_, any_, vmem, vmem, vmem),
        scratch_shapes=[
            pltpu.VMEM((GROUP, D), BF),
            pltpu.VMEM((GROUP, CB), BF),
            pltpu.VMEM((GROUP, CA), BF),
            pltpu.VMEM((2, FEATS, CA), BF),
            pltpu.VMEM((2, FEATS, CB), BF),
            *both(2, 4, 4, ROWS),
            pltpu.VMEM((2, 2, TOK, D), BF),
            *both(2, 2, 2, ROWS),
            *both(2, 2, 4, ROWS),
            *both(2, 2, ROWS // 2),
            *both(2, 2, ROWS),
            *both(2, ROWS, dtype=F32),
            pltpu.VMEM((2, 2, 2, TOK, D), BF),
            pltpu.VMEM((2, 2, 2, TOK, D), BF),
            pltpu.VMEM((2, 2, TOK // 2, D), BF),
            pltpu.VMEM((2, 2, TOK, D), BF),
            pltpu.VMEM((16, 2, D), F32),
            pltpu.VMEM((8, 2, D), F32),
            pltpu.VMEM((16, 8, 128), F32),
            pltpu.VMEM((8, 8, 128), F32),
            pltpu.SemaphoreType.DMA((224,)),
            pltpu.SemaphoreType.DMA((224,)),
            pltpu.SemaphoreType.DMA((8,)),
            pltpu.SemaphoreType.DMA((8,)),
        ],
        compiler_params=pltpu.CompilerParams(
            collective_id=1, has_side_effects=True, vmem_limit_bytes=62 * 2**20
        ),
    )(made, back, toks, wall_a, wall_b, tokens, cotangent, gains)


def swapped(field, lane):
    return jnp.where(lane % ROT < ROT // 2, pltpu.roll(field, 120, 1), pltpu.roll(field, ROT // 2, 1))


def middle_kernel(pre_a, pre_b, cosine, sine, lengths, made, back, bias):
    lane = lax.broadcasted_iota(jnp.int32, (1, 128), 1)
    mine = [lane < HEAD_DIM, lane >= HEAD_DIM]

    def sequence(s, carry):
        rows = pl.ds(pl.multiple_of(s * LEN, LEN), LEN)
        query_at = lax.broadcasted_iota(jnp.int32, (1, LEN), 1).astype(F32)
        key_at = lax.broadcasted_iota(jnp.int32, (LEN, 1), 0).astype(F32)
        start = jnp.zeros((1, LEN), F32)
        end = jnp.zeros((1, 1), F32)
        for j in range(3):
            length = lengths[s, 0:1, j : j + 1]
            end = end + length
            start = jnp.where(query_at >= end, end, start)
        bias[...] = jnp.where((key_at >= start) & (key_at <= query_at), 0.0, MASK_FILL)
        cos_rows = cosine[rows, :]
        sin_rows = sine[rows, :]

        def turned(at):
            field = pre_a[rows, pl.ds(at, 128)]
            return field * cos_rows + swapped(field, lane) * sin_rows

        def turned_back(field):
            return field * cos_rows - swapped(field, lane) * sin_rows

        for pair in range(HEADS // 2):
            at = pair * 128
            query = (turned(at) * (HEAD_DIM**-0.5)).astype(BF)
            key = turned(256 + at).astype(BF)
            value = pre_a[rows, pl.ds(512 + at, 128)].astype(BF)
            d_attn = pre_b[rows, pl.ds(at, 128)].astype(BF)
            key_t = key.T
            value_t = value.T
            d_key = [None, None]
            d_value = [None, None]
            zero = jnp.zeros((), BF)
            head_row = lax.broadcasted_iota(jnp.int32, (128, 1), 0) < HEAD_DIM
            for block in range(2):
                queries = slice(block * 256, block * 256 + 256)
                keys = (block + 1) * 256
                attn_t = []
                d_query_t = []
                for h in range(2):
                    query_h = jnp.where(mine[h], query[queries], zero)
                    d_attn_h = jnp.where(mine[h], d_attn[queries], zero)
                    scores = lax.dot_general(key[:keys], query_h, COLS_DIMS, preferred_element_type=F32)
                    scores = scores + bias[0:keys, queries]
                    peak = jnp.max(scores, 0, keepdims=True)
                    expo = jnp.exp(scores - peak)
                    probs = expo * (1.0 / jnp.sum(expo, 0, keepdims=True))
                    probs_low = probs.astype(BF)
                    d_prob = lax.dot_general(value[:keys], d_attn_h, COLS_DIMS, preferred_element_type=F32)
                    delta = jnp.sum(probs * d_prob, 0, keepdims=True)
                    d_score = (probs * (d_prob - delta)).astype(BF)
                    attn_t.append(jnp.dot(value_t[:, :keys], probs_low, preferred_element_type=F32))
                    d_query_t.append(jnp.dot(key_t[:, :keys], d_score, preferred_element_type=F32))
                    d_value_h = jnp.dot(probs_low, d_attn_h, preferred_element_type=F32)
                    d_key_h = jnp.dot(d_score, query_h, preferred_element_type=F32)
                    for p in range(block + 1):
                        part = slice(p * 256, p * 256 + 256)
                        d_value[p] = d_value_h[part] if d_value[p] is None else d_value[p] + d_value_h[part]
                        d_key[p] = d_key_h[part] if d_key[p] is None else d_key[p] + d_key_h[part]
                out_rows = pl.ds(pl.multiple_of(s * LEN + block * 256, 256), 256)
                made[out_rows, pl.ds(at, 128)] = jnp.where(head_row, attn_t[0], attn_t[1]).T.astype(BF)
                d_query = jnp.where(head_row, d_query_t[0], d_query_t[1]).T * (HEAD_DIM**-0.5)
                d_query = d_query * cosine[out_rows, :] - swapped(d_query, lane) * sine[out_rows, :]
                back[out_rows, pl.ds(at, 128)] = d_query.astype(BF)
            back[rows, pl.ds(256 + at, 128)] = turned_back(jnp.concatenate(d_key, 0)).astype(BF)
            back[rows, pl.ds(512 + at, 128)] = jnp.concatenate(d_value, 0).astype(BF)
        return carry

    lax.fori_loop(0, 2, sequence, 0)

    def units(gate, up, d_hidden):
        sigma = jax.nn.sigmoid(gate)
        silu = gate * sigma
        return silu * up, d_hidden * up * sigma * (1.0 + gate * (1.0 - sigma)), d_hidden * silu

    def unit_rows(g, carry):
        rows = pl.ds(pl.multiple_of(g * 32, 32), 32)
        hidden, d_gate, d_up = units(
            pre_a[rows, pl.ds(768, 640)], pre_a[rows, pl.ds(1408, 640)], pre_b[rows, pl.ds(256, 640)]
        )
        made[rows, pl.ds(256, 640)] = hidden.astype(BF)
        back[rows, pl.ds(768, 640)] = d_gate.astype(BF)
        back[rows, pl.ds(1408, 640)] = d_up.astype(BF)
        rest = pre_a[rows, pl.ds(2048, 128)]
        hidden, d_gate, d_up = units(rest, pltpu.roll(rest, 64, 1), pre_b[rows, pl.ds(896, 128)])
        made[rows, pl.ds(896, 128)] = jnp.where(mine[0], hidden, 0.0).astype(BF)
        back[rows, pl.ds(2048, 128)] = jnp.where(mine[0], d_gate, pltpu.roll(d_up, 64, 1)).astype(BF)
        return carry

    lax.fori_loop(0, GROUP // 32, unit_rows, 0)


def middle(pre_a, pre_b, cosine, sine, lengths):
    vmem = pl.BlockSpec(memory_space=pltpu.VMEM)
    return pl.pallas_call(
        middle_kernel,
        out_shape=(
            jax.ShapeDtypeStruct((GROUP, CB), BF),
            jax.ShapeDtypeStruct((GROUP, CA), BF),
        ),
        in_specs=[vmem] * 5,
        out_specs=(vmem, vmem),
        scratch_shapes=[pltpu.VMEM((LEN, LEN), F32)],
        compiler_params=pltpu.CompilerParams(vmem_limit_bytes=56 * 2**20),
    )(pre_a, pre_b, cosine, sine, lengths)


def turn_tables(lengths):
    index = jnp.arange(LEN, dtype=jnp.int32)
    ends = jnp.cumsum(lengths, 1)
    passed = (index[None, :, None] >= ends[:, None, :]).astype(jnp.int32)
    positions = (index[None] - jnp.sum(passed * lengths[:, None, :], 2)).reshape(GROUP).astype(F32)
    entry = jnp.arange(128, dtype=jnp.int32) % HEAD_DIM
    freq = 10000.0 ** (-2.0 * (entry % (ROT // 2)).astype(F32) / ROT)
    angle = positions[:, None] * freq[None, :]
    cosine = jnp.where(entry < ROT, jnp.cos(angle), 1.0)
    sine = jnp.where(entry < ROT, jnp.sin(angle), 0.0)
    return cosine, jnp.where(entry < ROT // 2, -sine, sine)


def halves(item):
    high = item.astype(BF)
    return high, (item - high.astype(F32)).astype(BF)


def near_product(left, right, dims):
    (a, a_low), (b, b_low) = left, right
    axis = 0 if dims == (((1,), (0,)), ((), ())) else 1
    return lax.dot_general(
        jnp.concatenate([a, a, a_low], 1),
        jnp.concatenate([b, b_low, b], axis),
        dims,
        preferred_element_type=F32,
    )


WIDTHS = (1536, 512, 1408, 1408, 1408)


def pieces():
    table = [[], [], [], [], []]
    for half in range(2):
        for head in range(HEADS):
            for kind in range(3):
                table[0].append((0, half, kind * 256 + head * 64))
        for head in range(HEADS):
            table[1].append((1, half, head * 64))
    for n, (i, start, rest) in enumerate(((0, 768, 2048), (0, 1408, 2112), (1, 256, 896))):
        table[2 + n] += [(i, 0, start + 64 * k) for k in range(10)]
        table[2 + n] += [(i, 0, rest), (i, 1, rest)]
        table[2 + n] += [(i, 1, start + 64 * k) for k in range(10)]
    return table


def update_kernel(clip_ref, grad_a, grad_b, *refs):
    weights, firsts, seconds, bases = refs[0:5], refs[5:10], refs[10:15], refs[15:20]
    grads, firsts_new, seconds_new, weights_new = refs[20:25], refs[25:30], refs[30:35], refs[35:40]
    parts = (grad_a, grad_b)
    left_lanes = lax.broadcasted_iota(jnp.int32, (1, 128), 1) < 64
    clip = clip_ref[0:1, 0:1]

    def fetch(piece, side):
        i, half, column = piece
        tile = parts[i][half, :, pl.ds(column // 128 * 128, 128)]
        return tile if column // 64 % 2 == side else pltpu.roll(tile, 64, 1)

    for i, table in enumerate(pieces()):
        for block in range(WIDTHS[i] // 128):
            cols = pl.ds(block * 128, 128)
            one, two = table[2 * block], table[2 * block + 1]
            if two == one[:2] + (one[2] + 64,) and one[2] % 128 == 0:
                grad = parts[one[0]][one[1], :, pl.ds(one[2], 128)]
            else:
                grad = jnp.where(left_lanes, fetch(one, 0), fetch(two, 1))
            grad = clip * grad
            grads[i][:, cols] = grad
            basis = halves(bases[i][block])
            turned = near_product(halves(grad), basis, (((1,), (0,)), ((), ())))
            first = BETA_ONE * firsts[i][:, cols] + (1.0 - BETA_ONE) * turned
            second = BETA_TWO * seconds[i][:, cols] + (1.0 - BETA_TWO) * turned * turned
            firsts_new[i][:, cols] = first
            seconds_new[i][:, cols] = second
            ratio = (
                first
                * (1.0 / (1.0 - BETA_ONE**STEP))
                / (jnp.sqrt(second * (1.0 / (1.0 - BETA_TWO**STEP))) + ADAM_EPS)
            )
            turned_back = near_product(halves(ratio), basis, COLS_DIMS)
            weight = weights[i][:, cols]
            weights_new[i][:, cols] = weight - RATE_LIST[i] * (turned_back + WEIGHT_DECAY * weight)


def update(clip, grad_a, grad_b, weights, firsts, seconds, bases):
    vmem = pl.BlockSpec(memory_space=pltpu.VMEM)
    shapes = [jax.ShapeDtypeStruct((ROWS, width), F32) for width in WIDTHS]
    return pl.pallas_call(
        update_kernel,
        out_shape=tuple(shapes * 4),
        in_specs=[vmem] * 23,
        out_specs=(vmem,) * 20,
        compiler_params=pltpu.CompilerParams(vmem_limit_bytes=56 * 2**20),
    )(jnp.broadcast_to(clip, (8, 128)), grad_a, grad_b, *weights, *firsts, *seconds, *bases)


def adam_plain(param, grad, first, second, rate):
    first_new = BETA_ONE * first + (1.0 - BETA_ONE) * grad
    second_new = BETA_TWO * second + (1.0 - BETA_TWO) * grad * grad
    ratio = (
        first_new
        / (1.0 - BETA_ONE**STEP)
        / (jnp.sqrt(second_new / (1.0 - BETA_TWO**STEP)) + ADAM_EPS)
    )
    return (first_new, second_new, param - rate * ratio)


def split_columns(weights):
    sides = {}
    for i, table in enumerate(pieces()):
        for n, (side, half, column) in enumerate(table):
            sides[side, half, column] = weights[i][:, n * 64 : n * 64 + 64]
    zeros = jnp.zeros((ROWS, 64), weights[0].dtype)
    return [
        jnp.stack(
            [
                jnp.concatenate([sides.get((side, half, k * 64), zeros) for k in range(width // 64)], 1)
                for half in range(2)
            ]
        )
        for side, width in enumerate((CA, CB))
    ]


def body(
    tokens,
    cotangent,
    doc_lengths,
    row_owner,
    norm_params,
    norm_moment1,
    norm_moment2,
    qkv_weight,
    out_weight,
    gate_weight,
    up_weight,
    down_weight,
    qkv_moment1,
    out_moment1,
    gate_moment1,
    up_moment1,
    down_moment1,
    qkv_moment2,
    out_moment2,
    gate_moment2,
    up_moment2,
    down_moment2,
    qkv_basis,
    out_basis,
    gate_basis,
    up_basis,
    down_basis,
):
    stored_at = (row_owner[:, None] * ROWS + jnp.arange(ROWS, dtype=jnp.int32)[None, :]).reshape(D)
    turn = (stored_at[:, None] == jnp.arange(D, dtype=jnp.int32)[None, :]).astype(BF)
    pair = jnp.dot(jnp.concatenate([tokens, cotangent], 0), turn, preferred_element_type=F32).astype(BF)
    inputs = pair[:TOK].astype(F32)
    blocks = jnp.arange(32, dtype=jnp.int32)
    inverse = jnp.sum((row_owner[None, :] == blocks[:, None]) * blocks[None, :], 1)
    params_stored = norm_params.reshape(2, 32, ROWS)[:, inverse].reshape(2, D)
    norm_gain = params_stored[0]
    norm_shift = params_stored[1]
    row_mean = jnp.mean(inputs, -1, keepdims=True)
    centered_input = inputs - row_mean
    row_variance = jnp.mean(centered_input * centered_input, -1, keepdims=True)
    inverse_deviation = lax.rsqrt(row_variance + NORM_EPSILON)
    standardized_input = centered_input * inverse_deviation
    normed_output = (standardized_input * norm_gain + norm_shift).astype(BF)

    masters = (qkv_weight, out_weight, gate_weight, up_weight, down_weight)
    own_a, own_b = split_columns([item.astype(BF) for item in masters])
    doc_item = jnp.zeros((8, 128), F32).at[0, :4].set(doc_lengths[0].astype(F32))
    wall_a, wall_b, toks, docs = gather_all(
        own_a, own_b, jnp.stack([normed_output, pair[TOK:]]), doc_item
    )
    wall_a = wall_a.reshape(D, CA)
    wall_b = wall_b.reshape(D, CB)
    normed_all = toks[0].reshape(GROUP, D)
    grad_all = toks[1].reshape(GROUP, D)
    lengths = docs[:, 0, :4].astype(jnp.int32)

    pre_a = jnp.dot(normed_all, wall_a, preferred_element_type=F32)
    pre_b = jnp.dot(grad_all, wall_b, preferred_element_type=F32)
    cosine, sine = turn_tables(lengths)
    made, back = middle(pre_a, pre_b, cosine, sine, docs)
    grad_a, grad_b, pair_out, norm_raw, squares = scatter_all(
        made, back, toks.reshape(2, GROUP, D), wall_a, wall_b, pair[:TOK], pair[TOK:], params_stored
    )
    pair_out = lax.dot_general(
        pair_out.reshape(2 * TOK, D), turn, COLS_DIMS, preferred_element_type=F32
    ).astype(BF)
    norm_raw = norm_raw.reshape(2, 32, ROWS)[:, row_owner].reshape(2, D)
    grad_norm = jnp.sqrt(jnp.sum(squares) + jnp.sum(norm_raw * norm_raw))
    clip = jnp.minimum(1.0, CLIP_LIMIT / grad_norm)
    norm_grads = clip * norm_raw
    norm_first, norm_second, norm_new = adam_plain(
        norm_params, norm_grads, norm_moment1, norm_moment2, NORM_RATE
    )
    firsts = (qkv_moment1, out_moment1, gate_moment1, up_moment1, down_moment1)
    seconds = (qkv_moment2, out_moment2, gate_moment2, up_moment2, down_moment2)
    bases = (qkv_basis, out_basis, gate_basis, up_basis, down_basis)
    updates = update(clip, grad_a, grad_b, masters, firsts, seconds, bases)
    return (
        pair_out[:TOK],
        pair_out[TOK:],
        grad_norm,
        norm_grads,
        norm_first,
        norm_second,
        norm_new,
        *updates,
    )


def solution(mesh):
    tok, weight, whole = P(("dp", "mp"), None), P("dp", "mp"), P()
    in_specs = (tok, tok, P("dp", None)) + (whole,) * 4 + (weight,) * 15 + (P("mp", None, None),) * 5
    out_specs = (tok, tok) + (whole,) * 5 + (weight,) * 20
    return jax.shard_map(body, mesh=mesh, in_specs=in_specs, out_specs=out_specs, check_vma=False)
```

```python
import jax
import jax.numpy as jnp
from jax import lax
from jax.experimental import pallas as pl
from jax.experimental.pallas import tpu as pltpu
from jax.sharding import PartitionSpec as P

MESH = pl.DeviceIdType.MESH
BF = jnp.bfloat16
F32 = jnp.float32

HEAD_DIM = 64
ROT = 16
STEP = 5

NORM_EPSILON = 1e-05
BETA_ONE = 0.5
BETA_TWO = 0.5
ADAM_EPS = 1e-08
WEIGHT_DECAY = 0.01
RATE_LIST = (0.02, 0.1, 0.02, 0.02, 0.015)
NORM_RATE = 0.2
CLIP_LIMIT = 1.0
MASK_FILL = -1e30
ROWS_DIMS = (((0,), (0,)), ((), ()))
COLS_DIMS = (((1,), (1,)), ((), ()))

D = 2048
LEN = 512
ROWS = 64
TOK = 128
GROUP = 1024
HEADS = 4
CA = 2176
CB = 1024
CHUNKS = ((1, 0, 512), (1, 512, 512), (0, 0, 512), (0, 512, 512), (0, 1024, 512), (0, 1536, 640))


def place():
    dp = lax.axis_index("dp")
    mp = lax.axis_index("mp")
    return (mp // 2) * 2 + dp // 16, dp % 4, (dp // 4) % 4, mp % 2


def device(x, y, z, c):
    return ((x % 2) * 16 + z * 4 + y, (x // 2) * 2 + c)


def near(me, name):
    x, y, z, c = me
    return {
        "y+": lambda: device(x, (y + 1) % 4, z, c),
        "y-": lambda: device(x, (y + 3) % 4, z, c),
        "z+": lambda: device(x, y, (z + 1) % 4, c),
        "z-": lambda: device(x, y, (z + 3) % 4, c),
        "x+": lambda: device((x + 1) % 4, y, z, c),
        "x-": lambda: device((x + 3) % 4, y, z, c),
        "c": lambda: device(x, y, z, 1 - c),
        "p": lambda: device((x // 2) * 2 + 1 - x % 2, y, z, c),
    }[name]()


NEIGHBOURS = ("y+", "y-", "z+", "z-", "x+", "x-", "c")


class Wires:
    def __init__(self, me, send, recv):
        self.me, self.send, self.recv = me, send, recv
        self.count = 0
        self.open = []

    def push(self, src, dst, to, at=None):
        if at is None:
            at = self.count
            self.count += 1
        if isinstance(to, str):
            to = near(self.me, to)
        copy = pltpu.make_async_remote_copy(
            src, dst, self.send.at[at], self.recv.at[at], device_id=to, device_id_type=MESH
        )
        copy.start()
        self.open.append(copy)
        return copy

    def take(self, number):
        at = self.count
        self.count += number
        return at

    def close(self):
        for copy in self.open:
            copy.wait_send()


WIDTHS = (1536, 512, 1408, 1408, 1408)


def pieces():
    table = [[], [], [], [], []]
    for half in range(2):
        for head in range(HEADS):
            for kind in range(3):
                table[0].append((0, half, kind * 256 + head * 64))
        for head in range(HEADS):
            table[1].append((1, half, head * 64))
    gate = [768 + 64 * k for k in range(6)] + [1536 + 64 * k for k in range(4)]
    up = [1152 + 64 * k for k in range(6)] + [1792 + 64 * k for k in range(4)]
    down = [256 + 64 * k for k in range(10)]
    for n, (i, starts, rest) in enumerate(((0, gate, 2048), (0, up, 2112), (1, down, 896))):
        table[2 + n] += [(i, 0, start) for start in starts]
        table[2 + n] += [(i, 0, rest), (i, 1, rest)]
        table[2 + n] += [(i, 1, start) for start in starts]
    return table


def reorder(staged, tiles, flips, store, rows=TOK):
    left = lax.broadcasted_iota(jnp.int32, (1, 128), 1) < 64
    for k in range(D // 128):
        sides = []
        for side in range(2):
            n = 2 * k + side
            tile = staged[tiles[n]][:rows]
            sides.append(jnp.where(flips[n : n + 1, :] > 0.0, pltpu.roll(tile, 64, 1), tile))
        store(pl.ds(k * 128, 128), jnp.where(left, sides[0], sides[1]))


def stage_tiles(staged, value, rows):
    for k in range(D // 128):
        staged[k, rows, :] = value[:, k * 128 : k * 128 + 128].astype(F32)


def places(order):
    spots = jnp.arange(32, dtype=jnp.int32)
    flips = ((order + spots) % 2).astype(F32)
    return order // 2, jnp.broadcast_to(flips[:, None], (32, 128))


LOADS = ((0, 0, 768), (1, 0, 256), (0, 768, 768), (1, 256, 768), (0, 1536, 640))


def swapped(field, lane):
    return jnp.where(lane % ROT < ROT // 2, pltpu.roll(field, 120, 1), pltpu.roll(field, ROT // 2, 1))


def gather_kernel(
    tiles, flips, tokens, cotangent, params, doc, freq, qkv_w, out_w, gate_w, up_w, down_w,
    wall_a, wall_b, toks, made, back, tokens_out, params_out,
    own_a, own_b, v_wall_a, v_wall_b, v_toks, pre_a, pre_b, docs, cosine, sine, bias, inputs, staged,
    send, recv, keep,
):
    me = x, y, z, c = place()
    xlo, xhi = x % 2, x // 2
    wires = Wires(me, send, recv)
    owns, walls, v_walls = (own_a, own_b), (wall_a, wall_b), (v_wall_a, v_wall_b)
    late = []
    lane = lax.broadcasted_iota(jnp.int32, (1, 128), 1)
    mine = [lane < HEAD_DIM, lane >= HEAD_DIM]
    four = ("y+", "y-", "z+", "z-")

    def local(src, dst):
        copy = pltpu.make_async_copy(src, dst, keep.at[len(late)])
        copy.start()
        late.append(copy)

    barrier = pltpu.get_barrier_semaphore()
    for name in NEIGHBOURS:
        pl.semaphore_signal(barrier, inc=1, device_id=near(me, name), device_id_type=MESH)

    sources = {}
    for weight, table in zip((qkv_w, out_w, gate_w, up_w, down_w), pieces()):
        for n, spot in enumerate(table):
            sources[spot] = (weight, n)
    def arrange(chunk):
        i, c0, cn = chunk
        for half in range(2):
            for column in range(c0, c0 + cn, 128):
                sides = []
                for side in range(2):
                    spot = (i, half, column + 64 * side)
                    if spot not in sources:
                        sides.append(jnp.zeros((ROWS, 128), F32))
                        continue
                    weight, n = sources[spot]
                    tile = weight[:, pl.ds(n // 2 * 128, 128)]
                    sides.append(tile if n % 2 == side else pltpu.roll(tile, 64, 1))
                owns[i][half, :, pl.ds(column, 128)] = jnp.where(mine[0], sides[0], sides[1]).astype(BF)


    axes = (("y+", "y-", "z+", "z-"), ("z+", "z-", "y+", "y-"))
    own_first = wires.take(8 * len(LOADS))
    swaps, forwards, seconds, lasts = {}, {}, {}, {}
    lo, hi = slice(0, ROWS // 2), slice(ROWS // 2, ROWS)

    def rows(half, zz, yy, part=slice(0, ROWS)):
        block = half * 16 + zz * 4 + yy
        return pl.ds(pl.multiple_of(block * ROWS + part.start, 32), part.stop - part.start)

    def block(n, half, a, b, part=slice(0, ROWS)):
        i, c0, cn = LOADS[n]
        at = rows(0, b, a, part) if half == 0 else rows(1, a, b, part)
        return v_walls[i].at[at, pl.ds(c0, cn)]

    def spots(half):
        return (y, z) if half == 0 else (z, y)

    def own_at(n, half, d):
        return own_first + n * 8 + half * 4 + d

    def own_block(n, half):
        i, c0, cn = LOADS[n]
        return v_walls[i].at[rows(half, z, y), pl.ds(c0, cn)]

    def send_own(n):
        i, c0, cn = LOADS[n]
        cols = pl.ds(c0, cn)
        own = owns[i].at[xlo, :, cols]
        for d, name in enumerate(four):
            wires.push(own, own_block(n, xlo), name, own_at(n, xlo, d))
        swaps[n] = wires.push(owns[i].at[1 - xlo, :, cols], own_block(n, xlo), "p")
        v_walls[i][rows(xlo, z, y), cols] = owns[i][xlo, :, cols]

    def send_swapped(n):
        swaps[n].wait_recv()
        for d, name in enumerate(four):
            wires.push(own_block(n, 1 - xlo), own_block(n, 1 - xlo), name, own_at(n, 1 - xlo, d))

    def wait_own(n, half, name):
        at = own_at(n, half, four.index(name))
        pltpu.make_async_remote_copy(
            own_block(n, half), own_block(n, half), send.at[at], recv.at[at],
            device_id=near(me, name), device_id_type=MESH,
        ).wait_recv()

    def hop1(n):
        for half in range(2):
            a, b = spots(half)
            f_up, f_down, s_up, s_down = axes[half]
            wait_own(n, half, f_up)
            part = block(n, half, (a + 3) % 4, b, lo)
            forwards[n, half, 0] = wires.push(part, part, f_up)
            wait_own(n, half, f_down)
            part = block(n, half, (a + 1) % 4, b, hi)
            forwards[n, half, 1] = wires.push(part, part, f_down)
            for j, spot in ((1, (a + 3) % 4), (2, (a + 1) % 4)):
                item = block(n, half, spot, b)
                seconds[n, half, j, 0] = wires.push(item, item, s_up)
                seconds[n, half, j, 1] = wires.push(item, item, s_down)

    def hop2(n):
        for half in range(2):
            a, b = spots(half)
            s_up, s_down = axes[half][2:]
            forwards[n, half, 0].wait_recv()
            forwards[n, half, 1].wait_recv()
            item = block(n, half, (a + 2) % 4, b)
            seconds[n, half, 3, 0] = wires.push(item, item, s_up)
            seconds[n, half, 3, 1] = wires.push(item, item, s_down)

    def hop3(n, steps=(0, 1, 2, 3)):
        for j in steps:
            for half in range(2):
                a, b = spots(half)
                s_up, s_down = axes[half][2:]
                spot = (a + (0, 3, 1, 2)[j]) % 4
                for d, name in ((0, s_up), (1, s_down)):
                    if j == 0:
                        wait_own(n, half, name)
                    else:
                        seconds[n, half, j, d].wait_recv()
                    part = block(n, half, spot, (b + 3) % 4 if d == 0 else (b + 1) % 4, lo if d == 0 else hi)
                    lasts[n, half, j, d] = wires.push(part, part, name)

    def arrived(n):
        for j in range(4):
            for half in range(2):
                for d in range(2):
                    lasts[n, half, j, d].wait_recv()
        i, c0, cn = LOADS[n]
        local(v_walls[i].at[:, pl.ds(c0, cn)], walls[i].at[:, pl.ds(c0, cn)])


    tok_x, tok_f, tok_c = {}, {}, []

    def tok_at(sx, cc, start=0, size=TOK):
        return pl.ds(pl.multiple_of(((sx % 2) * 4 + (sx // 2) * 2 + cc) * TOK + start, 64), size)

    def tokens_start():
        def keep_tokens(cols, value):
            inputs[:, cols] = value
            tokens_out[:, cols] = value.astype(BF)

        def keep_cotangent(cols, value):
            v_toks[1, tok_at(x, c), cols] = value.astype(BF)

        def keep_params(cols, value):
            params_out[:, cols] = value

        every = pl.ds(0, TOK)
        stage_tiles(staged, tokens, every)
        reorder(staged, tiles, flips, keep_tokens)
        stage_tiles(staged, cotangent, every)
        reorder(staged, tiles, flips, keep_cotangent)
        stage_tiles(staged, params, pl.ds(0, 8))
        reorder(staged, tiles, flips, keep_params, 8)

        def step(g, carry):
            at = pl.ds(pl.multiple_of(g * 16, 16), 16)
            item = inputs[at, :]
            centered = item - jnp.mean(item, -1, keepdims=True)
            variance = jnp.mean(centered * centered, -1, keepdims=True)
            standard = centered * lax.rsqrt(variance + NORM_EPSILON)
            normed = standard * params_out[0:1, :] + params_out[1:2, :]
            v_toks[0, pl.ds(pl.multiple_of((xlo * 4 + xhi * 2 + c) * TOK + g * 16, 16), 16), :] = normed.astype(BF)
            return carry

        lax.fori_loop(0, TOK // 16, step, 0)
        for k in range(2):
            item = v_toks.at[k, tok_at(x, c)]
            for name in ("x+", "x-"):
                tok_x[k, name] = wires.push(item, item, name)
            tok_c.append(wires.push(item, item, "c"))

    def tokens_forward():
        for k in range(2):
            for n, name in enumerate(("x+", "x-")):
                tok_x[k, name].wait_recv()
                sx = (x + 3) % 4 if n == 0 else (x + 1) % 4
                item = v_toks.at[k, tok_at(sx, c)]
                part = v_toks.at[k, tok_at(sx, c, n * (TOK // 2), TOK // 2)]
                tok_f[k, n] = wires.push(part, part, name)
                tok_c.append(wires.push(item, item, "c"))

    def tokens_last():
        for k in range(2):
            tok_f[k, 0].wait_recv()
            tok_f[k, 1].wait_recv()
            item = v_toks.at[k, tok_at((x + 2) % 4, c)]
            tok_c.append(wires.push(item, item, "c"))
        for copy in tok_c:
            copy.wait_recv()
        local(v_toks, toks)


    def product(n):
        i, c0, cn = LOADS[n]
        pre = (pre_a, pre_b)[i]

        def step(g, carry):
            at = pl.ds(pl.multiple_of(g * 256, 256), 256)
            pre[at, pl.ds(c0, cn)] = jnp.dot(
                v_toks[i, at, :], v_walls[i][:, pl.ds(c0, cn)], preferred_element_type=F32
            )
            return carry

        lax.fori_loop(0, GROUP // 256, step, 0)

    def doc_start(s, index, shape):
        start = jnp.zeros(shape, F32)
        end = jnp.zeros((1, 1), F32)
        for j in range(3):
            end = end + docs[s, 0:1, j : j + 1]
            start = jnp.where(index >= end, end, start)
        return start

    def tables():
        for s in range(2):
            index = lax.broadcasted_iota(jnp.int32, (LEN, 128), 0).astype(F32)
            angle = (index - doc_start(s, index, (LEN, 128))) * freq[0:1, :]
            entry = lane % HEAD_DIM
            turn = jnp.sin(angle)
            cosine[pl.ds(s * LEN, LEN), :] = jnp.where(entry < ROT, jnp.cos(angle), 1.0)
            sine[pl.ds(s * LEN, LEN), :] = jnp.where(
                entry < ROT // 2, -turn, jnp.where(entry < ROT, turn, 0.0)
            )

    def mask(s):
        query_at = lax.broadcasted_iota(jnp.int32, (1, LEN), 1).astype(F32)
        key_at = lax.broadcasted_iota(jnp.int32, (LEN, 1), 0).astype(F32)
        start = doc_start(s, query_at, (1, LEN))
        bias[...] = jnp.where((key_at >= start) & (key_at <= query_at), 0.0, MASK_FILL)

    def attend(s, pair):
        at_rows = pl.ds(s * LEN, LEN)
        cos_rows = cosine[at_rows, :]
        sin_rows = sine[at_rows, :]

        def turned(at):
            field = pre_a[at_rows, pl.ds(at, 128)]
            return field * cos_rows + swapped(field, lane) * sin_rows

        at = pair * 128
        query = (turned(at) * (HEAD_DIM**-0.5)).astype(BF)
        key = turned(256 + at).astype(BF)
        value = pre_a[at_rows, pl.ds(512 + at, 128)].astype(BF)
        d_attn = pre_b[at_rows, pl.ds(at, 128)].astype(BF)
        key_t = key.T
        value_t = value.T
        d_key = [None, None]
        d_value = [None, None]
        zero = jnp.zeros((), BF)
        head_row = lax.broadcasted_iota(jnp.int32, (128, 1), 0) < HEAD_DIM
        for block in range(2):
            queries = slice(block * 256, block * 256 + 256)
            keys = (block + 1) * 256
            attn_t = []
            d_query_t = []
            for h in range(2):
                query_h = jnp.where(mine[h], query[queries], zero)
                d_attn_h = jnp.where(mine[h], d_attn[queries], zero)
                scores = lax.dot_general(key[:keys], query_h, COLS_DIMS, preferred_element_type=F32)
                scores = scores + bias[0:keys, queries]
                peak = jnp.max(scores, 0, keepdims=True)
                expo = jnp.exp(scores - peak)
                probs = expo * (1.0 / jnp.sum(expo, 0, keepdims=True))
                probs_low = probs.astype(BF)
                d_prob = lax.dot_general(value[:keys], d_attn_h, COLS_DIMS, preferred_element_type=F32)
                delta = jnp.sum(probs * d_prob, 0, keepdims=True)
                d_score = (probs * (d_prob - delta)).astype(BF)
                attn_t.append(jnp.dot(value_t[:, :keys], probs_low, preferred_element_type=F32))
                d_query_t.append(jnp.dot(key_t[:, :keys], d_score, preferred_element_type=F32))
                d_value_h = jnp.dot(probs_low, d_attn_h, preferred_element_type=F32)
                d_key_h = jnp.dot(d_score, query_h, preferred_element_type=F32)
                for p in range(block + 1):
                    part = slice(p * 256, p * 256 + 256)
                    d_value[p] = d_value_h[part] if d_value[p] is None else d_value[p] + d_value_h[part]
                    d_key[p] = d_key_h[part] if d_key[p] is None else d_key[p] + d_key_h[part]
            out_rows = pl.ds(s * LEN + block * 256, 256)
            made[out_rows, pl.ds(at, 128)] = jnp.where(head_row, attn_t[0], attn_t[1]).T.astype(BF)
            d_query = jnp.where(head_row, d_query_t[0], d_query_t[1]).T * (HEAD_DIM**-0.5)
            d_query = d_query * cosine[out_rows, :] - swapped(d_query, lane) * sine[out_rows, :]
            back[out_rows, pl.ds(at, 128)] = d_query.astype(BF)
        d_key = jnp.concatenate(d_key, 0)
        d_key = d_key * cos_rows - swapped(d_key, lane) * sin_rows
        back[at_rows, pl.ds(256 + at, 128)] = d_key.astype(BF)
        back[at_rows, pl.ds(512 + at, 128)] = jnp.concatenate(d_value, 0).astype(BF)

    def unit(gate, up, d_hidden):
        sigma = jax.nn.sigmoid(gate)
        silu = gate * sigma
        return silu * up, d_hidden * up * sigma * (1.0 + gate * (1.0 - sigma)), d_hidden * silu

    def units(gate_at, width, down_at, rest):
        def step(g, carry):
            at = pl.ds(pl.multiple_of(g * 32, 32), 32)
            gates, ups, downs = pl.ds(gate_at, width), pl.ds(gate_at + width, width), pl.ds(down_at, width)
            hidden, d_gate, d_up = unit(pre_a[at, gates], pre_a[at, ups], pre_b[at, downs])
            made[at, downs] = hidden.astype(BF)
            back[at, gates] = d_gate.astype(BF)
            back[at, ups] = d_up.astype(BF)
            if rest:
                both = pre_a[at, pl.ds(2048, 128)]
                hidden, d_gate, d_up = unit(both, pltpu.roll(both, 64, 1), pre_b[at, pl.ds(896, 128)])
                made[at, pl.ds(896, 128)] = jnp.where(mine[0], hidden, 0.0).astype(BF)
                back[at, pl.ds(2048, 128)] = jnp.where(mine[0], d_gate, pltpu.roll(d_up, 64, 1)).astype(BF)
            return carry

        lax.fori_loop(0, GROUP // 32, step, 0)


    arrange(LOADS[0])
    arrange(LOADS[1])
    pl.semaphore_wait(barrier, len(NEIGHBOURS))
    send_own(0)
    doc_swap = wires.push(doc, docs.at[xlo], "p")
    docs[xlo] = doc[...]
    send_own(1)
    tokens_start()
    send_swapped(0)
    send_swapped(1)
    arrange(LOADS[2])
    send_own(2)
    hop1(0)
    arrange(LOADS[3])
    send_own(3)
    send_swapped(2)
    hop1(1)
    arrange(LOADS[4])
    send_own(4)
    hop2(0)
    doc_swap.wait_recv()
    tables()
    tokens_forward()
    hop3(0)
    hop2(1)
    hop1(2)
    tokens_last()
    hop3(1)
    send_swapped(3)
    arrived(0)
    product(0)
    hop2(2)
    hop1(3)
    arrived(1)
    product(1)
    mask(0)
    attend(0, 0)
    hop3(2, (0, 1))
    send_swapped(4)
    attend(0, 1)
    hop3(2, (2, 3))
    hop2(3)
    mask(1)
    attend(1, 0)
    hop1(4)
    arrived(2)
    product(2)
    hop3(3)
    hop2(4)
    attend(1, 1)
    hop3(4, (0, 1))
    arrived(3)
    product(3)
    hop3(4, (2, 3))
    units(768, 384, 256, False)
    arrived(4)
    product(4)
    units(1536, 256, 640, True)
    wires.close()
    for copy in late:
        copy.wait()


def gather_all(tiles, flips, tokens, cotangent, params, doc, freq, weights):
    any_ = pl.BlockSpec(memory_space=pl.ANY)
    vmem = pl.BlockSpec(memory_space=pltpu.VMEM)
    return pl.pallas_call(
        gather_kernel,
        out_shape=(
            jax.ShapeDtypeStruct((D, CA), BF),
            jax.ShapeDtypeStruct((D, CB), BF),
            jax.ShapeDtypeStruct((2, GROUP, D), BF),
            jax.ShapeDtypeStruct((GROUP, CB), BF),
            jax.ShapeDtypeStruct((GROUP, CA), BF),
            jax.ShapeDtypeStruct((TOK, D), BF),
            jax.ShapeDtypeStruct((8, D), F32),
        ),
        in_specs=[pl.BlockSpec(memory_space=pltpu.SMEM)] + [vmem] * 11,
        out_specs=(any_, any_, any_, vmem, vmem, vmem, vmem),
        scratch_shapes=[
            pltpu.VMEM((2, ROWS, CA), BF),
            pltpu.VMEM((2, ROWS, CB), BF),
            pltpu.VMEM((D, CA), BF),
            pltpu.VMEM((D, CB), BF),
            pltpu.VMEM((2, GROUP, D), BF),
            pltpu.VMEM((GROUP, CA), F32),
            pltpu.VMEM((GROUP, CB), F32),
            pltpu.VMEM((2, 8, 128), F32),
            pltpu.VMEM((GROUP, 128), F32),
            pltpu.VMEM((GROUP, 128), F32),
            pltpu.VMEM((LEN, LEN), F32),
            pltpu.VMEM((TOK, D), F32),
            pltpu.VMEM((D // 128, TOK, 128), F32),
            pltpu.SemaphoreType.DMA((230,)),
            pltpu.SemaphoreType.DMA((230,)),
            pltpu.SemaphoreType.DMA((8,)),
        ],
        compiler_params=pltpu.CompilerParams(
            collective_id=0, has_side_effects=True, vmem_limit_bytes=62 * 2**20
        ),
    )(tiles, flips, tokens, cotangent, params, doc, freq, *weights)


def add_rows(dst, src, rows, cols):
    def step(g, carry):
        at = pl.ds(pl.multiple_of(g * 16, 16), 16)
        dst[at, cols] = (dst[at, cols].astype(F32) + src[at, cols].astype(F32)).astype(dst.dtype)
        return carry

    lax.fori_loop(0, rows // 16, step, 0)


def peers(me):
    x, y, z, c = me
    here, there = z * 4 + y, x * 2 + c
    plane, line = [], []
    for k in range(1, 16):
        at = (here + k) % 16
        plane.append(device(x, at % 4, at // 4, c))
    for k in range(1, 8):
        at = (there + k) % 8
        line.append(device(at // 2, y, z, at % 2))
    return here, there, plane, line


FEATS = 256


def scatter_kernel(
    tiles, flips, made, back, toks, wall_a, wall_b, tokens, gains,
    grad_a, grad_b, tok_out, norm_out, square_out,
    v_act, v_made, v_back, v_wall_a, v_wall_b, part_a, part_b, stage,
    r1_a, r1_b, r2_a, r2_b, t1_a, t1_b, t2_a, t2_b, sum_a, sum_b,
    own, core, x1, x2, norm1, norm2, square1, square2, shown, cotangent,
    send, recv, keep, load,
):
    me = x, y, z, c = place()
    xlo = x % 2
    wires = Wires(me, send, recv)
    parts, grads = (part_a, part_b), (grad_a, grad_b)
    r1, r2 = (r1_a, r1_b), (r2_a, r2_b)
    t1, t2, sums = (t1_a, t1_b), (t2_a, t2_b), (sum_a, sum_b)
    late = []
    here, there, plane, line = peers(me)

    def fetch(src, dst, sem):
        for side in range(2):
            for g in range(4):
                at = g * 256 + (c if side == 0 else 1 - c) * TOK
                pltpu.make_async_copy(
                    src.at[pl.ds(at, TOK)], dst.at[pl.ds(side * 512 + g * TOK, TOK)], load.at[sem]
                ).start()

    def fetched(dst, sem):
        pltpu.make_async_copy(dst, dst, load.at[sem]).wait()

    def wall_copy(i, f):
        wall, buf = ((wall_a, v_wall_a), (wall_b, v_wall_b))[i]
        return pltpu.make_async_copy(
            wall.at[pl.ds(f * FEATS, FEATS)], buf.at[f % 2], load.at[4 + 2 * i + f % 2]
        )

    own_rows = pl.ds(pl.multiple_of((xlo * 4 + x // 2 * 2 + c) * TOK, TOK), TOK)
    pltpu.make_async_copy(toks.at[pl.ds(1, 1), own_rows], cotangent, load.at[3]).start()
    fetch(toks.at[1], v_act, 0)
    fetch(made, v_made, 1)
    fetch(back, v_back, 2)
    for i in (1, 0):
        for f in range(2):
            wall_copy(i, f).start()

    barrier = pltpu.get_barrier_semaphore()
    for to in plane + line:
        pl.semaphore_signal(barrier, inc=1, device_id=to, device_id_type=MESH)
    pl.semaphore_wait(barrier, 22)
    axes = (("z+", "z-", "y+", "y-"), ("y+", "y-", "z+", "z-"))

    def spots(half):
        return (z, y) if half == 0 else (y, z)

    def piece(half, chunk, spot, start, size):
        i, c0, cn = chunk
        cols = pl.ds(c0, cn)
        if half == 0:
            return parts[i].at[0, spot, pl.ds(start, size), :, cols]
        return parts[i].at[1, pl.ds(start, size), spot, :, cols]

    state = {}

    def product(n):
        i, c0, cn = CHUNKS[n]
        right = (v_back, v_made)[i]

        def step(f, carry):
            feats = pl.ds(pl.multiple_of(f * FEATS, FEATS), FEATS)
            got = lax.dot_general(
                v_act[:, feats], right[:, pl.ds(c0, cn)], ROWS_DIMS, preferred_element_type=F32
            )
            parts[i][f // 4, f % 4, :, :, pl.ds(c0, cn)] = got.astype(BF).reshape(4, ROWS, cn)
            return carry

        lax.fori_loop(0, D // FEATS, step, 0)

    def branch(k, blocks):
        i = 1 - k
        left, buf = (v_back, v_made)[i], (v_wall_a, v_wall_b)[i]
        for f in blocks:
            wall_copy(i, f).wait()
            feats = pl.ds(f * FEATS, FEATS)
            for side in range(2):
                got = lax.dot_general(
                    left[pl.ds(side * 512, 512), :], buf[f % 2], COLS_DIMS, preferred_element_type=F32
                )
                got = got.astype(BF).reshape(2, 2, TOK, FEATS)
                if side == 0:
                    own[k, :, :, :, feats] = got
                else:
                    stage[:, :, :, feats] = got
            if f + 2 < D // FEATS:
                wall_copy(i, f + 2).start()

    def cross(k):
        state["c", k] = wires.push(stage, core.at[k], "c")

    def stage0(n, half):
        chunk = i, c0, cn = CHUNKS[n]
        p, q = spots(half)
        up, down = axes[half][:2]
        cols = pl.ds(c0, cn)
        state["a", n, half, 0] = wires.push(
            piece(half, chunk, (p + 2) % 4, 0, 2), r1[i].at[half, 0, :, :, cols], up
        )
        state["a", n, half, 1] = wires.push(
            piece(half, chunk, (p + 2) % 4, 2, 2), r1[i].at[half, 1, :, :, cols], down
        )
        state["b", n, half, 0] = wires.push(
            piece(half, chunk, (p + 1) % 4, 2, 2), r2[i].at[half, 0, pl.ds(2, 2), :, cols], up
        )
        state["b", n, half, 1] = wires.push(
            piece(half, chunk, (p + 3) % 4, 0, 2), r2[i].at[half, 1, pl.ds(0, 2), :, cols], down
        )

    def stage1(n, half):
        chunk = i, c0, cn = CHUNKS[n]
        cols = pl.ds(c0, cn)
        p, q = spots(half)
        for d in range(2):
            state["a", n, half, d].wait_recv()
            spot = (p + 1) % 4 if d == 0 else (p + 3) % 4
            for m in range(2):
                block = 2 * d + m
                mine = parts[i].at[0, spot, block] if half == 0 else parts[i].at[1, block, spot]
                add_rows(mine, r1[i].at[half, d, m], ROWS, cols)
            state["s", n, half, d] = wires.push(
                piece(half, chunk, spot, 2 * d, 2), r2[i].at[half, d, pl.ds(2 * d, 2), :, cols], axes[half][d]
            )

    def kept(i, half, p, q):
        return parts[i].at[0, p, q] if half == 0 else parts[i].at[1, q, p]

    def stage2(n, half):
        i, c0, cn = CHUNKS[n]
        cols = pl.ds(c0, cn)
        p, q = spots(half)
        up, down = axes[half][2:]
        for d in range(2):
            state["b", n, half, d].wait_recv()
            state["s", n, half, d].wait_recv()

        def step(g, carry):
            at = pl.ds(pl.multiple_of((g % 4) * 16, 16), 16)
            m = g // 4
            mine = kept(i, half, p, m)
            total = (
                mine[at, cols].astype(F32)
                + r2[i][half, 0, m, at, cols].astype(F32)
                + r2[i][half, 1, m, at, cols].astype(F32)
            )
            mine[at, cols] = total.astype(BF)
            return carry

        lax.fori_loop(0, 16, step, 0)
        lo, hi = pl.ds(0, ROWS // 2), pl.ds(ROWS // 2, ROWS // 2)
        far = kept(i, half, p, (q + 2) % 4)
        state["t", n, half, 0] = wires.push(far.at[lo, cols], t1[i].at[half, 0, :, cols], up)
        state["t", n, half, 1] = wires.push(far.at[hi, cols], t1[i].at[half, 1, :, cols], down)
        state["u", n, half, 0] = wires.push(
            kept(i, half, p, (q + 1) % 4).at[hi, cols], t2[i].at[half, 0, hi, cols], up
        )
        state["u", n, half, 1] = wires.push(
            kept(i, half, p, (q + 3) % 4).at[lo, cols], t2[i].at[half, 1, lo, cols], down
        )

    def stage3(n, half):
        i, c0, cn = CHUNKS[n]
        cols = pl.ds(c0, cn)
        p, q = spots(half)
        for d in range(2):
            state["t", n, half, d].wait_recv()
            rows = pl.ds(d * (ROWS // 2), ROWS // 2)
            mine = kept(i, half, p, (q + 1) % 4 if d == 0 else (q + 3) % 4).at[rows]
            add_rows(mine, t1[i].at[half, d], ROWS // 2, cols)
            state["v", n, half, d] = wires.push(
                mine.at[:, cols], t2[i].at[half, d, rows, cols], axes[half][2 + d]
            )

    def stage4(n, half):
        i, c0, cn = CHUNKS[n]
        cols = pl.ds(c0, cn)
        p, q = spots(half)
        for d in range(2):
            state["u", n, half, d].wait_recv()
            state["v", n, half, d].wait_recv()
        mine = kept(i, half, p, q)

        def step(g, carry):
            at = pl.ds(pl.multiple_of(g * 16, 16), 16)
            total = (
                mine[at, cols].astype(F32)
                + t2[i][half, 0, at, cols].astype(F32)
                + t2[i][half, 1, at, cols].astype(F32)
            )
            sums[i][half, at, cols] = total
            squares = total * total
            for m in range(cn // 128):
                part = squares[:, m * 128 : m * 128 + 128]
                carry = carry + part[:8] + part[8:]
            return carry

        return lax.fori_loop(0, ROWS // 16, step, jnp.zeros((8, 128), F32))

    def stage5(n):
        i, c0, cn = CHUNKS[n]
        cols = pl.ds(c0, cn)
        state["g", n] = wires.push(sums[i].at[1 - xlo, :, cols], grads[i].at[xlo, :, cols], "p")
        copy = pltpu.make_async_copy(sums[i].at[xlo, :, cols], grads[i].at[xlo, :, cols], keep.at[n])
        copy.start()
        late.append(copy)

    half_tok = TOK // 2

    def tokens1(k):
        state["c", k].wait_recv()

        def step(g, carry):
            at = pl.ds(pl.multiple_of((g % 8) * 16, 16), 16)
            s = g // 8
            own[k, s // 2, s % 2, at, :] = (
                own[k, s // 2, s % 2, at, :].astype(F32) + core[k, s // 2, s % 2, at, :].astype(F32)
            ).astype(BF)
            return carry

        lax.fori_loop(0, 32, step, 0)

        def spot(s, d, far):
            rows = pl.ds((d if far else 1 - d) * half_tok, half_tok)
            return own.at[k, s % 2, s // 2, rows]

        for d, name in enumerate(("x+", "x-")):
            state["x1", k, d] = wires.push(spot((x + 2) % 4, d, True), x1.at[k, d], name)
        for d, name in enumerate(("x+", "x-")):
            to = (x + 1) % 4 if d == 0 else (x + 3) % 4
            rows = pl.ds((1 - d) * half_tok, half_tok)
            state["x2", k, d] = wires.push(spot(to, d, False), x2.at[k, d, rows], name)

    def tokens2(k):
        for d, name in enumerate(("x+", "x-")):
            state["x1", k, d].wait_recv()
            to = (x + 1) % 4 if d == 0 else (x + 3) % 4
            rows = pl.ds(d * half_tok, half_tok)
            mine = own.at[k, to % 2, to // 2, rows]
            add_rows(mine, x1.at[k, d], half_tok, pl.ds(0, D))
            state["x3", k, d] = wires.push(mine, x2.at[k, d, rows], name)

    def tokens3(k):
        for d in range(2):
            state["x2", k, d].wait_recv()
            state["x3", k, d].wait_recv()

        def total(at):
            return (
                own[k, xlo, x // 2, at, :].astype(F32)
                + x2[k, 0, at, :].astype(F32)
                + x2[k, 1, at, :].astype(F32)
            )

        def result(g, carry):
            at = pl.ds(pl.multiple_of(g * 16, 16), 16)
            stage_tiles(shown, tokens[at, :].astype(F32) + total(at), at)
            return carry

        def gradient(g, carry):
            at = pl.ds(pl.multiple_of(g * 16, 16), 16)
            inputs = tokens[at, :].astype(F32)
            centered = inputs - jnp.mean(inputs, -1, keepdims=True)
            variance = jnp.mean(centered * centered, -1, keepdims=True)
            deviation = lax.rsqrt(variance + NORM_EPSILON)
            standard = centered * deviation
            d_normed = total(at)
            d_standard = d_normed * gains[0:1, :]
            gradient_rows = cotangent[0, at, :].astype(F32) + deviation * (
                d_standard
                - jnp.mean(d_standard, -1, keepdims=True)
                - standard * jnp.mean(d_standard * standard, -1, keepdims=True)
            )
            stage_tiles(shown, gradient_rows, at)
            return (
                carry[0] + jnp.sum(d_normed * standard, 0, keepdims=True),
                carry[1] + jnp.sum(d_normed, 0, keepdims=True),
            )

        if k == 0:
            lax.fori_loop(0, TOK // 16, result, 0)
        else:
            zero = jnp.zeros((1, D), F32)
            gain_sum, shift_sum = lax.fori_loop(0, TOK // 16, gradient, (zero, zero))
            norm1[here, 0:1, :] = gain_sum
            norm1[here, 1:2, :] = shift_sum

        def show(cols, value):
            tok_out[k, :, cols] = value.astype(BF)

        reorder(shown, tiles, flips, show)

    def small1(slots):
        return [wires.push(slots.at[here], slots.at[here], to) for to in plane]

    def small2(copies, slots, after):
        for copy in copies:
            copy.wait_recv()
        total = slots[0]
        for k in range(1, 16):
            total = total + slots[k]
        after[there] = total
        return [wires.push(after.at[there], after.at[there], to) for to in line]

    def small3(copies, after):
        for copy in copies:
            copy.wait_recv()
        total = after[0]
        for k in range(1, 8):
            total = total + after[k]
        return total

    def both(step, n):
        for half in range(2):
            step(n, half)

    squares = [jnp.zeros((8, 128), F32)]

    def last(n):
        for half in range(2):
            squares[0] = squares[0] + stage4(n, half)
        stage5(n)

    fetched(v_act, 0)
    fetched(v_made, 1)
    fetched(cotangent, 3)
    product(0)
    both(stage0, 0)
    product(1)
    both(stage0, 1)
    fetch(toks.at[0], v_act, 0)
    branch(0, range(8))
    cross(0)
    fetched(v_act, 0)
    fetched(v_back, 2)
    product(2)
    both(stage0, 2)
    both(stage1, 0)
    product(3)
    both(stage0, 3)
    both(stage1, 1)
    tokens1(0)
    product(4)
    both(stage0, 4)
    both(stage2, 0)
    product(5)
    both(stage0, 5)
    both(stage1, 2)
    state["c", 0].wait_send()
    wires.open = [copy for copy in wires.open if copy is not state["c", 0]]
    branch(1, range(4))
    both(stage2, 1)
    tokens2(0)
    both(stage3, 0)
    branch(1, range(4, 8))
    cross(1)
    both(stage1, 3)
    both(stage2, 2)
    both(stage3, 1)
    last(0)
    tokens1(1)
    both(stage1, 4)
    both(stage2, 3)
    both(stage3, 2)
    tokens3(0)
    last(1)
    both(stage1, 5)
    tokens2(1)
    both(stage2, 4)
    both(stage3, 3)
    last(2)
    tokens3(1)
    norm_copies = small1(norm1)
    both(stage2, 5)
    both(stage3, 4)
    last(3)
    norm_copies = small2(norm_copies, norm1, norm2)
    both(stage3, 5)
    last(4)
    last(5)
    square1[here] = squares[0]
    square_copies = small1(square1)
    stage_tiles(shown, small3(norm_copies, norm2), pl.ds(0, 2))

    def show_norm(cols, value):
        norm_out[:, cols] = value

    reorder(shown, tiles, flips, show_norm, 8)
    square_copies = small2(square_copies, square1, square2)
    square_out[...] = small3(square_copies, square2)
    for n in range(len(CHUNKS)):
        state["g", n].wait_recv()
    wires.close()
    for copy in late:
        copy.wait()


def scatter_all(tiles, flips, made, back, toks, wall_a, wall_b, tokens, gains):
    any_ = pl.BlockSpec(memory_space=pl.ANY)
    vmem = pl.BlockSpec(memory_space=pltpu.VMEM)

    def both(*shape, dtype=BF):
        return [pltpu.VMEM(shape + (CA,), dtype), pltpu.VMEM(shape + (CB,), dtype)]

    return pl.pallas_call(
        scatter_kernel,
        out_shape=(
            jax.ShapeDtypeStruct((2, ROWS, CA), F32),
            jax.ShapeDtypeStruct((2, ROWS, CB), F32),
            jax.ShapeDtypeStruct((2, TOK, D), BF),
            jax.ShapeDtypeStruct((8, D), F32),
            jax.ShapeDtypeStruct((8, 128), F32),
        ),
        in_specs=[pl.BlockSpec(memory_space=pltpu.SMEM), vmem] + [any_] * 5 + [vmem] * 2,
        out_specs=(any_, any_, vmem, vmem, vmem),
        scratch_shapes=[
            pltpu.VMEM((GROUP, D), BF),
            pltpu.VMEM((GROUP, CB), BF),
            pltpu.VMEM((GROUP, CA), BF),
            pltpu.VMEM((2, FEATS, CA), BF),
            pltpu.VMEM((2, FEATS, CB), BF),
            *both(2, 4, 4, ROWS),
            pltpu.VMEM((2, 2, TOK, D), BF),
            *both(2, 2, 2, ROWS),
            *both(2, 2, 4, ROWS),
            *both(2, 2, ROWS // 2),
            *both(2, 2, ROWS),
            *both(2, ROWS, dtype=F32),
            pltpu.VMEM((2, 2, 2, TOK, D), BF),
            pltpu.VMEM((2, 2, 2, TOK, D), BF),
            pltpu.VMEM((2, 2, TOK // 2, D), BF),
            pltpu.VMEM((2, 2, TOK, D), BF),
            pltpu.VMEM((16, 2, D), F32),
            pltpu.VMEM((8, 2, D), F32),
            pltpu.VMEM((16, 8, 128), F32),
            pltpu.VMEM((8, 8, 128), F32),
            pltpu.VMEM((D // 128, TOK, 128), F32),
            pltpu.VMEM((1, TOK, D), BF),
            pltpu.SemaphoreType.DMA((224,)),
            pltpu.SemaphoreType.DMA((224,)),
            pltpu.SemaphoreType.DMA((8,)),
            pltpu.SemaphoreType.DMA((8,)),
        ],
        compiler_params=pltpu.CompilerParams(
            collective_id=1, has_side_effects=True, vmem_limit_bytes=62 * 2**20
        ),
    )(tiles, flips, made, back, toks, wall_a, wall_b, tokens, gains)


def halves(item):
    high = item.astype(BF)
    return high, (item - high.astype(F32)).astype(BF)


def near_product(left, right, dims):
    (a, a_low), (b, b_low) = left, right
    axis = 0 if dims == (((1,), (0,)), ((), ())) else 1
    return lax.dot_general(
        jnp.concatenate([a, a, a_low], 1),
        jnp.concatenate([b, b_low, b], axis),
        dims,
        preferred_element_type=F32,
    )


def update_kernel(squares, norm_raw, norm_params, norm_moment1, norm_moment2, grad_a, grad_b, *refs):
    weights, firsts, seconds, bases = refs[0:5], refs[5:10], refs[10:15], refs[15:20]
    refs = refs[20:]
    grad_norm, norm_grads, norm_first, norm_second, norm_new = refs[:5]
    grads, firsts_new, seconds_new, weights_new = refs[5:10], refs[10:15], refs[15:20], refs[20:25]
    parts = (grad_a, grad_b)
    left_lanes = lax.broadcasted_iota(jnp.int32, (1, 128), 1) < 64

    def whole(item):
        return jnp.sum(jnp.sum(item, 0, keepdims=True), 1, keepdims=True)

    raw = norm_raw[0:2, :]
    length = jnp.sqrt(whole(squares[...]) + whole(raw * raw))
    clip = jnp.minimum(1.0, CLIP_LIMIT / length)
    grad_norm[...] = length
    norm_grads[...] = clip * raw
    norm_first[...], norm_second[...], norm_new[...] = adam_plain(
        norm_params[...], clip * raw, norm_moment1[...], norm_moment2[...], NORM_RATE
    )

    def fetch(piece, side):
        i, half, column = piece
        tile = parts[i][half, :, pl.ds(column // 128 * 128, 128)]
        return tile if column // 64 % 2 == side else pltpu.roll(tile, 64, 1)

    for i, table in enumerate(pieces()):
        for block in range(WIDTHS[i] // 128):
            cols = pl.ds(block * 128, 128)
            one, two = table[2 * block], table[2 * block + 1]
            if two == one[:2] + (one[2] + 64,) and one[2] % 128 == 0:
                grad = parts[one[0]][one[1], :, pl.ds(one[2], 128)]
            else:
                grad = jnp.where(left_lanes, fetch(one, 0), fetch(two, 1))
            grad = clip * grad
            grads[i][:, cols] = grad
            basis = halves(bases[i][block])
            turned = near_product(halves(grad), basis, (((1,), (0,)), ((), ())))
            first = BETA_ONE * firsts[i][:, cols] + (1.0 - BETA_ONE) * turned
            second = BETA_TWO * seconds[i][:, cols] + (1.0 - BETA_TWO) * turned * turned
            firsts_new[i][:, cols] = first
            seconds_new[i][:, cols] = second
            ratio = (
                first
                * (1.0 / (1.0 - BETA_ONE**STEP))
                / (jnp.sqrt(second * (1.0 / (1.0 - BETA_TWO**STEP))) + ADAM_EPS)
            )
            turned_back = near_product(halves(ratio), basis, COLS_DIMS)
            weight = weights[i][:, cols]
            weights_new[i][:, cols] = weight - RATE_LIST[i] * (turned_back + WEIGHT_DECAY * weight)


def update(squares, norm, grad_a, grad_b, weights, firsts, seconds, bases):
    vmem = pl.BlockSpec(memory_space=pltpu.VMEM)
    shapes = [jax.ShapeDtypeStruct((ROWS, width), F32) for width in WIDTHS]
    small = [jax.ShapeDtypeStruct((1, 1), F32)] + [jax.ShapeDtypeStruct((2, D), F32)] * 4
    return pl.pallas_call(
        update_kernel,
        out_shape=tuple(small + shapes * 4),
        in_specs=[vmem] * 27,
        out_specs=(vmem,) * 25,
        compiler_params=pltpu.CompilerParams(vmem_limit_bytes=56 * 2**20),
    )(squares, *norm, grad_a, grad_b, *weights, *firsts, *seconds, *bases)


def adam_plain(param, grad, first, second, rate):
    first_new = BETA_ONE * first + (1.0 - BETA_ONE) * grad
    second_new = BETA_TWO * second + (1.0 - BETA_TWO) * grad * grad
    ratio = (
        first_new
        / (1.0 - BETA_ONE**STEP)
        / (jnp.sqrt(second_new / (1.0 - BETA_TWO**STEP)) + ADAM_EPS)
    )
    return (first_new, second_new, param - rate * ratio)


def body(
    tokens,
    cotangent,
    doc_lengths,
    row_owner,
    norm_params,
    norm_moment1,
    norm_moment2,
    qkv_weight,
    out_weight,
    gate_weight,
    up_weight,
    down_weight,
    qkv_moment1,
    out_moment1,
    gate_moment1,
    up_moment1,
    down_moment1,
    qkv_moment2,
    out_moment2,
    gate_moment2,
    up_moment2,
    down_moment2,
    qkv_basis,
    out_basis,
    gate_basis,
    up_basis,
    down_basis,
):
    blocks = jnp.arange(32, dtype=jnp.int32)
    inverse = jnp.sum((row_owner[None, :] == blocks[:, None]) * blocks[None, :], 1)
    doc_item = jnp.pad(doc_lengths.astype(F32), ((0, 7), (0, 124)))
    entry = jnp.arange(128, dtype=jnp.int32) % (ROT // 2)
    freq = jnp.broadcast_to(10000.0 ** (-2.0 * entry.astype(F32) / ROT), (8, 128))
    weights = (qkv_weight, out_weight, gate_weight, up_weight, down_weight)
    wall_a, wall_b, toks, made, back, tokens_stored, params_stored = gather_all(
        *places(inverse), tokens, cotangent, jnp.pad(norm_params, ((0, 6), (0, 0))), doc_item, freq, weights
    )
    grad_a, grad_b, tok_out, norm_raw, squares = scatter_all(
        *places(row_owner), made, back, toks, wall_a, wall_b, tokens_stored, params_stored
    )
    firsts = (qkv_moment1, out_moment1, gate_moment1, up_moment1, down_moment1)
    seconds = (qkv_moment2, out_moment2, gate_moment2, up_moment2, down_moment2)
    bases = (qkv_basis, out_basis, gate_basis, up_basis, down_basis)
    norm = (norm_raw, norm_params, norm_moment1, norm_moment2)
    grad_norm, *rest = update(squares, norm, grad_a, grad_b, weights, firsts, seconds, bases)
    return (tok_out[0], tok_out[1], grad_norm[0, 0], *rest)


def solution(mesh):
    tok, weight, whole = P(("dp", "mp"), None), P("dp", "mp"), P()
    in_specs = (tok, tok, P("dp", None)) + (whole,) * 4 + (weight,) * 15 + (P("mp", None, None),) * 5
    out_specs = (tok, tok) + (whole,) * 5 + (weight,) * 20
    return jax.shard_map(body, mesh=mesh, in_specs=in_specs, out_specs=out_specs, check_vma=False)
```

```python
import jax
import jax.numpy as jnp
from jax import lax
from jax.experimental import pallas as pl
from jax.experimental.pallas import tpu as pltpu
from jax.sharding import PartitionSpec as P

MESH = pl.DeviceIdType.MESH
BF = jnp.bfloat16
F32 = jnp.float32

HEAD_DIM = 64
ROT = 16
STEP = 5

NORM_EPSILON = 1e-05
BETA_ONE = 0.5
BETA_TWO = 0.5
ADAM_EPS = 1e-08
WEIGHT_DECAY = 0.01
RATE_LIST = (0.02, 0.1, 0.02, 0.02, 0.015)
NORM_RATE = 0.2
CLIP_LIMIT = 1.0
MASK_FILL = -1e30
ROWS_DIMS = (((0,), (0,)), ((), ()))
COLS_DIMS = (((1,), (1,)), ((), ()))

D = 2048
LEN = 512
ROWS = 64
TOK = 128
GROUP = 1024
HEADS = 4
CA = 2176
CB = 1024
CHUNKS = ((1, 0, 512), (1, 512, 512), (0, 0, 512), (0, 512, 512), (0, 1024, 512), (0, 1536, 640))


def place():
    dp = lax.axis_index("dp")
    mp = lax.axis_index("mp")
    return (mp // 2) * 2 + dp // 16, dp % 4, (dp // 4) % 4, mp % 2


def device(x, y, z, c):
    return ((x % 2) * 16 + z * 4 + y, (x // 2) * 2 + c)


def near(me, name):
    x, y, z, c = me
    return {
        "y+": lambda: device(x, (y + 1) % 4, z, c),
        "y-": lambda: device(x, (y + 3) % 4, z, c),
        "z+": lambda: device(x, y, (z + 1) % 4, c),
        "z-": lambda: device(x, y, (z + 3) % 4, c),
        "x+": lambda: device((x + 1) % 4, y, z, c),
        "x-": lambda: device((x + 3) % 4, y, z, c),
        "c": lambda: device(x, y, z, 1 - c),
        "p": lambda: device((x // 2) * 2 + 1 - x % 2, y, z, c),
    }[name]()


NEIGHBOURS = ("y+", "y-", "z+", "z-", "x+", "x-", "c")


class Wires:
    def __init__(self, me, send, recv):
        self.me, self.send, self.recv = me, send, recv
        self.count = 0
        self.open = []

    def push(self, src, dst, to, at=None):
        if at is None:
            at = self.count
            self.count += 1
        if isinstance(to, str):
            to = near(self.me, to)
        copy = pltpu.make_async_remote_copy(
            src, dst, self.send.at[at], self.recv.at[at], device_id=to, device_id_type=MESH
        )
        copy.start()
        self.open.append(copy)
        return copy

    def take(self, number):
        at = self.count
        self.count += number
        return at

    def close(self):
        for copy in self.open:
            copy.wait_send()


WIDTHS = (1536, 512, 1408, 1408, 1408)


def pieces():
    table = [[], [], [], [], []]
    for half in range(2):
        for head in range(HEADS):
            for kind in range(3):
                table[0].append((0, half, head // 2 * 384 + kind * 128 + head % 2 * 64))
        for head in range(HEADS):
            table[1].append((1, half, head * 64))
    gate = [768 + 64 * k for k in range(6)] + [1536 + 64 * k for k in range(4)]
    up = [1152 + 64 * k for k in range(6)] + [1792 + 64 * k for k in range(4)]
    down = [256 + 64 * k for k in range(10)]
    for n, (i, starts, rest) in enumerate(((0, gate, 2048), (0, up, 2112), (1, down, 896))):
        table[2 + n] += [(i, 0, start) for start in starts]
        table[2 + n] += [(i, 0, rest), (i, 1, rest)]
        table[2 + n] += [(i, 1, start) for start in starts]
    return table


def reorder(staged, tiles, flips, store, rows=TOK):
    left = lax.broadcasted_iota(jnp.int32, (1, 128), 1) < 64
    for k in range(D // 128):
        sides = []
        for side in range(2):
            n = 2 * k + side
            tile = staged[tiles[n]][:rows]
            sides.append(jnp.where(flips[n : n + 1, :] > 0.0, pltpu.roll(tile, 64, 1), tile))
        store(pl.ds(k * 128, 128), jnp.where(left, sides[0], sides[1]))


def stage_tiles(staged, value, rows):
    for k in range(D // 128):
        staged[k, rows, :] = value[:, k * 128 : k * 128 + 128].astype(F32)


def places(order):
    spots = jnp.arange(32, dtype=jnp.int32)
    flips = ((order + spots) % 2).astype(F32)
    return order // 2, jnp.broadcast_to(flips[:, None], (32, 128))


LOADS = ((0, 0, 384), (1, 0, 256), (0, 384, 384), (1, 256, 768), (0, 768, 768), (0, 1536, 640))


GATHER_ORDER = (
    ("AG", 2), ("OWN", 2), ("AG", 3), ("AG", 1), ("OWN", 1), ("OWN", 3), ("TS", 1), ("AG", 4), ("SW", 2),
    ("H1", 2, 0), ("AG", 5), ("AG", 0), ("OWN", 0), ("H3", 2, 0, 0), ("SW", 1), ("H1", 1, 0), ("SW", 3),
    ("H1", 3, 0), ("H3", 3, 0, 0), ("TS", 0), ("H3", 2, 0, 2), ("H2", 1, 0), ("H3", 3, 1, 0), ("H3", 2, 1, 0),
    ("H1", 1, 1), ("H3", 1, 0, 0), ("TB",), ("H1", 3, 1), ("H2", 3, 0), ("H3", 1, 1, 1), ("H3", 1, 0, 2),
    ("H1", 2, 1), ("H3", 1, 0, 1), ("H3", 1, 1, 2), ("OWN", 5), ("TF", 1), ("H3", 3, 0, 1), ("H3", 1, 1, 0),
    ("OWN", 4), ("H2", 2, 0), ("SW", 0), ("H1", 0, 0), ("H3", 2, 0, 1), ("H3", 0, 0, 0), ("H3", 3, 1, 1),
    ("H3", 3, 0, 2), ("H3", 3, 1, 2), ("H3", 1, 0, 3), ("H2", 1, 1), ("H3", 2, 1, 1), ("H3", 2, 1, 2),
    ("H2", 3, 1), ("H3", 3, 0, 3), ("H2", 2, 1), ("TF", 0), ("H3", 0, 1, 0), ("H2", 0, 0), ("SW", 5),
    ("H1", 5, 0), ("H3", 5, 0, 0), ("H3", 2, 0, 3), ("H3", 1, 1, 3), ("H1", 0, 1), ("H3", 0, 0, 1),
    ("H3", 0, 0, 2), ("H3", 3, 1, 3), ("SW", 4), ("H3", 4, 0, 0), ("TL", 1), ("H3", 2, 1, 3), ("H3", 5, 1, 0),
    ("H1", 4, 0), ("ARR", 1), ("H3", 0, 0, 3), ("H2", 5, 0), ("PR", 1), ("H3", 0, 1, 2), ("H1", 5, 1),
    ("ARR", 3), ("H3", 5, 0, 1), ("H3", 0, 1, 1), ("TL", 0), ("PR", 3), ("ARR", 2), ("H2", 0, 1),
    ("H2", 4, 0), ("H3", 4, 1, 0), ("PR", 2), ("H1", 4, 1), ("AT", 3), ("H3", 5, 1, 1), ("H3", 0, 1, 3),
    ("AT", 2), ("H3", 4, 1, 2), ("H3", 5, 0, 3), ("H3", 4, 1, 1), ("H3", 4, 0, 1), ("H3", 4, 0, 2),
    ("H2", 5, 1), ("H3", 5, 1, 2), ("H3", 5, 0, 2), ("ARR", 0), ("PR", 0), ("AT", 1), ("H2", 4, 1),
    ("H3", 5, 1, 3), ("AT", 0), ("H3", 4, 0, 3), ("H3", 4, 1, 3), ("ARR", 5), ("PR", 5), ("ARR", 4),
    ("PR", 4), ("U", 0), ("U", 1),
)


def swapped(field, lane):
    return jnp.where(lane % ROT < ROT // 2, pltpu.roll(field, 120, 1), pltpu.roll(field, ROT // 2, 1))


def gather_kernel(
    tiles, flips, tokens, cotangent, params, doc, freq, qkv_w, out_w, gate_w, up_w, down_w,
    wall_a, wall_b, toks, made, back, tokens_out, params_out,
    own_a, own_b, v_wall_a, v_wall_b, v_toks, v_made, v_back, pre_a, pre_b, docs, cosine, sine, bias, inputs, staged,
    send, recv, keep,
):
    me = x, y, z, c = place()
    xlo, xhi = x % 2, x // 2
    wires = Wires(me, send, recv)
    owns, walls, v_walls = (own_a, own_b), (wall_a, wall_b), (v_wall_a, v_wall_b)
    late = []
    lane = lax.broadcasted_iota(jnp.int32, (1, 128), 1)
    mine = [lane < HEAD_DIM, lane >= HEAD_DIM]

    def local(src, dst):
        copy = pltpu.make_async_copy(src, dst, keep.at[len(late)])
        copy.start()
        late.append(copy)

    barrier = pltpu.get_barrier_semaphore()
    for name in NEIGHBOURS:
        pl.semaphore_signal(barrier, inc=1, device_id=near(me, name), device_id_type=MESH)

    sources = {}
    for weight, table in zip((qkv_w, out_w, gate_w, up_w, down_w), pieces()):
        for n, spot in enumerate(table):
            sources[spot] = (weight, n)
    def arrange(chunk):
        i, c0, cn = chunk
        for half in range(2):
            for column in range(c0, c0 + cn, 128):
                sides = []
                for side in range(2):
                    spot = (i, half, column + 64 * side)
                    if spot not in sources:
                        sides.append(jnp.zeros((ROWS, 128), F32))
                        continue
                    weight, n = sources[spot]
                    tile = weight[:, pl.ds(n // 2 * 128, 128)]
                    sides.append(tile if n % 2 == side else pltpu.roll(tile, 64, 1))
                owns[i][half, :, pl.ds(column, 128)] = jnp.where(mine[0], sides[0], sides[1]).astype(BF)


    own_first = wires.take(8 * len(LOADS))
    swaps, forwards, seconds, lasts = {}, {}, {}, {}
    lo, hi = slice(0, ROWS // 2), slice(ROWS // 2, ROWS)

    def half_of(part):
        return (xlo + part) % 2

    def way(part, d):
        half = half_of(part)
        along_y = 1 - half if d < 2 else half
        move = 1 if d % 2 == 0 else 3
        return device(x, (y + along_y * move) % 4, (z + (1 - along_y) * move) % 4, c)

    def spots(part):
        half = half_of(part)
        return y + half * (z - y), z + half * (y - z)

    def block(n, part, a, b, some=slice(0, ROWS)):
        i, c0, cn = LOADS[n]
        half = half_of(part)
        at = half * 16 + (b + half * (a - b)) * 4 + a + half * (b - a)
        at = pl.ds(pl.multiple_of(at * ROWS + some.start, 32), some.stop - some.start)
        return v_walls[i].at[at, pl.ds(c0, cn)]

    def own_at(n, part, d):
        return own_first + n * 8 + part * 4 + d

    def own_block(n, part):
        a, b = spots(part)
        return block(n, part, a, b)

    def send_own(n):
        i, c0, cn = LOADS[n]
        cols = pl.ds(c0, cn)
        own = owns[i].at[xlo, :, cols]
        for d in range(4):
            wires.push(own, own_block(n, 0), way(0, d), own_at(n, 0, d))
        swaps[n] = wires.push(owns[i].at[1 - xlo, :, cols], own_block(n, 0), "p")
        v_walls[i][pl.ds(pl.multiple_of((xlo * 16 + z * 4 + y) * ROWS, ROWS), ROWS), cols] = owns[i][xlo, :, cols]

    def send_swapped(n):
        swaps[n].wait_recv()
        for d in range(4):
            wires.push(own_block(n, 1), own_block(n, 1), way(1, d), own_at(n, 1, d))

    def wait_own(n, part, d):
        at = own_at(n, part, d)
        pltpu.make_async_remote_copy(
            own_block(n, part), own_block(n, part), send.at[at], recv.at[at],
            device_id=way(part, d), device_id_type=MESH,
        ).wait_recv()

    def hop1(n, part):
        a, b = spots(part)
        wait_own(n, part, 0)
        some = block(n, part, (a + 3) % 4, b, lo)
        forwards[n, part, 0] = wires.push(some, some, way(part, 0))
        wait_own(n, part, 1)
        some = block(n, part, (a + 1) % 4, b, hi)
        forwards[n, part, 1] = wires.push(some, some, way(part, 1))
        for j, spot in ((1, (a + 3) % 4), (2, (a + 1) % 4)):
            item = block(n, part, spot, b)
            seconds[n, part, j, 0] = wires.push(item, item, way(part, 2))
            seconds[n, part, j, 1] = wires.push(item, item, way(part, 3))

    def hop2(n, part):
        a, b = spots(part)
        forwards[n, part, 0].wait_recv()
        forwards[n, part, 1].wait_recv()
        item = block(n, part, (a + 2) % 4, b)
        seconds[n, part, 3, 0] = wires.push(item, item, way(part, 2))
        seconds[n, part, 3, 1] = wires.push(item, item, way(part, 3))

    def hop3(n, part, j):
        a, b = spots(part)
        spot = (a + (0, 3, 1, 2)[j]) % 4
        for d in range(2):
            if j == 0:
                wait_own(n, part, 2 + d)
            else:
                seconds[n, part, j, d].wait_recv()
            some = block(n, part, spot, (b + 3) % 4 if d == 0 else (b + 1) % 4, lo if d == 0 else hi)
            lasts[n, part, j, d] = wires.push(some, some, way(part, 2 + d))

    def arrived(n):
        for j in range(4):
            for part in range(2):
                for d in range(2):
                    lasts[n, part, j, d].wait_recv()
        i, c0, cn = LOADS[n]
        local(v_walls[i].at[:, pl.ds(c0, cn)], walls[i].at[:, pl.ds(c0, cn)])


    tok_x, tok_f, tok_c = {}, {}, [[], []]
    whole = [False, False]

    def tok_at(sx, cc, start=0, size=TOK):
        return pl.ds(pl.multiple_of(((sx % 2) * 4 + (sx // 2) * 2 + cc) * TOK + start, 64), size)

    def tokens_start(k):
        def keep_tokens(cols, value):
            inputs[:, cols] = value
            tokens_out[:, cols] = value.astype(BF)

        def keep_cotangent(cols, value):
            v_toks[1, tok_at(x, c), cols] = value.astype(BF)

        def keep_params(cols, value):
            params_out[:, cols] = value

        def step(g, carry):
            at = pl.ds(pl.multiple_of(g * 16, 16), 16)
            item = inputs[at, :]
            centered = item - jnp.mean(item, -1, keepdims=True)
            variance = jnp.mean(centered * centered, -1, keepdims=True)
            standard = centered * lax.rsqrt(variance + NORM_EPSILON)
            normed = standard * params_out[0:1, :] + params_out[1:2, :]
            v_toks[0, pl.ds(pl.multiple_of((xlo * 4 + xhi * 2 + c) * TOK + g * 16, 16), 16), :] = normed.astype(BF)
            return carry

        every = pl.ds(0, TOK)
        if k == 0:
            stage_tiles(staged, params, pl.ds(0, 8))
            reorder(staged, tiles, flips, keep_params, 8)
            stage_tiles(staged, tokens, every)
            reorder(staged, tiles, flips, keep_tokens)
            lax.fori_loop(0, TOK // 16, step, 0)
        else:
            stage_tiles(staged, cotangent, every)
            reorder(staged, tiles, flips, keep_cotangent)
        item = v_toks.at[k, tok_at(x, c)]
        for name in ("x+", "x-"):
            tok_x[k, name] = wires.push(item, item, name)
        tok_c[k].append(wires.push(item, item, "c"))

    def tokens_forward(k):
        for n, name in enumerate(("x+", "x-")):
            tok_x[k, name].wait_recv()
            sx = (x + 3) % 4 if n == 0 else (x + 1) % 4
            item = v_toks.at[k, tok_at(sx, c)]
            part = v_toks.at[k, tok_at(sx, c, n * (TOK // 2), TOK // 2)]
            tok_f[k, n] = wires.push(part, part, name)
            tok_c[k].append(wires.push(item, item, "c"))

    def tokens_last(k):
        tok_f[k, 0].wait_recv()
        tok_f[k, 1].wait_recv()
        item = v_toks.at[k, tok_at((x + 2) % 4, c)]
        tok_c[k].append(wires.push(item, item, "c"))

    def tokens_whole(k):
        if whole[k]:
            return
        whole[k] = True
        for copy in tok_c[k]:
            copy.wait_recv()
        local(v_toks.at[k], toks.at[k])


    def product(n):
        i, c0, cn = LOADS[n]
        tokens_whole(i)
        pre = (pre_a, pre_b)[i]

        def step(g, carry):
            at = pl.ds(pl.multiple_of(g * 256, 256), 256)
            pre[at, pl.ds(c0, cn)] = jnp.dot(
                v_toks[i, at, :], v_walls[i][:, pl.ds(c0, cn)], preferred_element_type=F32
            )
            return carry

        lax.fori_loop(0, GROUP // 256, step, 0)

    def flush(src, dst, at, cols):
        local(src.at[at, cols], dst.at[at, cols])

    def doc_start(s, index, shape):
        start = jnp.zeros(shape, F32)
        end = jnp.zeros((1, 1), F32)
        for j in range(3):
            end = end + docs[s, 0:1, j : j + 1]
            start = jnp.where(index >= end, end, start)
        return start

    def tables():
        doc_swap[0].wait_recv()
        for s in range(2):
            mask(s)
            index = lax.broadcasted_iota(jnp.int32, (LEN, 128), 0).astype(F32)
            angle = (index - doc_start(s, index, (LEN, 128))) * freq[0:1, :]
            entry = lane % HEAD_DIM
            turn = jnp.sin(angle)
            cosine[pl.ds(s * LEN, LEN), :] = jnp.where(entry < ROT, jnp.cos(angle), 1.0)
            sine[pl.ds(s * LEN, LEN), :] = jnp.where(
                entry < ROT // 2, -turn, jnp.where(entry < ROT, turn, 0.0)
            )

    def mask(s):
        query_at = lax.broadcasted_iota(jnp.int32, (1, LEN), 1).astype(F32)
        key_at = lax.broadcasted_iota(jnp.int32, (LEN, 1), 0).astype(F32)
        start = doc_start(s, query_at, (1, LEN))
        bias[s] = jnp.where((key_at >= start) & (key_at <= query_at), 0.0, MASK_FILL)

    def attend(k):
        s, pair = k % 2, k // 2
        at_rows = pl.ds(s * LEN, LEN)
        cos_rows = cosine[at_rows, :]
        sin_rows = sine[at_rows, :]

        def turned(at):
            field = pre_a[at_rows, pl.ds(at, 128)]
            return field * cos_rows + swapped(field, lane) * sin_rows

        at, first = pair * 128, pair * 384
        query = (turned(first) * (HEAD_DIM**-0.5)).astype(BF)
        key = turned(first + 128).astype(BF)
        value = pre_a[at_rows, pl.ds(first + 256, 128)].astype(BF)
        d_attn = pre_b[at_rows, pl.ds(at, 128)].astype(BF)
        key_t = key.T
        value_t = value.T
        d_key = [None, None]
        d_value = [None, None]
        zero = jnp.zeros((), BF)
        head_row = lax.broadcasted_iota(jnp.int32, (128, 1), 0) < HEAD_DIM
        for block in range(2):
            queries = slice(block * 256, block * 256 + 256)
            keys = (block + 1) * 256
            attn_t = []
            d_query_t = []
            for h in range(2):
                query_h = jnp.where(mine[h], query[queries], zero)
                d_attn_h = jnp.where(mine[h], d_attn[queries], zero)
                scores = lax.dot_general(key[:keys], query_h, COLS_DIMS, preferred_element_type=F32)
                scores = scores + bias[s, 0:keys, queries]
                peak = jnp.max(scores, 0, keepdims=True)
                expo = jnp.exp(scores - peak)
                probs = expo * (1.0 / jnp.sum(expo, 0, keepdims=True))
                probs_low = probs.astype(BF)
                d_prob = lax.dot_general(value[:keys], d_attn_h, COLS_DIMS, preferred_element_type=F32)
                delta = jnp.sum(probs * d_prob, 0, keepdims=True)
                d_score = (probs * (d_prob - delta)).astype(BF)
                attn_t.append(jnp.dot(value_t[:, :keys], probs_low, preferred_element_type=F32))
                d_query_t.append(jnp.dot(key_t[:, :keys], d_score, preferred_element_type=F32))
                d_value_h = jnp.dot(probs_low, d_attn_h, preferred_element_type=F32)
                d_key_h = jnp.dot(d_score, query_h, preferred_element_type=F32)
                for p in range(block + 1):
                    part = slice(p * 256, p * 256 + 256)
                    d_value[p] = d_value_h[part] if d_value[p] is None else d_value[p] + d_value_h[part]
                    d_key[p] = d_key_h[part] if d_key[p] is None else d_key[p] + d_key_h[part]
            out_rows = pl.ds(s * LEN + block * 256, 256)
            v_made[out_rows, pl.ds(at, 128)] = jnp.where(head_row, attn_t[0], attn_t[1]).T.astype(BF)
            d_query = jnp.where(head_row, d_query_t[0], d_query_t[1]).T * (HEAD_DIM**-0.5)
            d_query = d_query * cosine[out_rows, :] - swapped(d_query, lane) * sine[out_rows, :]
            v_back[out_rows, pl.ds(first, 128)] = d_query.astype(BF)
        d_key = jnp.concatenate(d_key, 0)
        d_key = d_key * cos_rows - swapped(d_key, lane) * sin_rows
        v_back[at_rows, pl.ds(first + 128, 128)] = d_key.astype(BF)
        v_back[at_rows, pl.ds(first + 256, 128)] = jnp.concatenate(d_value, 0).astype(BF)
        flush(v_made, made, at_rows, pl.ds(at, 128))
        flush(v_back, back, at_rows, pl.ds(first, 384))

    def unit(gate, up, d_hidden):
        sigma = jax.nn.sigmoid(gate)
        silu = gate * sigma
        return silu * up, d_hidden * up * sigma * (1.0 + gate * (1.0 - sigma)), d_hidden * silu

    def units(gate_at, width, down_at, rest):
        def step(g, carry):
            at = pl.ds(pl.multiple_of(g * 32, 32), 32)
            gates, ups, downs = pl.ds(gate_at, width), pl.ds(gate_at + width, width), pl.ds(down_at, width)
            hidden, d_gate, d_up = unit(pre_a[at, gates], pre_a[at, ups], pre_b[at, downs])
            v_made[at, downs] = hidden.astype(BF)
            v_back[at, gates] = d_gate.astype(BF)
            v_back[at, ups] = d_up.astype(BF)
            if rest:
                both = pre_a[at, pl.ds(2048, 128)]
                hidden, d_gate, d_up = unit(both, pltpu.roll(both, 64, 1), pre_b[at, pl.ds(896, 128)])
                v_made[at, pl.ds(896, 128)] = jnp.where(mine[0], hidden, 0.0).astype(BF)
                v_back[at, pl.ds(2048, 128)] = jnp.where(mine[0], d_gate, pltpu.roll(d_up, 64, 1)).astype(BF)
            return carry

        lax.fori_loop(0, GROUP // 32, step, 0)
        every = pl.ds(0, GROUP)
        flush(v_made, made, every, pl.ds(down_at, width + (128 if rest else 0)))
        flush(v_back, back, every, pl.ds(gate_at, 2 * width + (128 if rest else 0)))


    doc_swap = [wires.take(1)]
    steps = {
        "AG": lambda n: arrange(LOADS[n]),
        "OWN": send_own,
        "SW": send_swapped,
        "H1": hop1,
        "H2": hop2,
        "H3": hop3,
        "ARR": arrived,
        "TS": tokens_start,
        "TF": tokens_forward,
        "TL": tokens_last,
        "PR": product,
        "TB": tables,
        "AT": attend,
        "U": lambda k: units(1536, 256, 640, True) if k else units(768, 384, 256, False),
    }
    met = False
    for name, *at in GATHER_ORDER:
        if name in ("OWN", "TS") and not met:
            met = True
            pl.semaphore_wait(barrier, len(NEIGHBOURS))
            doc_swap[0] = wires.push(doc, docs.at[xlo], "p", doc_swap[0])
            docs[xlo] = doc[...]
        steps[name](*at)
    wires.close()
    for copy in late:
        copy.wait()


def gather_all(tiles, flips, tokens, cotangent, params, doc, freq, weights):
    any_ = pl.BlockSpec(memory_space=pl.ANY)
    vmem = pl.BlockSpec(memory_space=pltpu.VMEM)
    return pl.pallas_call(
        gather_kernel,
        out_shape=(
            jax.ShapeDtypeStruct((D, CA), BF),
            jax.ShapeDtypeStruct((D, CB), BF),
            jax.ShapeDtypeStruct((2, GROUP, D), BF),
            jax.ShapeDtypeStruct((GROUP, CB), BF),
            jax.ShapeDtypeStruct((GROUP, CA), BF),
            jax.ShapeDtypeStruct((TOK, D), BF),
            jax.ShapeDtypeStruct((8, D), F32),
        ),
        in_specs=[pl.BlockSpec(memory_space=pltpu.SMEM)] + [vmem] * 11,
        out_specs=(any_,) * 5 + (vmem,) * 2,
        scratch_shapes=[
            pltpu.VMEM((2, ROWS, CA), BF),
            pltpu.VMEM((2, ROWS, CB), BF),
            pltpu.VMEM((D, CA), BF),
            pltpu.VMEM((D, CB), BF),
            pltpu.VMEM((2, GROUP, D), BF),
            pltpu.VMEM((GROUP, CB), BF),
            pltpu.VMEM((GROUP, CA), BF),
            pltpu.VMEM((GROUP, CA), F32),
            pltpu.VMEM((GROUP, CB), F32),
            pltpu.VMEM((2, 8, 128), F32),
            pltpu.VMEM((GROUP, 128), F32),
            pltpu.VMEM((GROUP, 128), F32),
            pltpu.VMEM((2, LEN, LEN), F32),
            pltpu.VMEM((TOK, D), F32),
            pltpu.VMEM((D // 128, TOK, 128), F32),
            pltpu.SemaphoreType.DMA((266,)),
            pltpu.SemaphoreType.DMA((266,)),
            pltpu.SemaphoreType.DMA((32,)),
        ],
        compiler_params=pltpu.CompilerParams(
            collective_id=0, has_side_effects=True, vmem_limit_bytes=62 * 2**20
        ),
    )(tiles, flips, tokens, cotangent, params, doc, freq, *weights)


SCATTER_ORDER = (
    ("P", 1), ("A", 1), ("B", 1), ("P", 0), ("R",), ("A", 0), ("B", 0), ("BR", 0, 0), ("S1", 1), ("BR", 0, 1),
    ("BR", 0, 2), ("BR", 0, 3), ("P", 2), ("A", 2), ("B", 2), ("S1", 0), ("X", 0), ("P", 3), ("A", 3),
    ("B", 3), ("BR", 1, 0), ("BR", 1, 1), ("T1", 0), ("S1", 2), ("BR", 1, 2), ("BR", 1, 3), ("X", 1),
    ("S1", 3), ("S2", 0), ("T2", 0), ("S2", 2), ("P", 4), ("S3", 0), ("B", 4), ("S2", 3), ("A", 4), ("T1", 1),
    ("P", 5), ("B", 5), ("A", 5), ("S3", 2), ("T3", 0), ("S1", 4), ("T2", 1), ("S3", 3), ("S2", 1), ("L", 0),
    ("S1", 5), ("L", 2), ("S2", 4), ("L", 3), ("S3", 1), ("T3", 1), ("N1",), ("S2", 5), ("S3", 4), ("L", 1),
    ("N2",), ("S3", 5), ("L", 4), ("N3",), ("L", 5),
)


def add_rows(dst, src, rows, cols):
    def step(g, carry):
        at = pl.ds(pl.multiple_of(g * 16, 16), 16)
        dst[at, cols] = (dst[at, cols].astype(F32) + src[at, cols].astype(F32)).astype(dst.dtype)
        return carry

    lax.fori_loop(0, rows // 16, step, 0)


def peers(me):
    x, y, z, c = me
    here, there = z * 4 + y, x * 2 + c
    plane, line = [], []
    for k in range(1, 16):
        at = (here + k) % 16
        plane.append(device(x, at % 4, at // 4, c))
    for k in range(1, 8):
        at = (there + k) % 8
        line.append(device(at // 2, y, z, at % 2))
    return here, there, plane, line


FEATS = 256


def scatter_kernel(
    tiles, flips, made, back, toks, wall_a, wall_b, tokens, gains,
    grad_a, grad_b, tok_out, norm_out, square_out,
    v_act, v_made, v_back, v_wall_a, v_wall_b, part_a, part_b, stage,
    r1_a, r1_b, r2_a, r2_b, t1_a, t1_b, t2_a, t2_b, sum_a, sum_b,
    own, core, x1, x2, norm1, norm2, square1, square2, shown, cotangent,
    send, recv, keep, load,
):
    me = x, y, z, c = place()
    xlo = x % 2
    wires = Wires(me, send, recv)
    parts, grads = (part_a, part_b), (grad_a, grad_b)
    r1, r2 = (r1_a, r1_b), (r2_a, r2_b)
    t1, t2, sums = (t1_a, t1_b), (t2_a, t2_b), (sum_a, sum_b)
    late = []
    here, there, plane, line = peers(me)

    def fetch(src, dst, sem):
        for side in range(2):
            for g in range(4):
                at = g * 256 + (c if side == 0 else 1 - c) * TOK
                pltpu.make_async_copy(
                    src.at[pl.ds(at, TOK)], dst.at[pl.ds(side * 512 + g * TOK, TOK)], load.at[sem]
                ).start()

    def fetched(dst, sem):
        pltpu.make_async_copy(dst, dst, load.at[sem]).wait()

    def wall_copy(i, f):
        wall, buf = ((wall_a, v_wall_a), (wall_b, v_wall_b))[i]
        return pltpu.make_async_copy(
            wall.at[pl.ds(f * FEATS, FEATS)], buf.at[f % 2], load.at[4 + 2 * i + f % 2]
        )

    own_rows = pl.ds(pl.multiple_of((xlo * 4 + x // 2 * 2 + c) * TOK, TOK), TOK)
    pltpu.make_async_copy(toks.at[pl.ds(1, 1), own_rows], cotangent, load.at[3]).start()
    fetch(toks.at[1], v_act, 0)
    fetch(made, v_made, 1)
    fetch(back, v_back, 2)
    for i in (1, 0):
        for f in range(2):
            wall_copy(i, f).start()

    barrier = pltpu.get_barrier_semaphore()
    for to in plane + line:
        pl.semaphore_signal(barrier, inc=1, device_id=to, device_id_type=MESH)
    pl.semaphore_wait(barrier, 22)
    axes = (("z+", "z-", "y+", "y-"), ("y+", "y-", "z+", "z-"))

    def spots(half):
        return (z, y) if half == 0 else (y, z)

    def piece(half, chunk, spot, start, size):
        i, c0, cn = chunk
        cols = pl.ds(c0, cn)
        if half == 0:
            return parts[i].at[0, spot, pl.ds(start, size), :, cols]
        return parts[i].at[1, pl.ds(start, size), spot, :, cols]

    state = {}

    def product(n):
        i, c0, cn = CHUNKS[n]
        right = (v_back, v_made)[i]

        def step(f, carry):
            feats = pl.ds(pl.multiple_of(f * FEATS, FEATS), FEATS)
            got = lax.dot_general(
                v_act[:, feats], right[:, pl.ds(c0, cn)], ROWS_DIMS, preferred_element_type=F32
            )
            parts[i][f // 4, f % 4, :, :, pl.ds(c0, cn)] = got.astype(BF).reshape(4, ROWS, cn)
            return carry

        lax.fori_loop(0, D // FEATS, step, 0)

    def branch(k, blocks):
        i = 1 - k
        left, buf = (v_back, v_made)[i], (v_wall_a, v_wall_b)[i]
        for f in blocks:
            wall_copy(i, f).wait()
            feats = pl.ds(f * FEATS, FEATS)
            for side in range(2):
                got = lax.dot_general(
                    left[pl.ds(side * 512, 512), :], buf[f % 2], COLS_DIMS, preferred_element_type=F32
                )
                got = got.astype(BF).reshape(2, 2, TOK, FEATS)
                if side == 0:
                    own[k, :, :, :, feats] = got
                else:
                    stage[:, :, :, feats] = got
            if f + 2 < D // FEATS:
                wall_copy(i, f + 2).start()

    def cross(k):
        state["c", k] = wires.push(stage, core.at[k], "c")

    def stage0(n, half):
        chunk = i, c0, cn = CHUNKS[n]
        p, q = spots(half)
        up, down = axes[half][:2]
        cols = pl.ds(c0, cn)
        state["a", n, half, 0] = wires.push(
            piece(half, chunk, (p + 2) % 4, 0, 2), r1[i].at[half, 0, :, :, cols], up
        )
        state["a", n, half, 1] = wires.push(
            piece(half, chunk, (p + 2) % 4, 2, 2), r1[i].at[half, 1, :, :, cols], down
        )

    def stage0b(n, half):
        chunk = i, c0, cn = CHUNKS[n]
        p, q = spots(half)
        up, down = axes[half][:2]
        cols = pl.ds(c0, cn)
        state["b", n, half, 0] = wires.push(
            piece(half, chunk, (p + 1) % 4, 2, 2), r2[i].at[half, 0, pl.ds(2, 2), :, cols], up
        )
        state["b", n, half, 1] = wires.push(
            piece(half, chunk, (p + 3) % 4, 0, 2), r2[i].at[half, 1, pl.ds(0, 2), :, cols], down
        )

    def stage1(n, half):
        chunk = i, c0, cn = CHUNKS[n]
        cols = pl.ds(c0, cn)
        p, q = spots(half)
        for d in range(2):
            state["a", n, half, d].wait_recv()
            spot = (p + 1) % 4 if d == 0 else (p + 3) % 4
            for m in range(2):
                block = 2 * d + m
                mine = parts[i].at[0, spot, block] if half == 0 else parts[i].at[1, block, spot]
                add_rows(mine, r1[i].at[half, d, m], ROWS, cols)
            state["s", n, half, d] = wires.push(
                piece(half, chunk, spot, 2 * d, 2), r2[i].at[half, d, pl.ds(2 * d, 2), :, cols], axes[half][d]
            )

    def kept(i, half, p, q):
        return parts[i].at[0, p, q] if half == 0 else parts[i].at[1, q, p]

    def stage2(n, half):
        i, c0, cn = CHUNKS[n]
        cols = pl.ds(c0, cn)
        p, q = spots(half)
        up, down = axes[half][2:]
        for d in range(2):
            state["b", n, half, d].wait_recv()
            state["s", n, half, d].wait_recv()

        def step(g, carry):
            at = pl.ds(pl.multiple_of((g % 4) * 16, 16), 16)
            m = g // 4
            mine = kept(i, half, p, m)
            total = (
                mine[at, cols].astype(F32)
                + r2[i][half, 0, m, at, cols].astype(F32)
                + r2[i][half, 1, m, at, cols].astype(F32)
            )
            mine[at, cols] = total.astype(BF)
            return carry

        lax.fori_loop(0, 16, step, 0)
        lo, hi = pl.ds(0, ROWS // 2), pl.ds(ROWS // 2, ROWS // 2)
        far = kept(i, half, p, (q + 2) % 4)
        state["t", n, half, 0] = wires.push(far.at[lo, cols], t1[i].at[half, 0, :, cols], up)
        state["t", n, half, 1] = wires.push(far.at[hi, cols], t1[i].at[half, 1, :, cols], down)
        state["u", n, half, 0] = wires.push(
            kept(i, half, p, (q + 1) % 4).at[hi, cols], t2[i].at[half, 0, hi, cols], up
        )
        state["u", n, half, 1] = wires.push(
            kept(i, half, p, (q + 3) % 4).at[lo, cols], t2[i].at[half, 1, lo, cols], down
        )

    def stage3(n, half):
        i, c0, cn = CHUNKS[n]
        cols = pl.ds(c0, cn)
        p, q = spots(half)
        for d in range(2):
            state["t", n, half, d].wait_recv()
            rows = pl.ds(d * (ROWS // 2), ROWS // 2)
            mine = kept(i, half, p, (q + 1) % 4 if d == 0 else (q + 3) % 4).at[rows]
            add_rows(mine, t1[i].at[half, d], ROWS // 2, cols)
            state["v", n, half, d] = wires.push(
                mine.at[:, cols], t2[i].at[half, d, rows, cols], axes[half][2 + d]
            )

    def stage4(n, half):
        i, c0, cn = CHUNKS[n]
        cols = pl.ds(c0, cn)
        p, q = spots(half)
        for d in range(2):
            state["u", n, half, d].wait_recv()
            state["v", n, half, d].wait_recv()
        mine = kept(i, half, p, q)

        def step(g, carry):
            at = pl.ds(pl.multiple_of(g * 16, 16), 16)
            total = (
                mine[at, cols].astype(F32)
                + t2[i][half, 0, at, cols].astype(F32)
                + t2[i][half, 1, at, cols].astype(F32)
            )
            sums[i][half, at, cols] = total
            squares = total * total
            for m in range(cn // 128):
                part = squares[:, m * 128 : m * 128 + 128]
                carry = carry + part[:8] + part[8:]
            return carry

        return lax.fori_loop(0, ROWS // 16, step, jnp.zeros((8, 128), F32))

    def stage5(n):
        i, c0, cn = CHUNKS[n]
        cols = pl.ds(c0, cn)
        state["g", n] = wires.push(sums[i].at[1 - xlo, :, cols], grads[i].at[xlo, :, cols], "p")
        copy = pltpu.make_async_copy(sums[i].at[xlo, :, cols], grads[i].at[xlo, :, cols], keep.at[n])
        copy.start()
        late.append(copy)

    half_tok = TOK // 2

    def tokens1(k):
        state["c", k].wait_recv()

        def step(g, carry):
            at = pl.ds(pl.multiple_of((g % 8) * 16, 16), 16)
            s = g // 8
            own[k, s // 2, s % 2, at, :] = (
                own[k, s // 2, s % 2, at, :].astype(F32) + core[k, s // 2, s % 2, at, :].astype(F32)
            ).astype(BF)
            return carry

        lax.fori_loop(0, 32, step, 0)

        def spot(s, d, far):
            rows = pl.ds((d if far else 1 - d) * half_tok, half_tok)
            return own.at[k, s % 2, s // 2, rows]

        for d, name in enumerate(("x+", "x-")):
            state["x1", k, d] = wires.push(spot((x + 2) % 4, d, True), x1.at[k, d], name)
        for d, name in enumerate(("x+", "x-")):
            to = (x + 1) % 4 if d == 0 else (x + 3) % 4
            rows = pl.ds((1 - d) * half_tok, half_tok)
            state["x2", k, d] = wires.push(spot(to, d, False), x2.at[k, d, rows], name)

    def tokens2(k):
        for d, name in enumerate(("x+", "x-")):
            state["x1", k, d].wait_recv()
            to = (x + 1) % 4 if d == 0 else (x + 3) % 4
            rows = pl.ds(d * half_tok, half_tok)
            mine = own.at[k, to % 2, to // 2, rows]
            add_rows(mine, x1.at[k, d], half_tok, pl.ds(0, D))
            state["x3", k, d] = wires.push(mine, x2.at[k, d, rows], name)

    def tokens3(k):
        for d in range(2):
            state["x2", k, d].wait_recv()
            state["x3", k, d].wait_recv()

        def total(at):
            return (
                own[k, xlo, x // 2, at, :].astype(F32)
                + x2[k, 0, at, :].astype(F32)
                + x2[k, 1, at, :].astype(F32)
            )

        def result(g, carry):
            at = pl.ds(pl.multiple_of(g * 16, 16), 16)
            stage_tiles(shown, tokens[at, :].astype(F32) + total(at), at)
            return carry

        def gradient(g, carry):
            at = pl.ds(pl.multiple_of(g * 16, 16), 16)
            inputs = tokens[at, :].astype(F32)
            centered = inputs - jnp.mean(inputs, -1, keepdims=True)
            variance = jnp.mean(centered * centered, -1, keepdims=True)
            deviation = lax.rsqrt(variance + NORM_EPSILON)
            standard = centered * deviation
            d_normed = total(at)
            d_standard = d_normed * gains[0:1, :]
            gradient_rows = cotangent[0, at, :].astype(F32) + deviation * (
                d_standard
                - jnp.mean(d_standard, -1, keepdims=True)
                - standard * jnp.mean(d_standard * standard, -1, keepdims=True)
            )
            stage_tiles(shown, gradient_rows, at)
            return (
                carry[0] + jnp.sum(d_normed * standard, 0, keepdims=True),
                carry[1] + jnp.sum(d_normed, 0, keepdims=True),
            )

        if k == 0:
            lax.fori_loop(0, TOK // 16, result, 0)
        else:
            zero = jnp.zeros((1, D), F32)
            gain_sum, shift_sum = lax.fori_loop(0, TOK // 16, gradient, (zero, zero))
            norm1[here, 0:1, :] = gain_sum
            norm1[here, 1:2, :] = shift_sum

        def show(cols, value):
            tok_out[k, :, cols] = value.astype(BF)

        reorder(shown, tiles, flips, show)

    def small1(slots):
        return [wires.push(slots.at[here], slots.at[here], to) for to in plane]

    def small2(copies, slots, after):
        for copy in copies:
            copy.wait_recv()
        total = slots[0]
        for k in range(1, 16):
            total = total + slots[k]
        after[there] = total
        return [wires.push(after.at[there], after.at[there], to) for to in line]

    def small3(copies, after):
        for copy in copies:
            copy.wait_recv()
        total = after[0]
        for k in range(1, 8):
            total = total + after[k]
        return total

    def both(step, n):
        for half in range(2):
            step(n, half)

    squares = [jnp.zeros((8, 128), F32)]

    def last(n):
        for half in range(2):
            squares[0] = squares[0] + stage4(n, half)
        stage5(n)

    fetched(v_act, 0)
    fetched(v_made, 1)
    fetched(cotangent, 3)
    waiting = [True]
    norm_copies = [None]

    def next_product(n):
        if CHUNKS[n][0] == 0 and waiting[0]:
            waiting[0] = False
            fetched(v_act, 0)
            fetched(v_back, 2)
        product(n)

    def some_branch(k, j):
        if k == 1 and j == 0:
            if waiting[0]:
                fetched(v_back, 2)
                waiting[0] = False
                fetched(v_act, 0)
            state["c", 0].wait_send()
            wires.open = [copy for copy in wires.open if copy is not state["c", 0]]
        branch(k, range(2 * j, 2 * j + 2))

    def norm_step(number):
        if number == 1:
            norm_copies[0] = small1(norm1)
        elif number == 2:
            norm_copies[0] = small2(norm_copies[0], norm1, norm2)
        else:
            stage_tiles(shown, small3(norm_copies[0], norm2), pl.ds(0, 2))

            def show_norm(cols, value):
                norm_out[:, cols] = value

            reorder(shown, tiles, flips, show_norm, 8)

    steps = {
        "P": next_product,
        "R": lambda: fetch(toks.at[0], v_act, 0),
        "A": lambda n: both(stage0, n),
        "B": lambda n: both(stage0b, n),
        "S1": lambda n: both(stage1, n),
        "S2": lambda n: both(stage2, n),
        "S3": lambda n: both(stage3, n),
        "L": last,
        "BR": some_branch,
        "X": cross,
        "T1": tokens1,
        "T2": tokens2,
        "T3": tokens3,
        "N1": lambda: norm_step(1),
        "N2": lambda: norm_step(2),
        "N3": lambda: norm_step(3),
    }
    for name, *at in SCATTER_ORDER:
        steps[name](*at)
    square1[here] = squares[0]
    square_copies = small1(square1)
    square_copies = small2(square_copies, square1, square2)
    square_out[...] = small3(square_copies, square2)
    for n in range(len(CHUNKS)):
        state["g", n].wait_recv()
    wires.close()
    for copy in late:
        copy.wait()


def scatter_all(tiles, flips, made, back, toks, wall_a, wall_b, tokens, gains):
    any_ = pl.BlockSpec(memory_space=pl.ANY)
    vmem = pl.BlockSpec(memory_space=pltpu.VMEM)

    def both(*shape, dtype=BF):
        return [pltpu.VMEM(shape + (CA,), dtype), pltpu.VMEM(shape + (CB,), dtype)]

    return pl.pallas_call(
        scatter_kernel,
        out_shape=(
            jax.ShapeDtypeStruct((2, ROWS, CA), F32),
            jax.ShapeDtypeStruct((2, ROWS, CB), F32),
            jax.ShapeDtypeStruct((2, TOK, D), BF),
            jax.ShapeDtypeStruct((8, D), F32),
            jax.ShapeDtypeStruct((8, 128), F32),
        ),
        in_specs=[pl.BlockSpec(memory_space=pltpu.SMEM), vmem] + [any_] * 5 + [vmem] * 2,
        out_specs=(any_, any_, vmem, vmem, vmem),
        scratch_shapes=[
            pltpu.VMEM((GROUP, D), BF),
            pltpu.VMEM((GROUP, CB), BF),
            pltpu.VMEM((GROUP, CA), BF),
            pltpu.VMEM((2, FEATS, CA), BF),
            pltpu.VMEM((2, FEATS, CB), BF),
            *both(2, 4, 4, ROWS),
            pltpu.VMEM((2, 2, TOK, D), BF),
            *both(2, 2, 2, ROWS),
            *both(2, 2, 4, ROWS),
            *both(2, 2, ROWS // 2),
            *both(2, 2, ROWS),
            *both(2, ROWS, dtype=F32),
            pltpu.VMEM((2, 2, 2, TOK, D), BF),
            pltpu.VMEM((2, 2, 2, TOK, D), BF),
            pltpu.VMEM((2, 2, TOK // 2, D), BF),
            pltpu.VMEM((2, 2, TOK, D), BF),
            pltpu.VMEM((16, 2, D), F32),
            pltpu.VMEM((8, 2, D), F32),
            pltpu.VMEM((16, 8, 128), F32),
            pltpu.VMEM((8, 8, 128), F32),
            pltpu.VMEM((D // 128, TOK, 128), F32),
            pltpu.VMEM((1, TOK, D), BF),
            pltpu.SemaphoreType.DMA((224,)),
            pltpu.SemaphoreType.DMA((224,)),
            pltpu.SemaphoreType.DMA((8,)),
            pltpu.SemaphoreType.DMA((8,)),
        ],
        compiler_params=pltpu.CompilerParams(
            collective_id=1, has_side_effects=True, vmem_limit_bytes=62 * 2**20
        ),
    )(tiles, flips, made, back, toks, wall_a, wall_b, tokens, gains)


def halves(item):
    high = item.astype(BF)
    return high, (item - high.astype(F32)).astype(BF)


def near_product(left, right, dims):
    (a, a_low), (b, b_low) = left, right
    axis = 0 if dims == (((1,), (0,)), ((), ())) else 1
    return lax.dot_general(
        jnp.concatenate([a, a, a_low], 1),
        jnp.concatenate([b, b_low, b], axis),
        dims,
        preferred_element_type=F32,
    )


def update_kernel(tok, squares, norm_raw, norm_params, norm_moment1, norm_moment2, grad_a, grad_b, *refs):
    ins, refs = refs[:20], refs[20:]
    out, input_grad, grad_norm, norm_grads, norm_first, norm_second, norm_new = refs[:7]
    outs, v_ins, v_outs, came, left = refs[7:27], refs[27:47], refs[47:67], refs[67], refs[68]
    weights, firsts, seconds, bases = v_ins[0:5], v_ins[5:10], v_ins[10:15], v_ins[15:20]
    grads, firsts_new, seconds_new, weights_new = v_outs[0:5], v_outs[5:10], v_outs[10:15], v_outs[15:20]
    parts = (grad_a, grad_b)
    order = (1, 2, 3, 4, 0)
    arriving = {}
    for i in order:
        for k in range(4):
            n = 5 * k + i
            arriving[i, k] = pltpu.make_async_copy(ins[n], v_ins[n], came.at[n])
            arriving[i, k].start()
    out[...] = tok[0]
    input_grad[...] = tok[1]
    leaving = []
    left_lanes = lax.broadcasted_iota(jnp.int32, (1, 128), 1) < 64

    def whole(item):
        return jnp.sum(jnp.sum(item, 0, keepdims=True), 1, keepdims=True)

    raw = norm_raw[0:2, :]
    length = jnp.sqrt(whole(squares[...]) + whole(raw * raw))
    clip = jnp.minimum(1.0, CLIP_LIMIT / length)
    grad_norm[...] = length
    norm_grads[...] = clip * raw
    norm_first[...], norm_second[...], norm_new[...] = adam_plain(
        norm_params[...], clip * raw, norm_moment1[...], norm_moment2[...], NORM_RATE
    )

    def fetch(piece, side):
        i, half, column = piece
        tile = parts[i][half, :, pl.ds(column // 128 * 128, 128)]
        return tile if column // 64 % 2 == side else pltpu.roll(tile, 64, 1)

    tables = pieces()
    for i in order:
        table = tables[i]
        for k in range(4):
            arriving[i, k].wait()
        blocks = range(WIDTHS[i] // 128)
        for group in (blocks[at : at + 4] for at in range(0, len(blocks), 4)):
            bases_of = [halves(bases[i][block]) for block in group]
            clipped = []
            for block in group:
                one, two = table[2 * block], table[2 * block + 1]
                if two == one[:2] + (one[2] + 64,) and one[2] % 128 == 0:
                    grad = parts[one[0]][one[1], :, pl.ds(one[2], 128)]
                else:
                    grad = jnp.where(left_lanes, fetch(one, 0), fetch(two, 1))
                clipped.append(clip * grad)
            turned = [
                near_product(halves(grad), basis, (((1,), (0,)), ((), ())))
                for grad, basis in zip(clipped, bases_of)
            ]
            ratios = []
            for block, grad, item in zip(group, clipped, turned):
                cols = pl.ds(block * 128, 128)
                first = BETA_ONE * firsts[i][:, cols] + (1.0 - BETA_ONE) * item
                second = BETA_TWO * seconds[i][:, cols] + (1.0 - BETA_TWO) * item * item
                grads[i][:, cols] = grad
                firsts_new[i][:, cols] = first
                seconds_new[i][:, cols] = second
                ratios.append(
                    first
                    * (1.0 / (1.0 - BETA_ONE**STEP))
                    / (jnp.sqrt(second * (1.0 / (1.0 - BETA_TWO**STEP))) + ADAM_EPS)
                )
            turned_back = [
                near_product(halves(ratio), basis, COLS_DIMS) for ratio, basis in zip(ratios, bases_of)
            ]
            for block, item in zip(group, turned_back):
                cols = pl.ds(block * 128, 128)
                weight = weights[i][:, cols]
                weights_new[i][:, cols] = weight - RATE_LIST[i] * (item + WEIGHT_DECAY * weight)
        for k in range(4):
            n = 5 * k + i
            copy = pltpu.make_async_copy(v_outs[n], outs[n], left.at[n])
            copy.start()
            leaving.append(copy)
    for copy in leaving:
        copy.wait()


def update(tok, squares, norm, grad_a, grad_b, weights, firsts, seconds, bases):
    vmem = pl.BlockSpec(memory_space=pltpu.VMEM)
    any_ = pl.BlockSpec(memory_space=pl.ANY)
    shapes = [jax.ShapeDtypeStruct((ROWS, width), F32) for width in WIDTHS]
    small = [jax.ShapeDtypeStruct((TOK, D), BF)] * 2
    small += [jax.ShapeDtypeStruct((1, 1), F32)] + [jax.ShapeDtypeStruct((2, D), F32)] * 4
    state = (*weights, *firsts, *seconds, *bases)
    return pl.pallas_call(
        update_kernel,
        out_shape=tuple(small + shapes * 4),
        in_specs=[vmem] * 8 + [any_] * 20,
        out_specs=(vmem,) * 7 + (any_,) * 20,
        scratch_shapes=[pltpu.VMEM(item.shape, F32) for item in state]
        + [pltpu.VMEM(item.shape, F32) for item in shapes * 4]
        + [pltpu.SemaphoreType.DMA((20,))] * 2,
        compiler_params=pltpu.CompilerParams(vmem_limit_bytes=56 * 2**20),
    )(tok, squares, *norm, grad_a, grad_b, *state)


def adam_plain(param, grad, first, second, rate):
    first_new = BETA_ONE * first + (1.0 - BETA_ONE) * grad
    second_new = BETA_TWO * second + (1.0 - BETA_TWO) * grad * grad
    ratio = (
        first_new
        / (1.0 - BETA_ONE**STEP)
        / (jnp.sqrt(second_new / (1.0 - BETA_TWO**STEP)) + ADAM_EPS)
    )
    return (first_new, second_new, param - rate * ratio)


def body(
    tokens,
    cotangent,
    doc_lengths,
    row_owner,
    norm_params,
    norm_moment1,
    norm_moment2,
    qkv_weight,
    out_weight,
    gate_weight,
    up_weight,
    down_weight,
    qkv_moment1,
    out_moment1,
    gate_moment1,
    up_moment1,
    down_moment1,
    qkv_moment2,
    out_moment2,
    gate_moment2,
    up_moment2,
    down_moment2,
    qkv_basis,
    out_basis,
    gate_basis,
    up_basis,
    down_basis,
):
    blocks = jnp.arange(32, dtype=jnp.int32)
    inverse = jnp.sum((row_owner[None, :] == blocks[:, None]) * blocks[None, :], 1)
    doc_item = jnp.pad(doc_lengths.astype(F32), ((0, 7), (0, 124)))
    entry = jnp.arange(128, dtype=jnp.int32) % (ROT // 2)
    freq = jnp.broadcast_to(10000.0 ** (-2.0 * entry.astype(F32) / ROT), (8, 128))
    weights = (qkv_weight, out_weight, gate_weight, up_weight, down_weight)
    wall_a, wall_b, toks, made, back, tokens_stored, params_stored = gather_all(
        *places(inverse), tokens, cotangent, jnp.pad(norm_params, ((0, 6), (0, 0))), doc_item, freq, weights
    )
    grad_a, grad_b, tok_out, norm_raw, squares = scatter_all(
        *places(row_owner), made, back, toks, wall_a, wall_b, tokens_stored, params_stored
    )
    firsts = (qkv_moment1, out_moment1, gate_moment1, up_moment1, down_moment1)
    seconds = (qkv_moment2, out_moment2, gate_moment2, up_moment2, down_moment2)
    bases = (qkv_basis, out_basis, gate_basis, up_basis, down_basis)
    norm = (norm_raw, norm_params, norm_moment1, norm_moment2)
    out, input_grad, grad_norm, *rest = update(
        tok_out, squares, norm, grad_a, grad_b, weights, firsts, seconds, bases
    )
    return (out, input_grad, grad_norm[0, 0], *rest)


def solution(mesh):
    tok, weight, whole = P(("dp", "mp"), None), P("dp", "mp"), P()
    in_specs = (tok, tok, P("dp", None)) + (whole,) * 4 + (weight,) * 15 + (P("mp", None, None),) * 5
    out_specs = (tok, tok) + (whole,) * 5 + (weight,) * 20
    return jax.shard_map(body, mesh=mesh, in_specs=in_specs, out_specs=out_specs, check_vma=False)
```

```python
import jax
import jax.numpy as jnp
from jax import lax
from jax.experimental import pallas as pl
from jax.experimental.pallas import tpu as pltpu
from jax.sharding import PartitionSpec as P

MESH = pl.DeviceIdType.MESH
BF = jnp.bfloat16
F32 = jnp.float32

HEAD_DIM = 64
ROT = 16
STEP = 5

NORM_EPSILON = 1e-05
BETA_ONE = 0.5
BETA_TWO = 0.5
ADAM_EPS = 1e-08
WEIGHT_DECAY = 0.01
RATE_LIST = (0.02, 0.1, 0.02, 0.02, 0.015)
NORM_RATE = 0.2
CLIP_LIMIT = 1.0
MASK_FILL = -1e30
ROWS_DIMS = (((0,), (0,)), ((), ()))
COLS_DIMS = (((1,), (1,)), ((), ()))

D = 2048
LEN = 512
ROWS = 64
TOK = 128
GROUP = 1024
HEADS = 4
CA = 2176
CB = 1024
CHUNKS = ((1, 0, 512), (1, 512, 512), (0, 0, 512), (0, 512, 512), (0, 1024, 512), (0, 1536, 640))


def place():
    dp = lax.axis_index("dp")
    mp = lax.axis_index("mp")
    return (mp // 2) * 2 + dp // 16, dp % 4, (dp // 4) % 4, mp % 2


def device(x, y, z, c):
    return ((x % 2) * 16 + z * 4 + y, (x // 2) * 2 + c)


def near(me, name):
    x, y, z, c = me
    return {
        "y+": lambda: device(x, (y + 1) % 4, z, c),
        "y-": lambda: device(x, (y + 3) % 4, z, c),
        "z+": lambda: device(x, y, (z + 1) % 4, c),
        "z-": lambda: device(x, y, (z + 3) % 4, c),
        "x+": lambda: device((x + 1) % 4, y, z, c),
        "x-": lambda: device((x + 3) % 4, y, z, c),
        "c": lambda: device(x, y, z, 1 - c),
        "p": lambda: device((x // 2) * 2 + 1 - x % 2, y, z, c),
    }[name]()


NEIGHBOURS = ("y+", "y-", "z+", "z-", "x+", "x-", "c")


class Wires:
    def __init__(self, me, send, recv):
        self.me, self.send, self.recv = me, send, recv
        self.count = 0
        self.open = []

    def push(self, src, dst, to, at=None):
        if at is None:
            at = self.count
            self.count += 1
        if isinstance(to, str):
            to = near(self.me, to)
        copy = pltpu.make_async_remote_copy(
            src, dst, self.send.at[at], self.recv.at[at], device_id=to, device_id_type=MESH
        )
        copy.start()
        self.open.append(copy)
        return copy

    def take(self, number):
        at = self.count
        self.count += number
        return at

    def close(self):
        for copy in self.open:
            copy.wait_send()


WIDTHS = (1536, 512, 1408, 1408, 1408)


def pieces():
    table = [[], [], [], [], []]
    for half in range(2):
        for head in range(HEADS):
            for kind in range(3):
                table[0].append((0, half, head // 2 * 384 + kind * 128 + head % 2 * 64))
        for head in range(HEADS):
            table[1].append((1, half, head * 64))
    gate = [768 + 64 * k for k in range(6)] + [1536 + 64 * k for k in range(4)]
    up = [1152 + 64 * k for k in range(6)] + [1792 + 64 * k for k in range(4)]
    down = [256 + 64 * k for k in range(10)]
    for n, (i, starts, rest) in enumerate(((0, gate, 2048), (0, up, 2112), (1, down, 896))):
        table[2 + n] += [(i, 0, start) for start in starts]
        table[2 + n] += [(i, 0, rest), (i, 1, rest)]
        table[2 + n] += [(i, 1, start) for start in starts]
    return table


def reorder(staged, which, tiles, flips, store, rows=TOK):
    left = lax.broadcasted_iota(jnp.int32, (1, 128), 1) < 64
    for k in range(D // 128):
        sides = []
        for side in range(2):
            n = 2 * k + side
            tile = staged[tiles[which, n]][:rows]
            flip = jnp.broadcast_to(flips[which : which + 1, n : n + 1], (1, 128))
            sides.append(jnp.where(flip > 0.0, pltpu.roll(tile, 64, 1), tile))
        store(pl.ds(k * 128, 128), jnp.where(left, sides[0], sides[1]))


def stage_tiles(staged, value, rows):
    for k in range(D // 128):
        staged[k, rows, :] = value[:, k * 128 : k * 128 + 128].astype(F32)


def places(orders):
    spots = jnp.arange(32, dtype=jnp.int32)
    return orders // 2, ((orders + spots) % 2).astype(F32)


LOADS = ((0, 0, 768), (1, 0, 256), (1, 256, 768), (0, 768, 768), (0, 1536, 640))


GATHER_ORDER = (
    ("AG", 1), ("OWN", 1), ("AG", 0), ("OWN", 0), ("TS", 1), ("SW", 1), ("H3", 1, 0, 0), ("H1", 1, 0),
    ("AG", 2), ("SW", 0), ("H3", 0, 0, 0), ("AG", 4), ("AG", 3), ("OWN", 3), ("H3", 1, 1, 0), ("TS", 0),
    ("H3", 1, 0, 1), ("H3", 1, 0, 2), ("H1", 1, 1), ("H1", 0, 0), ("H1", 0, 1), ("OWN", 2), ("H2", 1, 0),
    ("H3", 0, 1, 0), ("TB",), ("H3", 1, 1, 1), ("H2", 1, 1), ("H3", 1, 1, 2), ("H2", 0, 0), ("OWN", 4),
    ("TF", 1), ("H3", 0, 0, 1), ("H3", 0, 1, 1), ("SW", 3), ("H1", 3, 0), ("H3", 3, 0, 0), ("H3", 0, 0, 2),
    ("H2", 0, 1), ("H3", 0, 1, 2), ("H3", 1, 0, 3), ("H3", 1, 1, 3), ("H3", 0, 0, 3), ("SW", 2), ("H2", 3, 0),
    ("H3", 2, 0, 0), ("TF", 0), ("H3", 0, 1, 3), ("H3", 3, 1, 0), ("H3", 3, 0, 1), ("H1", 2, 0), ("H1", 3, 1),
    ("H3", 2, 1, 0), ("ARR", 1), ("PR", 1, 0), ("ARR", 0), ("PR", 0, 0), ("H1", 2, 1), ("AT", 1, 0),
    ("H3", 3, 0, 3), ("H2", 2, 0), ("H3", 3, 1, 2), ("TL", 1), ("AT", 0, 0), ("TL", 0), ("H3", 2, 1, 1),
    ("H3", 2, 0, 2), ("PR", 1, 1), ("H3", 2, 1, 2), ("H2", 3, 1), ("H3", 2, 0, 1), ("H3", 3, 0, 2),
    ("H3", 3, 1, 1), ("SW", 4), ("H1", 4, 0), ("H3", 4, 0, 0), ("H2", 2, 1), ("PR", 0, 1), ("H3", 2, 0, 3),
    ("AT", 0, 1), ("H2", 4, 0), ("H3", 3, 1, 3), ("H3", 4, 1, 0), ("H1", 4, 1), ("AT", 1, 1), ("H3", 4, 0, 2),
    ("H3", 2, 1, 3), ("ARR", 3), ("PR", 3, 1), ("H3", 4, 1, 1), ("PR", 3, 0), ("H2", 4, 1), ("H3", 4, 0, 1),
    ("H3", 4, 1, 2), ("H3", 4, 0, 3), ("ARR", 2), ("PR", 2, 1), ("U", 0, 1), ("H3", 4, 1, 3), ("PR", 2, 0),
    ("ARR", 4), ("PR", 4, 1), ("U", 1, 1), ("PR", 4, 0), ("U", 1, 0), ("U", 0, 0),
)


def swapped(field, lane):
    return jnp.where(lane % ROT < ROT // 2, pltpu.roll(field, 120, 1), pltpu.roll(field, ROT // 2, 1))


def gather_kernel(
    tiles, flips, tokens, cotangent, params, lengths, qkv_w, out_w, gate_w, up_w, down_w,
    wall_a, wall_b, toks, made, back, tokens_out, params_out,
    own_a, own_b, v_wall_a, v_wall_b, v_toks, v_made, v_back, pre_a, pre_b, docs, cosine, sine, bias, inputs, staged,
    send, recv, keep,
):
    me = x, y, z, c = place()
    xlo, xhi = x % 2, x // 2
    wires = Wires(me, send, recv)
    owns, walls, v_walls = (own_a, own_b), (wall_a, wall_b), (v_wall_a, v_wall_b)
    late = []
    lane = lax.broadcasted_iota(jnp.int32, (1, 128), 1)
    mine = [lane < HEAD_DIM, lane >= HEAD_DIM]

    def local(src, dst):
        copy = pltpu.make_async_copy(src, dst, keep.at[len(late)])
        copy.start()
        late.append(copy)

    barrier = pltpu.get_barrier_semaphore()
    for name in NEIGHBOURS:
        pl.semaphore_signal(barrier, inc=1, device_id=near(me, name), device_id_type=MESH)

    sources = {}
    for weight, table in zip((qkv_w, out_w, gate_w, up_w, down_w), pieces()):
        for n, spot in enumerate(table):
            sources[spot] = (weight, n)
    def arrange(chunk):
        i, c0, cn = chunk
        for half in range(2):
            for column in range(c0, c0 + cn, 128):
                sides = []
                for side in range(2):
                    spot = (i, half, column + 64 * side)
                    if spot not in sources:
                        sides.append(jnp.zeros((ROWS, 128), F32))
                        continue
                    weight, n = sources[spot]
                    tile = weight[:, pl.ds(n // 2 * 128, 128)]
                    sides.append(tile if n % 2 == side else pltpu.roll(tile, 64, 1))
                owns[i][half, :, pl.ds(column, 128)] = jnp.where(mine[0], sides[0], sides[1]).astype(BF)


    own_first = wires.take(8 * len(LOADS))
    swaps, forwards, seconds, lasts = {}, {}, {}, {}
    lo, hi = slice(0, ROWS // 2), slice(ROWS // 2, ROWS)

    def half_of(part):
        return (xlo + part) % 2

    def way(part, d):
        half = half_of(part)
        along_y = 1 - half if d < 2 else half
        move = 1 if d % 2 == 0 else 3
        return device(x, (y + along_y * move) % 4, (z + (1 - along_y) * move) % 4, c)

    def spots(part):
        half = half_of(part)
        return y + half * (z - y), z + half * (y - z)

    def block(n, part, a, b, some=slice(0, ROWS)):
        i, c0, cn = LOADS[n]
        half = half_of(part)
        at = half * 16 + (b + half * (a - b)) * 4 + a + half * (b - a)
        at = pl.ds(pl.multiple_of(at * ROWS + some.start, 32), some.stop - some.start)
        return v_walls[i].at[at, pl.ds(c0, cn)]

    def own_at(n, part, d):
        return own_first + n * 8 + part * 4 + d

    def own_block(n, part):
        a, b = spots(part)
        return block(n, part, a, b)

    def send_own(n):
        i, c0, cn = LOADS[n]
        cols = pl.ds(c0, cn)
        own = owns[i].at[xlo, :, cols]
        for d in range(4):
            wires.push(own, own_block(n, 0), way(0, d), own_at(n, 0, d))
        swaps[n] = wires.push(owns[i].at[1 - xlo, :, cols], own_block(n, 0), "p")
        v_walls[i][pl.ds(pl.multiple_of((xlo * 16 + z * 4 + y) * ROWS, ROWS), ROWS), cols] = owns[i][xlo, :, cols]

    def send_swapped(n):
        swaps[n].wait_recv()
        for d in range(4):
            wires.push(own_block(n, 1), own_block(n, 1), way(1, d), own_at(n, 1, d))

    def wait_own(n, part, d):
        at = own_at(n, part, d)
        pltpu.make_async_remote_copy(
            own_block(n, part), own_block(n, part), send.at[at], recv.at[at],
            device_id=way(part, d), device_id_type=MESH,
        ).wait_recv()

    def hop1(n, part):
        a, b = spots(part)
        wait_own(n, part, 0)
        some = block(n, part, (a + 3) % 4, b, lo)
        forwards[n, part, 0] = wires.push(some, some, way(part, 0))
        wait_own(n, part, 1)
        some = block(n, part, (a + 1) % 4, b, hi)
        forwards[n, part, 1] = wires.push(some, some, way(part, 1))
        for j, spot in ((1, (a + 3) % 4), (2, (a + 1) % 4)):
            item = block(n, part, spot, b)
            seconds[n, part, j, 0] = wires.push(item, item, way(part, 2))
            seconds[n, part, j, 1] = wires.push(item, item, way(part, 3))

    def hop2(n, part):
        a, b = spots(part)
        forwards[n, part, 0].wait_recv()
        forwards[n, part, 1].wait_recv()
        item = block(n, part, (a + 2) % 4, b)
        seconds[n, part, 3, 0] = wires.push(item, item, way(part, 2))
        seconds[n, part, 3, 1] = wires.push(item, item, way(part, 3))

    def hop3(n, part, j):
        a, b = spots(part)
        spot = (a + (0, 3, 1, 2)[j]) % 4
        for d in range(2):
            if j == 0:
                wait_own(n, part, 2 + d)
            else:
                seconds[n, part, j, d].wait_recv()
            some = block(n, part, spot, (b + 3) % 4 if d == 0 else (b + 1) % 4, lo if d == 0 else hi)
            lasts[n, part, j, d] = wires.push(some, some, way(part, 2 + d))

    def arrived(n):
        for j in range(4):
            for part in range(2):
                for d in range(2):
                    lasts[n, part, j, d].wait_recv()
        i, c0, cn = LOADS[n]
        local(v_walls[i].at[:, pl.ds(c0, cn)], walls[i].at[:, pl.ds(c0, cn)])


    tok_x, tok_f, tok_c = {}, {}, [[], []]
    whole = set()

    def tok_at(sx, cc, start=0, size=TOK):
        return pl.ds(pl.multiple_of(((sx % 2) * 4 + (sx // 2) * 2 + cc) * TOK + start, 64), size)

    def tokens_start(k):
        def keep_tokens(cols, value):
            inputs[:, cols] = value
            tokens_out[:, cols] = value.astype(BF)

        def keep_cotangent(cols, value):
            v_toks[1, tok_at(x, c), cols] = value.astype(BF)

        def keep_params(cols, value):
            params_out[:, cols] = value

        def step(g, carry):
            at = pl.ds(pl.multiple_of(g * 16, 16), 16)
            item = inputs[at, :]
            centered = item - jnp.mean(item, -1, keepdims=True)
            variance = jnp.mean(centered * centered, -1, keepdims=True)
            standard = centered * lax.rsqrt(variance + NORM_EPSILON)
            normed = standard * params_out[0:1, :] + params_out[1:2, :]
            v_toks[0, pl.ds(pl.multiple_of((xlo * 4 + xhi * 2 + c) * TOK + g * 16, 16), 16), :] = normed.astype(BF)
            return carry

        every = pl.ds(0, TOK)
        if k == 0:
            stage_tiles(staged, jnp.zeros((8, D), F32), pl.ds(0, 8))
            stage_tiles(staged, params, pl.ds(0, 2))
            reorder(staged, 0, tiles, flips, keep_params, 8)
            stage_tiles(staged, tokens, every)
            reorder(staged, 0, tiles, flips, keep_tokens)
            lax.fori_loop(0, TOK // 16, step, 0)
        else:
            stage_tiles(staged, cotangent, every)
            reorder(staged, 0, tiles, flips, keep_cotangent)
        item = v_toks.at[k, tok_at(x, c)]
        for name in ("x+", "x-"):
            tok_x[k, name] = wires.push(item, item, name)
        tok_c[k].append(wires.push(item, item, "c"))

    def tokens_forward(k):
        for n, name in enumerate(("x+", "x-")):
            tok_x[k, name].wait_recv()
            sx = (x + 3) % 4 if n == 0 else (x + 1) % 4
            item = v_toks.at[k, tok_at(sx, c)]
            part = v_toks.at[k, tok_at(sx, c, n * (TOK // 2), TOK // 2)]
            tok_f[k, n] = wires.push(part, part, name)
            tok_c[k].append(wires.push(item, item, "c"))

    def tokens_last(k):
        tok_f[k, 0].wait_recv()
        tok_f[k, 1].wait_recv()
        item = v_toks.at[k, tok_at((x + 2) % 4, c)]
        tok_c[k].append(wires.push(item, item, "c"))

    def tokens_whole(k, part):
        if (k, part) in whole:
            return
        whole.add((k, part))
        for n in ((1, 2), (0, 3))[part]:
            tok_c[k][n].wait_recv()
        if len(whole & {(k, 0), (k, 1)}) == 2:
            local(v_toks.at[k], toks.at[k])

    def first_row(part):
        return (xlo + 1 + part) % 2 * LEN


    def product(n, part):
        i, c0, cn = LOADS[n]
        tokens_whole(i, part)
        start = first_row(part)
        pre = (pre_a, pre_b)[i]

        at = pl.ds(pl.multiple_of(start, LEN), LEN)
        pre[at, pl.ds(c0, cn)] = jnp.dot(
            v_toks[i, at, :], v_walls[i][:, pl.ds(c0, cn)], preferred_element_type=F32
        )

    def flush(src, dst, at, cols):
        local(src.at[at, cols], dst.at[at, cols])

    def doc_start(s, index, shape):
        start = jnp.zeros(shape, F32)
        end = jnp.zeros((1, 1), F32)
        for j in range(3):
            end = end + docs[s, 0:1, j : j + 1]
            start = jnp.where(index >= end, end, start)
        return start

    def tables():
        doc_swap[0].wait_recv()
        for s in range(2):
            mask(s)
            index = lax.broadcasted_iota(jnp.int32, (LEN, 128), 0).astype(F32)
            entry = lane % HEAD_DIM
            freq = jnp.zeros((1, 128), F32)
            for e in range(ROT // 2):
                freq = jnp.where(entry % (ROT // 2) == e, 10000.0 ** (-2.0 * e / ROT), freq)
            angle = (index - doc_start(s, index, (LEN, 128))) * freq
            turn = jnp.sin(angle)
            cosine[pl.ds(s * LEN, LEN), :] = jnp.where(entry < ROT, jnp.cos(angle), 1.0)
            sine[pl.ds(s * LEN, LEN), :] = jnp.where(
                entry < ROT // 2, -turn, jnp.where(entry < ROT, turn, 0.0)
            )

    def mask(s):
        query_at = lax.broadcasted_iota(jnp.int32, (1, LEN), 1).astype(F32)
        key_at = lax.broadcasted_iota(jnp.int32, (LEN, 1), 0).astype(F32)
        start = doc_start(s, query_at, (1, LEN))
        bias[s] = jnp.where((key_at >= start) & (key_at <= query_at), 0.0, MASK_FILL)

    def attend(pair, part):
        s, start = (xlo + 1 + part) % 2, first_row(part)
        at_rows = pl.ds(pl.multiple_of(start, LEN), LEN)
        cos_rows = cosine[at_rows, :]
        sin_rows = sine[at_rows, :]

        def turned(at):
            field = pre_a[at_rows, pl.ds(at, 128)]
            return field * cos_rows + swapped(field, lane) * sin_rows

        at, first = pair * 128, pair * 384
        query = (turned(first) * (HEAD_DIM**-0.5)).astype(BF)
        key = turned(first + 128).astype(BF)
        value = pre_a[at_rows, pl.ds(first + 256, 128)].astype(BF)
        d_attn = pre_b[at_rows, pl.ds(at, 128)].astype(BF)
        key_t = key.T
        value_t = value.T
        d_key = [None, None]
        d_value = [None, None]
        zero = jnp.zeros((), BF)
        head_row = lax.broadcasted_iota(jnp.int32, (128, 1), 0) < HEAD_DIM
        for block in range(2):
            queries = slice(block * 256, block * 256 + 256)
            keys = (block + 1) * 256
            attn_t = []
            d_query_t = []
            for h in range(2):
                query_h = jnp.where(mine[h], query[queries], zero)
                d_attn_h = jnp.where(mine[h], d_attn[queries], zero)
                scores = lax.dot_general(key[:keys], query_h, COLS_DIMS, preferred_element_type=F32)
                scores = scores + bias[s, 0:keys, queries]
                peak = jnp.max(scores, 0, keepdims=True)
                expo = jnp.exp(scores - peak)
                probs = expo * (1.0 / jnp.sum(expo, 0, keepdims=True))
                probs_low = probs.astype(BF)
                d_prob = lax.dot_general(value[:keys], d_attn_h, COLS_DIMS, preferred_element_type=F32)
                delta = jnp.sum(probs * d_prob, 0, keepdims=True)
                d_score = (probs * (d_prob - delta)).astype(BF)
                attn_t.append(jnp.dot(value_t[:, :keys], probs_low, preferred_element_type=F32))
                d_query_t.append(jnp.dot(key_t[:, :keys], d_score, preferred_element_type=F32))
                d_value_h = jnp.dot(probs_low, d_attn_h, preferred_element_type=F32)
                d_key_h = jnp.dot(d_score, query_h, preferred_element_type=F32)
                for p in range(block + 1):
                    part = slice(p * 256, p * 256 + 256)
                    d_value[p] = d_value_h[part] if d_value[p] is None else d_value[p] + d_value_h[part]
                    d_key[p] = d_key_h[part] if d_key[p] is None else d_key[p] + d_key_h[part]
            out_rows = pl.ds(pl.multiple_of(start + block * 256, 256), 256)
            v_made[out_rows, pl.ds(at, 128)] = jnp.where(head_row, attn_t[0], attn_t[1]).T.astype(BF)
            d_query = jnp.where(head_row, d_query_t[0], d_query_t[1]).T * (HEAD_DIM**-0.5)
            d_query = d_query * cosine[out_rows, :] - swapped(d_query, lane) * sine[out_rows, :]
            v_back[out_rows, pl.ds(first, 128)] = d_query.astype(BF)
        d_key = jnp.concatenate(d_key, 0)
        d_key = d_key * cos_rows - swapped(d_key, lane) * sin_rows
        v_back[at_rows, pl.ds(first + 128, 128)] = d_key.astype(BF)
        v_back[at_rows, pl.ds(first + 256, 128)] = jnp.concatenate(d_value, 0).astype(BF)
        flush(v_made, made, at_rows, pl.ds(at, 128))
        flush(v_back, back, at_rows, pl.ds(first, 384))

    def unit(gate, up, d_hidden):
        sigma = jax.nn.sigmoid(gate)
        silu = gate * sigma
        return silu * up, d_hidden * up * sigma * (1.0 + gate * (1.0 - sigma)), d_hidden * silu

    def units(gate_at, width, down_at, rest, part):
        start = first_row(part)

        def step(g, carry):
            at = pl.ds(pl.multiple_of(start + g * 32, 32), 32)
            gates, ups, downs = pl.ds(gate_at, width), pl.ds(gate_at + width, width), pl.ds(down_at, width)
            hidden, d_gate, d_up = unit(pre_a[at, gates], pre_a[at, ups], pre_b[at, downs])
            v_made[at, downs] = hidden.astype(BF)
            v_back[at, gates] = d_gate.astype(BF)
            v_back[at, ups] = d_up.astype(BF)
            if rest:
                both = pre_a[at, pl.ds(2048, 128)]
                hidden, d_gate, d_up = unit(both, pltpu.roll(both, 64, 1), pre_b[at, pl.ds(896, 128)])
                v_made[at, pl.ds(896, 128)] = jnp.where(mine[0], hidden, 0.0).astype(BF)
                v_back[at, pl.ds(2048, 128)] = jnp.where(mine[0], d_gate, pltpu.roll(d_up, 64, 1)).astype(BF)
            return carry

        lax.fori_loop(0, LEN // 32, step, 0)
        every = pl.ds(pl.multiple_of(start, LEN), LEN)
        flush(v_made, made, every, pl.ds(down_at, width + (128 if rest else 0)))
        flush(v_back, back, every, pl.ds(gate_at, 2 * width + (128 if rest else 0)))


    doc_swap = [wires.take(1)]
    steps = {
        "AG": lambda n: arrange(LOADS[n]),
        "OWN": send_own,
        "SW": send_swapped,
        "H1": hop1,
        "H2": hop2,
        "H3": hop3,
        "ARR": arrived,
        "TS": tokens_start,
        "TF": tokens_forward,
        "TL": tokens_last,
        "PR": product,
        "TB": tables,
        "AT": attend,
        "U": lambda k, part: units(1536, 256, 640, True, part) if k else units(768, 384, 256, False, part),
    }
    met = False
    for name, *at in GATHER_ORDER:
        if name in ("OWN", "TS") and not met:
            met = True
            pl.semaphore_wait(barrier, len(NEIGHBOURS))
            item = jnp.zeros((8, 128), F32)
            for j in range(4):
                item = jnp.where(lane == j, lengths[0:1, j : j + 1].astype(F32), item)
            docs[xlo] = item
            doc_swap[0] = wires.push(docs.at[xlo], docs.at[xlo], "p", doc_swap[0])
        steps[name](*at)
    wires.close()
    for copy in late:
        copy.wait()


def gather_all(tiles, flips, tokens, cotangent, params, lengths, weights):
    any_ = pl.BlockSpec(memory_space=pl.ANY)
    vmem = pl.BlockSpec(memory_space=pltpu.VMEM)
    return pl.pallas_call(
        gather_kernel,
        out_shape=(
            jax.ShapeDtypeStruct((D, CA), BF),
            jax.ShapeDtypeStruct((D, CB), BF),
            jax.ShapeDtypeStruct((2, GROUP, D), BF),
            jax.ShapeDtypeStruct((GROUP, CB), BF),
            jax.ShapeDtypeStruct((GROUP, CA), BF),
            jax.ShapeDtypeStruct((TOK, D), BF),
            jax.ShapeDtypeStruct((8, D), F32),
        ),
        in_specs=[pl.BlockSpec(memory_space=pltpu.SMEM)] + [vmem] * 10,
        out_specs=(any_,) * 5 + (vmem,) * 2,
        scratch_shapes=[
            pltpu.VMEM((2, ROWS, CA), BF),
            pltpu.VMEM((2, ROWS, CB), BF),
            pltpu.VMEM((D, CA), BF),
            pltpu.VMEM((D, CB), BF),
            pltpu.VMEM((2, GROUP, D), BF),
            pltpu.VMEM((GROUP, CB), BF),
            pltpu.VMEM((GROUP, CA), BF),
            pltpu.VMEM((GROUP, CA), F32),
            pltpu.VMEM((GROUP, CB), F32),
            pltpu.VMEM((2, 8, 128), F32),
            pltpu.VMEM((GROUP, 128), F32),
            pltpu.VMEM((GROUP, 128), F32),
            pltpu.VMEM((2, LEN, LEN), F32),
            pltpu.VMEM((TOK, D), F32),
            pltpu.VMEM((D // 128, TOK, 128), F32),
            pltpu.SemaphoreType.DMA((266,)),
            pltpu.SemaphoreType.DMA((266,)),
            pltpu.SemaphoreType.DMA((32,)),
        ],
        compiler_params=pltpu.CompilerParams(
            collective_id=0, has_side_effects=True, vmem_limit_bytes=62 * 2**20
        ),
    )(tiles, flips, tokens, cotangent, params, lengths, *weights)


SCATTER_ORDER = (
    ("P", 1), ("A", 1), ("B", 1), ("P", 0), ("R",), ("A", 0), ("B", 0), ("BR", 0, 0), ("S1", 1), ("BR", 0, 1),
    ("BR", 0, 2), ("BR", 0, 3), ("P", 2), ("A", 2), ("B", 2), ("S1", 0), ("X", 0), ("P", 3), ("A", 3),
    ("B", 3), ("BR", 1, 0), ("BR", 1, 1), ("T1", 0), ("S1", 2), ("BR", 1, 2), ("BR", 1, 3), ("X", 1),
    ("S1", 3), ("S2", 0), ("T2", 0), ("S2", 2), ("P", 4), ("S3", 0), ("B", 4), ("S2", 3), ("A", 4), ("T1", 1),
    ("P", 5), ("B", 5), ("A", 5), ("S3", 2), ("T3", 0), ("S1", 4), ("T2", 1), ("S3", 3), ("S2", 1), ("L", 0),
    ("S1", 5), ("L", 2), ("S2", 4), ("L", 3), ("S3", 1), ("T3", 1), ("N1",), ("S2", 5), ("S3", 4), ("L", 1),
    ("N2",), ("S3", 5), ("L", 4), ("N3",), ("L", 5),
)


def add_rows(dst, src, rows, cols):
    def step(g, carry):
        at = pl.ds(pl.multiple_of(g * 16, 16), 16)
        dst[at, cols] = (dst[at, cols].astype(F32) + src[at, cols].astype(F32)).astype(dst.dtype)
        return carry

    lax.fori_loop(0, rows // 16, step, 0)


def peers(me):
    x, y, z, c = me
    here, there = z * 4 + y, x * 2 + c
    plane, line = [], []
    for k in range(1, 16):
        at = (here + k) % 16
        plane.append(device(x, at % 4, at // 4, c))
    for k in range(1, 8):
        at = (there + k) % 8
        line.append(device(at // 2, y, z, at % 2))
    return here, there, plane, line


FEATS = 256


def scatter_kernel(
    tiles, flips, made, back, toks, wall_a, wall_b, tokens, gains,
    grad_a, grad_b, tok_out, norm_out, square_out,
    v_act, v_made, v_back, v_wall_a, v_wall_b, part_a, part_b, stage,
    r1_a, r1_b, r2_a, r2_b, t1_a, t1_b, t2_a, t2_b, sum_a, sum_b,
    own, core, x1, x2, norm1, norm2, square1, square2, shown, cotangent,
    send, recv, keep, load,
):
    me = x, y, z, c = place()
    xlo = x % 2
    wires = Wires(me, send, recv)
    parts, grads = (part_a, part_b), (grad_a, grad_b)
    r1, r2 = (r1_a, r1_b), (r2_a, r2_b)
    t1, t2, sums = (t1_a, t1_b), (t2_a, t2_b), (sum_a, sum_b)
    late = []
    here, there, plane, line = peers(me)

    def fetch(src, dst, sem):
        for side in range(2):
            for g in range(4):
                at = g * 256 + (c if side == 0 else 1 - c) * TOK
                pltpu.make_async_copy(
                    src.at[pl.ds(at, TOK)], dst.at[pl.ds(side * 512 + g * TOK, TOK)], load.at[sem]
                ).start()

    def fetched(dst, sem):
        pltpu.make_async_copy(dst, dst, load.at[sem]).wait()

    def wall_copy(i, f):
        wall, buf = ((wall_a, v_wall_a), (wall_b, v_wall_b))[i]
        return pltpu.make_async_copy(
            wall.at[pl.ds(f * FEATS, FEATS)], buf.at[f % 2], load.at[4 + 2 * i + f % 2]
        )

    own_rows = pl.ds(pl.multiple_of((xlo * 4 + x // 2 * 2 + c) * TOK, TOK), TOK)
    pltpu.make_async_copy(toks.at[pl.ds(1, 1), own_rows], cotangent, load.at[3]).start()
    fetch(toks.at[1], v_act, 0)
    fetch(made, v_made, 1)
    fetch(back, v_back, 2)
    for i in (1, 0):
        for f in range(2):
            wall_copy(i, f).start()

    barrier = pltpu.get_barrier_semaphore()
    for to in plane + line:
        pl.semaphore_signal(barrier, inc=1, device_id=to, device_id_type=MESH)
    pl.semaphore_wait(barrier, 22)
    axes = (("z+", "z-", "y+", "y-"), ("y+", "y-", "z+", "z-"))

    def spots(half):
        return (z, y) if half == 0 else (y, z)

    def piece(half, chunk, spot, start, size):
        i, c0, cn = chunk
        cols = pl.ds(c0, cn)
        if half == 0:
            return parts[i].at[0, spot, pl.ds(start, size), :, cols]
        return parts[i].at[1, pl.ds(start, size), spot, :, cols]

    state = {}

    def product(n):
        i, c0, cn = CHUNKS[n]
        right = (v_back, v_made)[i]

        def step(f, carry):
            feats = pl.ds(pl.multiple_of(f * 512, 512), 512)
            got = lax.dot_general(
                v_act[:, feats], right[:, pl.ds(c0, cn)], ROWS_DIMS, preferred_element_type=F32
            )
            at = pl.ds(f % 2 * 2, 2)
            parts[i][f // 2, at, :, :, pl.ds(c0, cn)] = got.astype(BF).reshape(2, 4, ROWS, cn)
            return carry

        lax.fori_loop(0, D // 512, step, 0)

    def branch(k, blocks):
        i = 1 - k
        left, buf = (v_back, v_made)[i], (v_wall_a, v_wall_b)[i]
        for f in blocks:
            wall_copy(i, f).wait()
            feats = pl.ds(f * FEATS, FEATS)
            for side in range(2):
                got = lax.dot_general(
                    left[pl.ds(side * 512, 512), :], buf[f % 2], COLS_DIMS, preferred_element_type=F32
                )
                got = got.astype(BF).reshape(2, 2, TOK, FEATS)
                if side == 0:
                    own[k, :, :, :, feats] = got
                else:
                    stage[:, :, :, feats] = got
            if f + 2 < D // FEATS:
                wall_copy(i, f + 2).start()

    def cross(k):
        state["c", k] = wires.push(stage, core.at[k], "c")

    def stage0(n, half):
        chunk = i, c0, cn = CHUNKS[n]
        p, q = spots(half)
        up, down = axes[half][:2]
        cols = pl.ds(c0, cn)
        state["a", n, half, 0] = wires.push(
            piece(half, chunk, (p + 2) % 4, 0, 2), r1[i].at[half, 0, :, :, cols], up
        )
        state["a", n, half, 1] = wires.push(
            piece(half, chunk, (p + 2) % 4, 2, 2), r1[i].at[half, 1, :, :, cols], down
        )

    def stage0b(n, half):
        chunk = i, c0, cn = CHUNKS[n]
        p, q = spots(half)
        up, down = axes[half][:2]
        cols = pl.ds(c0, cn)
        state["b", n, half, 0] = wires.push(
            piece(half, chunk, (p + 1) % 4, 2, 2), r2[i].at[half, 0, pl.ds(2, 2), :, cols], up
        )
        state["b", n, half, 1] = wires.push(
            piece(half, chunk, (p + 3) % 4, 0, 2), r2[i].at[half, 1, pl.ds(0, 2), :, cols], down
        )

    def stage1(n, half):
        chunk = i, c0, cn = CHUNKS[n]
        cols = pl.ds(c0, cn)
        p, q = spots(half)
        for d in range(2):
            state["a", n, half, d].wait_recv()
            spot = (p + 1) % 4 if d == 0 else (p + 3) % 4
            for m in range(2):
                block = 2 * d + m
                mine = parts[i].at[0, spot, block] if half == 0 else parts[i].at[1, block, spot]
                add_rows(mine, r1[i].at[half, d, m], ROWS, cols)
            state["s", n, half, d] = wires.push(
                piece(half, chunk, spot, 2 * d, 2), r2[i].at[half, d, pl.ds(2 * d, 2), :, cols], axes[half][d]
            )

    def kept(i, half, p, q):
        return parts[i].at[0, p, q] if half == 0 else parts[i].at[1, q, p]

    def stage2(n, half):
        i, c0, cn = CHUNKS[n]
        cols = pl.ds(c0, cn)
        p, q = spots(half)
        up, down = axes[half][2:]
        for d in range(2):
            state["b", n, half, d].wait_recv()
            state["s", n, half, d].wait_recv()

        def step(g, carry):
            at = pl.ds(pl.multiple_of((g % 4) * 16, 16), 16)
            m = g // 4
            mine = kept(i, half, p, m)
            total = (
                mine[at, cols].astype(F32)
                + r2[i][half, 0, m, at, cols].astype(F32)
                + r2[i][half, 1, m, at, cols].astype(F32)
            )
            mine[at, cols] = total.astype(BF)
            return carry

        lax.fori_loop(0, 16, step, 0)
        lo, hi = pl.ds(0, ROWS // 2), pl.ds(ROWS // 2, ROWS // 2)
        far = kept(i, half, p, (q + 2) % 4)
        state["t", n, half, 0] = wires.push(far.at[lo, cols], t1[i].at[half, 0, :, cols], up)
        state["t", n, half, 1] = wires.push(far.at[hi, cols], t1[i].at[half, 1, :, cols], down)
        state["u", n, half, 0] = wires.push(
            kept(i, half, p, (q + 1) % 4).at[hi, cols], t2[i].at[half, 0, hi, cols], up
        )
        state["u", n, half, 1] = wires.push(
            kept(i, half, p, (q + 3) % 4).at[lo, cols], t2[i].at[half, 1, lo, cols], down
        )

    def stage3(n, half):
        i, c0, cn = CHUNKS[n]
        cols = pl.ds(c0, cn)
        p, q = spots(half)
        for d in range(2):
            state["t", n, half, d].wait_recv()
            rows = pl.ds(d * (ROWS // 2), ROWS // 2)
            mine = kept(i, half, p, (q + 1) % 4 if d == 0 else (q + 3) % 4).at[rows]
            add_rows(mine, t1[i].at[half, d], ROWS // 2, cols)
            state["v", n, half, d] = wires.push(
                mine.at[:, cols], t2[i].at[half, d, rows, cols], axes[half][2 + d]
            )

    def stage4(n, half):
        i, c0, cn = CHUNKS[n]
        cols = pl.ds(c0, cn)
        p, q = spots(half)
        for d in range(2):
            state["u", n, half, d].wait_recv()
            state["v", n, half, d].wait_recv()
        mine = kept(i, half, p, q)

        def step(g, carry):
            at = pl.ds(pl.multiple_of(g * 16, 16), 16)
            total = (
                mine[at, cols].astype(F32)
                + t2[i][half, 0, at, cols].astype(F32)
                + t2[i][half, 1, at, cols].astype(F32)
            )
            sums[i][half, at, cols] = total
            squares = total * total
            for m in range(cn // 128):
                part = squares[:, m * 128 : m * 128 + 128]
                carry = carry + part[:8] + part[8:]
            return carry

        return lax.fori_loop(0, ROWS // 16, step, jnp.zeros((8, 128), F32))

    def stage5(n):
        i, c0, cn = CHUNKS[n]
        cols = pl.ds(c0, cn)
        state["g", n] = wires.push(sums[i].at[1 - xlo, :, cols], grads[i].at[xlo, :, cols], "p")
        copy = pltpu.make_async_copy(sums[i].at[xlo, :, cols], grads[i].at[xlo, :, cols], keep.at[n])
        copy.start()
        late.append(copy)

    half_tok = TOK // 2

    def tokens1(k):
        state["c", k].wait_recv()

        def step(g, carry):
            at = pl.ds(pl.multiple_of((g % 8) * 16, 16), 16)
            s = g // 8
            own[k, s // 2, s % 2, at, :] = (
                own[k, s // 2, s % 2, at, :].astype(F32) + core[k, s // 2, s % 2, at, :].astype(F32)
            ).astype(BF)
            return carry

        lax.fori_loop(0, 32, step, 0)

        def spot(s, d, far):
            rows = pl.ds((d if far else 1 - d) * half_tok, half_tok)
            return own.at[k, s % 2, s // 2, rows]

        for d, name in enumerate(("x+", "x-")):
            state["x1", k, d] = wires.push(spot((x + 2) % 4, d, True), x1.at[k, d], name)
        for d, name in enumerate(("x+", "x-")):
            to = (x + 1) % 4 if d == 0 else (x + 3) % 4
            rows = pl.ds((1 - d) * half_tok, half_tok)
            state["x2", k, d] = wires.push(spot(to, d, False), x2.at[k, d, rows], name)

    def tokens2(k):
        for d, name in enumerate(("x+", "x-")):
            state["x1", k, d].wait_recv()
            to = (x + 1) % 4 if d == 0 else (x + 3) % 4
            rows = pl.ds(d * half_tok, half_tok)
            mine = own.at[k, to % 2, to // 2, rows]
            add_rows(mine, x1.at[k, d], half_tok, pl.ds(0, D))
            state["x3", k, d] = wires.push(mine, x2.at[k, d, rows], name)

    def tokens3(k):
        for d in range(2):
            state["x2", k, d].wait_recv()
            state["x3", k, d].wait_recv()

        def total(at):
            return (
                own[k, xlo, x // 2, at, :].astype(F32)
                + x2[k, 0, at, :].astype(F32)
                + x2[k, 1, at, :].astype(F32)
            )

        def result(g, carry):
            at = pl.ds(pl.multiple_of(g * 16, 16), 16)
            stage_tiles(shown, tokens[at, :].astype(F32) + total(at), at)
            return carry

        def gradient(g, carry):
            at = pl.ds(pl.multiple_of(g * 16, 16), 16)
            inputs = tokens[at, :].astype(F32)
            centered = inputs - jnp.mean(inputs, -1, keepdims=True)
            variance = jnp.mean(centered * centered, -1, keepdims=True)
            deviation = lax.rsqrt(variance + NORM_EPSILON)
            standard = centered * deviation
            d_normed = total(at)
            d_standard = d_normed * gains[0:1, :]
            gradient_rows = cotangent[0, at, :].astype(F32) + deviation * (
                d_standard
                - jnp.mean(d_standard, -1, keepdims=True)
                - standard * jnp.mean(d_standard * standard, -1, keepdims=True)
            )
            stage_tiles(shown, gradient_rows, at)
            return (
                carry[0] + jnp.sum(d_normed * standard, 0, keepdims=True),
                carry[1] + jnp.sum(d_normed, 0, keepdims=True),
            )

        if k == 0:
            lax.fori_loop(0, TOK // 16, result, 0)
        else:
            zero = jnp.zeros((1, D), F32)
            gain_sum, shift_sum = lax.fori_loop(0, TOK // 16, gradient, (zero, zero))
            norm1[here, 0:1, :] = gain_sum
            norm1[here, 1:2, :] = shift_sum

        def show(cols, value):
            tok_out[k, :, cols] = value.astype(BF)

        reorder(shown, 1, tiles, flips, show)

    def small1(slots):
        return [wires.push(slots.at[here], slots.at[here], to) for to in plane]

    def small2(copies, slots, after):
        for copy in copies:
            copy.wait_recv()
        total = slots[0]
        for k in range(1, 16):
            total = total + slots[k]
        after[there] = total
        return [wires.push(after.at[there], after.at[there], to) for to in line]

    def small3(copies, after):
        for copy in copies:
            copy.wait_recv()
        total = after[0]
        for k in range(1, 8):
            total = total + after[k]
        return total

    def both(step, n):
        for half in range(2):
            step(n, half)

    squares = [jnp.zeros((8, 128), F32)]

    def last(n):
        for half in range(2):
            squares[0] = squares[0] + stage4(n, half)
        stage5(n)

    fetched(v_act, 0)
    fetched(v_made, 1)
    fetched(cotangent, 3)
    waiting = [True]
    norm_copies = [None]

    def next_product(n):
        if CHUNKS[n][0] == 0 and waiting[0]:
            waiting[0] = False
            fetched(v_act, 0)
            fetched(v_back, 2)
        product(n)

    def some_branch(k, j):
        if k == 1 and j == 0:
            if waiting[0]:
                fetched(v_back, 2)
                waiting[0] = False
                fetched(v_act, 0)
            state["c", 0].wait_send()
            wires.open = [copy for copy in wires.open if copy is not state["c", 0]]
        branch(k, range(2 * j, 2 * j + 2))

    def norm_step(number):
        if number == 1:
            norm_copies[0] = small1(norm1)
        elif number == 2:
            norm_copies[0] = small2(norm_copies[0], norm1, norm2)
        else:
            stage_tiles(shown, small3(norm_copies[0], norm2), pl.ds(0, 2))

            def show_norm(cols, value):
                norm_out[:, cols] = value

            reorder(shown, 1, tiles, flips, show_norm, 8)

    steps = {
        "P": next_product,
        "R": lambda: fetch(toks.at[0], v_act, 0),
        "A": lambda n: both(stage0, n),
        "B": lambda n: both(stage0b, n),
        "S1": lambda n: both(stage1, n),
        "S2": lambda n: both(stage2, n),
        "S3": lambda n: both(stage3, n),
        "L": last,
        "BR": some_branch,
        "X": cross,
        "T1": tokens1,
        "T2": tokens2,
        "T3": tokens3,
        "N1": lambda: norm_step(1),
        "N2": lambda: norm_step(2),
        "N3": lambda: norm_step(3),
    }
    for name, *at in SCATTER_ORDER:
        steps[name](*at)
    square1[here] = squares[0]
    square_copies = small1(square1)
    square_copies = small2(square_copies, square1, square2)
    square_out[...] = small3(square_copies, square2)
    for n in range(len(CHUNKS)):
        state["g", n].wait_recv()
    wires.close()
    for copy in late:
        copy.wait()


def scatter_all(tiles, flips, made, back, toks, wall_a, wall_b, tokens, gains):
    any_ = pl.BlockSpec(memory_space=pl.ANY)
    vmem = pl.BlockSpec(memory_space=pltpu.VMEM)

    def both(*shape, dtype=BF):
        return [pltpu.VMEM(shape + (CA,), dtype), pltpu.VMEM(shape + (CB,), dtype)]

    return pl.pallas_call(
        scatter_kernel,
        out_shape=(
            jax.ShapeDtypeStruct((2, ROWS, CA), F32),
            jax.ShapeDtypeStruct((2, ROWS, CB), F32),
            jax.ShapeDtypeStruct((2, TOK, D), BF),
            jax.ShapeDtypeStruct((8, D), F32),
            jax.ShapeDtypeStruct((8, 128), F32),
        ),
        in_specs=[pl.BlockSpec(memory_space=pltpu.SMEM), vmem] + [any_] * 5 + [vmem] * 2,
        out_specs=(any_, any_, vmem, vmem, vmem),
        scratch_shapes=[
            pltpu.VMEM((GROUP, D), BF),
            pltpu.VMEM((GROUP, CB), BF),
            pltpu.VMEM((GROUP, CA), BF),
            pltpu.VMEM((2, FEATS, CA), BF),
            pltpu.VMEM((2, FEATS, CB), BF),
            *both(2, 4, 4, ROWS),
            pltpu.VMEM((2, 2, TOK, D), BF),
            *both(2, 2, 2, ROWS),
            *both(2, 2, 4, ROWS),
            *both(2, 2, ROWS // 2),
            *both(2, 2, ROWS),
            *both(2, ROWS, dtype=F32),
            pltpu.VMEM((2, 2, 2, TOK, D), BF),
            pltpu.VMEM((2, 2, 2, TOK, D), BF),
            pltpu.VMEM((2, 2, TOK // 2, D), BF),
            pltpu.VMEM((2, 2, TOK, D), BF),
            pltpu.VMEM((16, 2, D), F32),
            pltpu.VMEM((8, 2, D), F32),
            pltpu.VMEM((16, 8, 128), F32),
            pltpu.VMEM((8, 8, 128), F32),
            pltpu.VMEM((D // 128, TOK, 128), F32),
            pltpu.VMEM((1, TOK, D), BF),
            pltpu.SemaphoreType.DMA((224,)),
            pltpu.SemaphoreType.DMA((224,)),
            pltpu.SemaphoreType.DMA((8,)),
            pltpu.SemaphoreType.DMA((8,)),
        ],
        compiler_params=pltpu.CompilerParams(
            collective_id=1, has_side_effects=True, vmem_limit_bytes=62 * 2**20
        ),
    )(tiles, flips, made, back, toks, wall_a, wall_b, tokens, gains)


def halves(item):
    high = item.astype(BF)
    return high, (item - high.astype(F32)).astype(BF)


def near_product(left, right, dims):
    (a, a_low), (b, b_low) = left, right
    axis = 0 if dims == (((1,), (0,)), ((), ())) else 1
    return lax.dot_general(
        jnp.concatenate([a, a, a_low], 1),
        jnp.concatenate([b, b_low, b], axis),
        dims,
        preferred_element_type=F32,
    )


def update_kernel(tok, squares, norm_raw, norm_params, norm_moment1, norm_moment2, grad_a, grad_b, *refs):
    ins, refs = refs[:20], refs[20:]
    out, input_grad, grad_norm, norm_grads, norm_first, norm_second, norm_new = refs[:7]
    outs, v_ins, v_outs, came, left = refs[7:27], refs[27:47], refs[47:67], refs[67], refs[68]
    weights, firsts, seconds, bases = v_ins[0:5], v_ins[5:10], v_ins[10:15], v_ins[15:20]
    grads, firsts_new, seconds_new, weights_new = v_outs[0:5], v_outs[5:10], v_outs[10:15], v_outs[15:20]
    parts = (grad_a, grad_b)
    order = (1, 2, 3, 4, 0)
    arriving = {}
    for i in order:
        for k in range(4):
            n = 5 * k + i
            arriving[i, k] = pltpu.make_async_copy(ins[n], v_ins[n], came.at[n])
            arriving[i, k].start()
    out[...] = tok[0]
    input_grad[...] = tok[1]
    leaving = []
    left_lanes = lax.broadcasted_iota(jnp.int32, (1, 128), 1) < 64

    def whole(item):
        return jnp.sum(jnp.sum(item, 0, keepdims=True), 1, keepdims=True)

    raw = norm_raw[0:2, :]
    length = jnp.sqrt(whole(squares[...]) + whole(raw * raw))
    clip = jnp.minimum(1.0, CLIP_LIMIT / length)
    grad_norm[...] = length
    norm_grads[...] = clip * raw
    norm_first[...], norm_second[...], norm_new[...] = adam_plain(
        norm_params[...], clip * raw, norm_moment1[...], norm_moment2[...], NORM_RATE
    )

    def fetch(piece, side):
        i, half, column = piece
        tile = parts[i][half, :, pl.ds(column // 128 * 128, 128)]
        return tile if column // 64 % 2 == side else pltpu.roll(tile, 64, 1)

    tables = pieces()
    for i in order:
        table = tables[i]
        for k in range(4):
            arriving[i, k].wait()
        blocks = range(WIDTHS[i] // 128)
        for group in (blocks[at : at + 4] for at in range(0, len(blocks), 4)):
            bases_of = [halves(bases[i][block]) for block in group]
            clipped = []
            for block in group:
                one, two = table[2 * block], table[2 * block + 1]
                if two == one[:2] + (one[2] + 64,) and one[2] % 128 == 0:
                    grad = parts[one[0]][one[1], :, pl.ds(one[2], 128)]
                else:
                    grad = jnp.where(left_lanes, fetch(one, 0), fetch(two, 1))
                clipped.append(clip * grad)
            turned = [
                near_product(halves(grad), basis, (((1,), (0,)), ((), ())))
                for grad, basis in zip(clipped, bases_of)
            ]
            ratios = []
            for block, grad, item in zip(group, clipped, turned):
                cols = pl.ds(block * 128, 128)
                first = BETA_ONE * firsts[i][:, cols] + (1.0 - BETA_ONE) * item
                second = BETA_TWO * seconds[i][:, cols] + (1.0 - BETA_TWO) * item * item
                grads[i][:, cols] = grad
                firsts_new[i][:, cols] = first
                seconds_new[i][:, cols] = second
                ratios.append(
                    first
                    * (1.0 / (1.0 - BETA_ONE**STEP))
                    / (jnp.sqrt(second * (1.0 / (1.0 - BETA_TWO**STEP))) + ADAM_EPS)
                )
            turned_back = [
                near_product(halves(ratio), basis, COLS_DIMS) for ratio, basis in zip(ratios, bases_of)
            ]
            for block, item in zip(group, turned_back):
                cols = pl.ds(block * 128, 128)
                weight = weights[i][:, cols]
                weights_new[i][:, cols] = weight - RATE_LIST[i] * (item + WEIGHT_DECAY * weight)
        for k in range(4):
            n = 5 * k + i
            copy = pltpu.make_async_copy(v_outs[n], outs[n], left.at[n])
            copy.start()
            leaving.append(copy)
    for copy in leaving:
        copy.wait()


def update(tok, squares, norm, grad_a, grad_b, weights, firsts, seconds, bases):
    vmem = pl.BlockSpec(memory_space=pltpu.VMEM)
    any_ = pl.BlockSpec(memory_space=pl.ANY)
    shapes = [jax.ShapeDtypeStruct((ROWS, width), F32) for width in WIDTHS]
    small = [jax.ShapeDtypeStruct((TOK, D), BF)] * 2
    small += [jax.ShapeDtypeStruct((1, 1), F32)] + [jax.ShapeDtypeStruct((2, D), F32)] * 4
    state = (*weights, *firsts, *seconds, *bases)
    return pl.pallas_call(
        update_kernel,
        out_shape=tuple(small + shapes * 4),
        in_specs=[vmem] * 8 + [any_] * 20,
        out_specs=(vmem,) * 7 + (any_,) * 20,
        scratch_shapes=[pltpu.VMEM(item.shape, F32) for item in state]
        + [pltpu.VMEM(item.shape, F32) for item in shapes * 4]
        + [pltpu.SemaphoreType.DMA((20,))] * 2,
        compiler_params=pltpu.CompilerParams(vmem_limit_bytes=56 * 2**20),
    )(tok, squares, *norm, grad_a, grad_b, *state)


def adam_plain(param, grad, first, second, rate):
    first_new = BETA_ONE * first + (1.0 - BETA_ONE) * grad
    second_new = BETA_TWO * second + (1.0 - BETA_TWO) * grad * grad
    ratio = (
        first_new
        / (1.0 - BETA_ONE**STEP)
        / (jnp.sqrt(second_new / (1.0 - BETA_TWO**STEP)) + ADAM_EPS)
    )
    return (first_new, second_new, param - rate * ratio)


def body(
    tokens,
    cotangent,
    doc_lengths,
    row_owner,
    norm_params,
    norm_moment1,
    norm_moment2,
    qkv_weight,
    out_weight,
    gate_weight,
    up_weight,
    down_weight,
    qkv_moment1,
    out_moment1,
    gate_moment1,
    up_moment1,
    down_moment1,
    qkv_moment2,
    out_moment2,
    gate_moment2,
    up_moment2,
    down_moment2,
    qkv_basis,
    out_basis,
    gate_basis,
    up_basis,
    down_basis,
):
    blocks = jnp.arange(32, dtype=jnp.int32)
    inverse = jnp.sum((row_owner[None, :] == blocks[:, None]) * blocks[None, :], 1)
    tiles, flips = places(jnp.stack([inverse, row_owner]))
    weights = (qkv_weight, out_weight, gate_weight, up_weight, down_weight)
    wall_a, wall_b, toks, made, back, tokens_stored, params_stored = gather_all(
        tiles, flips, tokens, cotangent, norm_params, doc_lengths, weights
    )
    grad_a, grad_b, tok_out, norm_raw, squares = scatter_all(
        tiles, flips, made, back, toks, wall_a, wall_b, tokens_stored, params_stored
    )
    firsts = (qkv_moment1, out_moment1, gate_moment1, up_moment1, down_moment1)
    seconds = (qkv_moment2, out_moment2, gate_moment2, up_moment2, down_moment2)
    bases = (qkv_basis, out_basis, gate_basis, up_basis, down_basis)
    norm = (norm_raw, norm_params, norm_moment1, norm_moment2)
    out, input_grad, grad_norm, *rest = update(
        tok_out, squares, norm, grad_a, grad_b, weights, firsts, seconds, bases
    )
    return (out, input_grad, grad_norm[0, 0], *rest)


def solution(mesh):
    tok, weight, whole = P(("dp", "mp"), None), P("dp", "mp"), P()
    in_specs = (tok, tok, P("dp", None)) + (whole,) * 4 + (weight,) * 15 + (P("mp", None, None),) * 5
    out_specs = (tok, tok) + (whole,) * 5 + (weight,) * 20
    return jax.shard_map(body, mesh=mesh, in_specs=in_specs, out_specs=out_specs, check_vma=False)
```

```python
import jax
import jax.numpy as jnp
from jax import lax
from jax.experimental import pallas as pl
from jax.experimental.pallas import tpu as pltpu
from jax.sharding import PartitionSpec as P

MESH = pl.DeviceIdType.MESH
BF = jnp.bfloat16
F32 = jnp.float32

HEAD_DIM = 64
ROT = 16
STEP = 5

NORM_EPSILON = 1e-05
BETA_ONE = 0.5
BETA_TWO = 0.5
ADAM_EPS = 1e-08
WEIGHT_DECAY = 0.01
RATE_LIST = (0.02, 0.1, 0.02, 0.02, 0.015)
NORM_RATE = 0.2
CLIP_LIMIT = 1.0
MASK_FILL = -1e30
ROWS_DIMS = (((0,), (0,)), ((), ()))
COLS_DIMS = (((1,), (1,)), ((), ()))

D = 2048
LEN = 512
ROWS = 64
TOK = 128
GROUP = 1024
HEADS = 4
CA = 2176
CB = 1024
CHUNKS = ((1, 0, 512), (1, 512, 512), (0, 0, 512), (0, 512, 512), (0, 1024, 512), (0, 1536, 640))


def place():
    dp = lax.axis_index("dp")
    mp = lax.axis_index("mp")
    return (mp // 2) * 2 + dp // 16, dp % 4, (dp // 4) % 4, mp % 2


def device(x, y, z, c):
    return ((x % 2) * 16 + z * 4 + y, (x // 2) * 2 + c)


def near(me, name):
    x, y, z, c = me
    return {
        "y+": lambda: device(x, (y + 1) % 4, z, c),
        "y-": lambda: device(x, (y + 3) % 4, z, c),
        "z+": lambda: device(x, y, (z + 1) % 4, c),
        "z-": lambda: device(x, y, (z + 3) % 4, c),
        "x+": lambda: device((x + 1) % 4, y, z, c),
        "x-": lambda: device((x + 3) % 4, y, z, c),
        "c": lambda: device(x, y, z, 1 - c),
        "p": lambda: device((x // 2) * 2 + 1 - x % 2, y, z, c),
    }[name]()


NEIGHBOURS = ("y+", "y-", "z+", "z-", "x+", "x-", "c")


class Wires:
    def __init__(self, me, send, recv):
        self.me, self.send, self.recv = me, send, recv
        self.count = 0
        self.open = []

    def push(self, src, dst, to, at=None):
        if at is None:
            at = self.count
            self.count += 1
        if isinstance(to, str):
            to = near(self.me, to)
        copy = pltpu.make_async_remote_copy(
            src, dst, self.send.at[at], self.recv.at[at], device_id=to, device_id_type=MESH
        )
        copy.start()
        self.open.append(copy)
        return copy

    def take(self, number):
        at = self.count
        self.count += number
        return at

    def close(self, number=None):
        number = len(self.open) if number is None else number
        for copy in self.open[:number]:
            copy.wait_send()
        self.open = self.open[number:]


WIDTHS = (1536, 512, 1408, 1408, 1408)


def pieces():
    table = [[], [], [], [], []]
    for half in range(2):
        for head in range(HEADS):
            for kind in range(3):
                table[0].append((0, half, head // 2 * 384 + kind * 128 + head % 2 * 64))
        for head in range(HEADS):
            table[1].append((1, half, head * 64))
    gate = [768 + 64 * k for k in range(6)] + [1536 + 64 * k for k in range(4)]
    up = [1152 + 64 * k for k in range(6)] + [1792 + 64 * k for k in range(4)]
    down = [256 + 64 * k for k in range(10)]
    for n, (i, starts, rest) in enumerate(((0, gate, 2048), (0, up, 2112), (1, down, 896))):
        table[2 + n] += [(i, 0, start) for start in starts]
        table[2 + n] += [(i, 0, rest), (i, 1, rest)]
        table[2 + n] += [(i, 1, start) for start in starts]
    return table


def reorder(staged, which, tiles, flips, store, rows=TOK):
    left = lax.broadcasted_iota(jnp.int32, (1, 128), 1) < 64
    for k in range(D // 128):
        sides = []
        for side in range(2):
            n = 2 * k + side
            tile = staged[tiles[which, n]][:rows]
            flip = jnp.broadcast_to(flips[which : which + 1, n : n + 1], (1, 128))
            sides.append(jnp.where(flip > 0.0, pltpu.roll(tile, 64, 1), tile))
        store(pl.ds(k * 128, 128), jnp.where(left, sides[0], sides[1]))


def stage_tiles(staged, value, rows):
    for k in range(D // 128):
        staged[k, rows, :] = value[:, k * 128 : k * 128 + 128].astype(F32)


def places(orders):
    spots = jnp.arange(32, dtype=jnp.int32)
    return orders // 2, ((orders + spots) % 2).astype(F32)


LOADS = ((0, 0, 768), (1, 0, 256), (1, 256, 768), (0, 768, 768), (0, 1536, 640))


GATHER_ORDER = (
    ("AG", 1), ("OWN", 1), ("AG", 0), ("OWN", 0), ("TS", 1), ("SW", 1), ("H3", 1, 0, 0), ("H1", 1, 0),
    ("AG", 2), ("SW", 0), ("H3", 0, 0, 0), ("AG", 4), ("AG", 3), ("OWN", 3), ("H3", 1, 1, 0), ("TS", 0),
    ("H3", 1, 0, 1), ("H3", 1, 0, 2), ("H1", 1, 1), ("H1", 0, 0), ("H1", 0, 1), ("OWN", 2), ("H2", 1, 0),
    ("H3", 0, 1, 0), ("TB",), ("H3", 1, 1, 1), ("H2", 1, 1), ("H3", 1, 1, 2), ("H2", 0, 0), ("OWN", 4),
    ("TF", 1), ("H3", 0, 0, 1), ("H3", 0, 1, 1), ("SW", 3), ("H1", 3, 0), ("H3", 3, 0, 0), ("H3", 0, 0, 2),
    ("H2", 0, 1), ("H3", 0, 1, 2), ("H3", 1, 0, 3), ("H3", 1, 1, 3), ("H3", 0, 0, 3), ("SW", 2), ("H2", 3, 0),
    ("H3", 2, 0, 0), ("TF", 0), ("H3", 0, 1, 3), ("H3", 3, 1, 0), ("H3", 3, 0, 1), ("H1", 2, 0), ("H1", 3, 1),
    ("H3", 2, 1, 0), ("ARR", 1), ("PR", 1, 0), ("ARR", 0), ("PR", 0, 0), ("H1", 2, 1), ("AT", 1, 0),
    ("H3", 3, 0, 3), ("H2", 2, 0), ("H3", 3, 1, 2), ("TL", 1), ("AT", 0, 0), ("TL", 0), ("H3", 2, 1, 1),
    ("H3", 2, 0, 2), ("PR", 1, 1), ("H3", 2, 1, 2), ("H2", 3, 1), ("H3", 2, 0, 1), ("H3", 3, 0, 2),
    ("H3", 3, 1, 1), ("SW", 4), ("H1", 4, 0), ("H3", 4, 0, 0), ("H2", 2, 1), ("PR", 0, 1), ("H3", 2, 0, 3),
    ("AT", 0, 1), ("H2", 4, 0), ("H3", 3, 1, 3), ("H3", 4, 1, 0), ("H1", 4, 1), ("AT", 1, 1), ("H3", 4, 0, 2),
    ("H3", 2, 1, 3), ("ARR", 3), ("PR", 3, 1), ("H3", 4, 1, 1), ("PR", 3, 0), ("H2", 4, 1), ("H3", 4, 0, 1),
    ("H3", 4, 1, 2), ("H3", 4, 0, 3), ("ARR", 2), ("PR", 2, 1), ("H3", 4, 1, 3), ("PR", 2, 0), ("U", 0, 0),
    ("U", 0, 1), ("ARR", 4), ("PR", 4, 1), ("U", 1, 1), ("PR", 4, 0), ("U", 1, 0),
)


def swapped(field, lane):
    return jnp.where(lane % ROT < ROT // 2, pltpu.roll(field, 120, 1), pltpu.roll(field, ROT // 2, 1))


def gather_kernel(
    tiles, flips, tokens, cotangent, params, lengths, qkv_w, out_w, gate_w, up_w, down_w,
    wall_a, wall_b, toks, made, back, tokens_out, params_out,
    own_a, own_b, v_wall_a, v_wall_b, v_toks, v_made, v_back, pre_a, pre_b, docs, cosine, sine, bias, inputs, staged,
    send, recv, keep,
):
    me = x, y, z, c = place()
    xlo, xhi = x % 2, x // 2
    wires = Wires(me, send, recv)
    owns, walls, v_walls = (own_a, own_b), (wall_a, wall_b), (v_wall_a, v_wall_b)
    late = []
    lane = lax.broadcasted_iota(jnp.int32, (1, 128), 1)
    mine = [lane < HEAD_DIM, lane >= HEAD_DIM]

    def local(src, dst):
        copy = pltpu.make_async_copy(src, dst, keep.at[len(late)])
        copy.start()
        late.append(copy)

    barrier = pltpu.get_barrier_semaphore()
    for name in NEIGHBOURS:
        pl.semaphore_signal(barrier, inc=1, device_id=near(me, name), device_id_type=MESH)

    sources = {}
    for weight, table in zip((qkv_w, out_w, gate_w, up_w, down_w), pieces()):
        for n, spot in enumerate(table):
            sources[spot] = (weight, n)
    def arrange(chunk):
        i, c0, cn = chunk
        for half in range(2):
            for column in range(c0, c0 + cn, 128):
                sides = []
                for side in range(2):
                    spot = (i, half, column + 64 * side)
                    if spot not in sources:
                        sides.append(jnp.zeros((ROWS, 128), F32))
                        continue
                    weight, n = sources[spot]
                    tile = weight[:, pl.ds(n // 2 * 128, 128)]
                    sides.append(tile if n % 2 == side else pltpu.roll(tile, 64, 1))
                owns[i][half, :, pl.ds(column, 128)] = jnp.where(mine[0], sides[0], sides[1]).astype(BF)


    own_first = wires.take(8 * len(LOADS))
    swaps, forwards, seconds, lasts = {}, {}, {}, {}
    lo, hi = slice(0, ROWS // 2), slice(ROWS // 2, ROWS)

    def half_of(part):
        return (xlo + part) % 2

    def way(part, d):
        half = half_of(part)
        along_y = 1 - half if d < 2 else half
        move = 1 if d % 2 == 0 else 3
        return device(x, (y + along_y * move) % 4, (z + (1 - along_y) * move) % 4, c)

    def spots(part):
        half = half_of(part)
        return y + half * (z - y), z + half * (y - z)

    def block(n, part, a, b, some=slice(0, ROWS)):
        i, c0, cn = LOADS[n]
        half = half_of(part)
        at = half * 16 + (b + half * (a - b)) * 4 + a + half * (b - a)
        at = pl.ds(pl.multiple_of(at * ROWS + some.start, 32), some.stop - some.start)
        return v_walls[i].at[at, pl.ds(c0, cn)]

    def own_at(n, part, d):
        return own_first + n * 8 + part * 4 + d

    def own_block(n, part):
        a, b = spots(part)
        return block(n, part, a, b)

    def send_own(n):
        i, c0, cn = LOADS[n]
        cols = pl.ds(c0, cn)
        own = owns[i].at[xlo, :, cols]
        for d in range(4):
            wires.push(own, own_block(n, 0), way(0, d), own_at(n, 0, d))
        swaps[n] = wires.push(owns[i].at[1 - xlo, :, cols], own_block(n, 0), "p")
        v_walls[i][pl.ds(pl.multiple_of((xlo * 16 + z * 4 + y) * ROWS, ROWS), ROWS), cols] = owns[i][xlo, :, cols]

    def send_swapped(n):
        swaps[n].wait_recv()
        for d in range(4):
            wires.push(own_block(n, 1), own_block(n, 1), way(1, d), own_at(n, 1, d))

    def wait_own(n, part, d):
        at = own_at(n, part, d)
        pltpu.make_async_remote_copy(
            own_block(n, part), own_block(n, part), send.at[at], recv.at[at],
            device_id=way(part, d), device_id_type=MESH,
        ).wait_recv()

    def hop1(n, part):
        a, b = spots(part)
        wait_own(n, part, 0)
        some = block(n, part, (a + 3) % 4, b, lo)
        forwards[n, part, 0] = wires.push(some, some, way(part, 0))
        wait_own(n, part, 1)
        some = block(n, part, (a + 1) % 4, b, hi)
        forwards[n, part, 1] = wires.push(some, some, way(part, 1))
        for j, spot in ((1, (a + 3) % 4), (2, (a + 1) % 4)):
            item = block(n, part, spot, b)
            seconds[n, part, j, 0] = wires.push(item, item, way(part, 2))
            seconds[n, part, j, 1] = wires.push(item, item, way(part, 3))

    def hop2(n, part):
        a, b = spots(part)
        forwards[n, part, 0].wait_recv()
        forwards[n, part, 1].wait_recv()
        item = block(n, part, (a + 2) % 4, b)
        seconds[n, part, 3, 0] = wires.push(item, item, way(part, 2))
        seconds[n, part, 3, 1] = wires.push(item, item, way(part, 3))

    def hop3(n, part, j):
        a, b = spots(part)
        spot = (a + (0, 3, 1, 2)[j]) % 4
        for d in range(2):
            if j == 0:
                wait_own(n, part, 2 + d)
            else:
                seconds[n, part, j, d].wait_recv()
            some = block(n, part, spot, (b + 3) % 4 if d == 0 else (b + 1) % 4, lo if d == 0 else hi)
            lasts[n, part, j, d] = wires.push(some, some, way(part, 2 + d))

    def arrived(n):
        for j in range(4):
            for part in range(2):
                for d in range(2):
                    lasts[n, part, j, d].wait_recv()
        i, c0, cn = LOADS[n]
        local(v_walls[i].at[:, pl.ds(c0, cn)], walls[i].at[:, pl.ds(c0, cn)])


    tok_x, tok_f, tok_c = {}, {}, [[], []]
    whole = set()

    def tok_at(sx, cc, start=0, size=TOK):
        return pl.ds(pl.multiple_of(((sx % 2) * 4 + (sx // 2) * 2 + cc) * TOK + start, 64), size)

    def tokens_start(k):
        def keep_tokens(cols, value):
            inputs[:, cols] = value
            tokens_out[:, cols] = value.astype(BF)

        def keep_cotangent(cols, value):
            v_toks[1, tok_at(x, c), cols] = value.astype(BF)

        def keep_params(cols, value):
            params_out[:, cols] = value

        def step(g, carry):
            at = pl.ds(pl.multiple_of(g * 16, 16), 16)
            item = inputs[at, :]
            centered = item - jnp.mean(item, -1, keepdims=True)
            variance = jnp.mean(centered * centered, -1, keepdims=True)
            standard = centered * lax.rsqrt(variance + NORM_EPSILON)
            normed = standard * params_out[0:1, :] + params_out[1:2, :]
            v_toks[0, pl.ds(pl.multiple_of((xlo * 4 + xhi * 2 + c) * TOK + g * 16, 16), 16), :] = normed.astype(BF)
            return carry

        every = pl.ds(0, TOK)
        if k == 0:
            stage_tiles(staged, jnp.zeros((8, D), F32), pl.ds(0, 8))
            stage_tiles(staged, params, pl.ds(0, 2))
            reorder(staged, 0, tiles, flips, keep_params, 8)
            stage_tiles(staged, tokens, every)
            reorder(staged, 0, tiles, flips, keep_tokens)
            lax.fori_loop(0, TOK // 16, step, 0)
        else:
            stage_tiles(staged, cotangent, every)
            reorder(staged, 0, tiles, flips, keep_cotangent)
        item = v_toks.at[k, tok_at(x, c)]
        for name in ("x+", "x-"):
            tok_x[k, name] = wires.push(item, item, name)
        tok_c[k].append(wires.push(item, item, "c"))

    def tokens_forward(k):
        for n, name in enumerate(("x+", "x-")):
            tok_x[k, name].wait_recv()
            sx = (x + 3) % 4 if n == 0 else (x + 1) % 4
            item = v_toks.at[k, tok_at(sx, c)]
            part = v_toks.at[k, tok_at(sx, c, n * (TOK // 2), TOK // 2)]
            tok_f[k, n] = wires.push(part, part, name)
            tok_c[k].append(wires.push(item, item, "c"))

    def tokens_last(k):
        tok_f[k, 0].wait_recv()
        tok_f[k, 1].wait_recv()
        item = v_toks.at[k, tok_at((x + 2) % 4, c)]
        tok_c[k].append(wires.push(item, item, "c"))

    def tokens_whole(k, part):
        if (k, part) in whole:
            return
        whole.add((k, part))
        for n in ((1, 2), (0, 3))[part]:
            tok_c[k][n].wait_recv()
        if len(whole & {(k, 0), (k, 1)}) == 2:
            local(v_toks.at[k], toks.at[k])

    def first_row(part):
        return (xlo + 1 + part) % 2 * LEN


    def product(n, part):
        i, c0, cn = LOADS[n]
        tokens_whole(i, part)
        start = first_row(part)
        pre = (pre_a, pre_b)[i]

        at = pl.ds(pl.multiple_of(start, LEN), LEN)
        pre[at, pl.ds(c0, cn)] = jnp.dot(
            v_toks[i, at, :], v_walls[i][:, pl.ds(c0, cn)], preferred_element_type=F32
        )

    def flush(src, dst, at, cols):
        local(src.at[at, cols], dst.at[at, cols])

    def doc_start(s, index, shape):
        start = jnp.zeros(shape, F32)
        end = jnp.zeros((1, 1), F32)
        for j in range(3):
            end = end + docs[s, 0:1, j : j + 1]
            start = jnp.where(index >= end, end, start)
        return start

    def tables():
        doc_swap[0].wait_recv()
        for s in range(2):
            mask(s)
            index = lax.broadcasted_iota(jnp.int32, (LEN, 128), 0).astype(F32)
            entry = lane % HEAD_DIM
            freq = jnp.zeros((1, 128), F32)
            for e in range(ROT // 2):
                freq = jnp.where(entry % (ROT // 2) == e, 10000.0 ** (-2.0 * e / ROT), freq)
            angle = (index - doc_start(s, index, (LEN, 128))) * freq
            turn = jnp.sin(angle)
            cosine[pl.ds(s * LEN, LEN), :] = jnp.where(entry < ROT, jnp.cos(angle), 1.0)
            sine[pl.ds(s * LEN, LEN), :] = jnp.where(
                entry < ROT // 2, -turn, jnp.where(entry < ROT, turn, 0.0)
            )

    def mask(s):
        query_at = lax.broadcasted_iota(jnp.int32, (1, LEN), 1).astype(F32)
        key_at = lax.broadcasted_iota(jnp.int32, (LEN, 1), 0).astype(F32)
        start = doc_start(s, query_at, (1, LEN))
        bias[s] = jnp.where((key_at >= start) & (key_at <= query_at), 0.0, MASK_FILL)

    def attend(pair, part):
        s, start = (xlo + 1 + part) % 2, first_row(part)
        at_rows = pl.ds(pl.multiple_of(start, LEN), LEN)
        cos_rows = cosine[at_rows, :]
        sin_rows = sine[at_rows, :]

        def turned(at):
            field = pre_a[at_rows, pl.ds(at, 128)]
            return field * cos_rows + swapped(field, lane) * sin_rows

        at, first = pair * 128, pair * 384
        query = (turned(first) * (HEAD_DIM**-0.5)).astype(BF)
        key = turned(first + 128).astype(BF)
        value = pre_a[at_rows, pl.ds(first + 256, 128)].astype(BF)
        d_attn = pre_b[at_rows, pl.ds(at, 128)].astype(BF)
        key_t = key.T
        value_t = value.T
        d_key = [None, None]
        d_value = [None, None]
        zero = jnp.zeros((), BF)
        head_row = lax.broadcasted_iota(jnp.int32, (128, 1), 0) < HEAD_DIM
        for block in range(2):
            queries = slice(block * 256, block * 256 + 256)
            keys = (block + 1) * 256
            attn_t = []
            d_query_t = []
            for h in range(2):
                query_h = jnp.where(mine[h], query[queries], zero)
                d_attn_h = jnp.where(mine[h], d_attn[queries], zero)
                scores = lax.dot_general(key[:keys], query_h, COLS_DIMS, preferred_element_type=F32)
                scores = scores + bias[s, 0:keys, queries]
                peak = jnp.max(scores, 0, keepdims=True)
                expo = jnp.exp(scores - peak)
                probs = expo * (1.0 / jnp.sum(expo, 0, keepdims=True))
                probs_low = probs.astype(BF)
                d_prob = lax.dot_general(value[:keys], d_attn_h, COLS_DIMS, preferred_element_type=F32)
                delta = jnp.sum(probs * d_prob, 0, keepdims=True)
                d_score = (probs * (d_prob - delta)).astype(BF)
                attn_t.append(jnp.dot(value_t[:, :keys], probs_low, preferred_element_type=F32))
                d_query_t.append(jnp.dot(key_t[:, :keys], d_score, preferred_element_type=F32))
                d_value_h = jnp.dot(probs_low, d_attn_h, preferred_element_type=F32)
                d_key_h = jnp.dot(d_score, query_h, preferred_element_type=F32)
                for p in range(block + 1):
                    part = slice(p * 256, p * 256 + 256)
                    d_value[p] = d_value_h[part] if d_value[p] is None else d_value[p] + d_value_h[part]
                    d_key[p] = d_key_h[part] if d_key[p] is None else d_key[p] + d_key_h[part]
            out_rows = pl.ds(pl.multiple_of(start + block * 256, 256), 256)
            v_made[out_rows, pl.ds(at, 128)] = jnp.where(head_row, attn_t[0], attn_t[1]).T.astype(BF)
            d_query = jnp.where(head_row, d_query_t[0], d_query_t[1]).T * (HEAD_DIM**-0.5)
            d_query = d_query * cosine[out_rows, :] - swapped(d_query, lane) * sine[out_rows, :]
            v_back[out_rows, pl.ds(first, 128)] = d_query.astype(BF)
        d_key = jnp.concatenate(d_key, 0)
        d_key = d_key * cos_rows - swapped(d_key, lane) * sin_rows
        v_back[at_rows, pl.ds(first + 128, 128)] = d_key.astype(BF)
        v_back[at_rows, pl.ds(first + 256, 128)] = jnp.concatenate(d_value, 0).astype(BF)
        flush(v_made, made, at_rows, pl.ds(at, 128))
        flush(v_back, back, at_rows, pl.ds(first, 384))

    def unit(gate, up, d_hidden):
        sigma = 0.5 + 0.5 * jnp.tanh(0.5 * gate)
        silu = gate * sigma
        return silu * up, d_hidden * up * sigma * (1.0 + gate * (1.0 - sigma)), d_hidden * silu

    def units(gate_at, width, down_at, rest, part):
        start = first_row(part)

        def step(g, carry):
            at = pl.ds(pl.multiple_of(start + g * 32, 32), 32)
            gates, ups, downs = pl.ds(gate_at, width), pl.ds(gate_at + width, width), pl.ds(down_at, width)
            hidden, d_gate, d_up = unit(pre_a[at, gates], pre_a[at, ups], pre_b[at, downs])
            v_made[at, downs] = hidden.astype(BF)
            v_back[at, gates] = d_gate.astype(BF)
            v_back[at, ups] = d_up.astype(BF)
            if rest:
                both = pre_a[at, pl.ds(2048, 128)]
                hidden, d_gate, d_up = unit(both, pltpu.roll(both, 64, 1), pre_b[at, pl.ds(896, 128)])
                v_made[at, pl.ds(896, 128)] = jnp.where(mine[0], hidden, 0.0).astype(BF)
                v_back[at, pl.ds(2048, 128)] = jnp.where(mine[0], d_gate, pltpu.roll(d_up, 64, 1)).astype(BF)
            return carry

        lax.fori_loop(0, LEN // 32, step, 0)
        every = pl.ds(pl.multiple_of(start, LEN), LEN)
        flush(v_made, made, every, pl.ds(down_at, width + (128 if rest else 0)))
        flush(v_back, back, every, pl.ds(gate_at, 2 * width + (128 if rest else 0)))


    doc_swap = [wires.take(1)]
    steps = {
        "AG": lambda n: arrange(LOADS[n]),
        "OWN": send_own,
        "SW": send_swapped,
        "H1": hop1,
        "H2": hop2,
        "H3": hop3,
        "ARR": arrived,
        "TS": tokens_start,
        "TF": tokens_forward,
        "TL": tokens_last,
        "PR": product,
        "TB": tables,
        "AT": attend,
        "U": lambda k, part: units(1536, 256, 640, True, part) if k else units(768, 384, 256, False, part),
    }
    met = False
    for name, *at in GATHER_ORDER:
        if name in ("OWN", "TS") and not met:
            met = True
            pl.semaphore_wait(barrier, len(NEIGHBOURS))
            item = jnp.zeros((8, 128), F32)
            for j in range(4):
                item = jnp.where(lane == j, lengths[0:1, j : j + 1].astype(F32), item)
            docs[xlo] = item
            doc_swap[0] = wires.push(docs.at[xlo], docs.at[xlo], "p", doc_swap[0])
        if (name, *at) == ("ARR", len(LOADS) - 1):
            wires.close()
        steps[name](*at)
    for copy in late:
        copy.wait()


def gather_all(tiles, flips, tokens, cotangent, params, lengths, weights):
    any_ = pl.BlockSpec(memory_space=pl.ANY)
    vmem = pl.BlockSpec(memory_space=pltpu.VMEM)
    return pl.pallas_call(
        gather_kernel,
        out_shape=(
            jax.ShapeDtypeStruct((D, CA), BF),
            jax.ShapeDtypeStruct((D, CB), BF),
            jax.ShapeDtypeStruct((2, GROUP, D), BF),
            jax.ShapeDtypeStruct((GROUP, CB), BF),
            jax.ShapeDtypeStruct((GROUP, CA), BF),
            jax.ShapeDtypeStruct((TOK, D), BF),
            jax.ShapeDtypeStruct((8, D), F32),
        ),
        in_specs=[pl.BlockSpec(memory_space=pltpu.SMEM)] + [vmem] * 10,
        out_specs=(any_,) * 5 + (vmem,) * 2,
        scratch_shapes=[
            pltpu.VMEM((2, ROWS, CA), BF),
            pltpu.VMEM((2, ROWS, CB), BF),
            pltpu.VMEM((D, CA), BF),
            pltpu.VMEM((D, CB), BF),
            pltpu.VMEM((2, GROUP, D), BF),
            pltpu.VMEM((GROUP, CB), BF),
            pltpu.VMEM((GROUP, CA), BF),
            pltpu.VMEM((GROUP, CA), F32),
            pltpu.VMEM((GROUP, CB), F32),
            pltpu.VMEM((2, 8, 128), F32),
            pltpu.VMEM((GROUP, 128), F32),
            pltpu.VMEM((GROUP, 128), F32),
            pltpu.VMEM((2, LEN, LEN), F32),
            pltpu.VMEM((TOK, D), F32),
            pltpu.VMEM((D // 128, TOK, 128), F32),
            pltpu.SemaphoreType.DMA((266,)),
            pltpu.SemaphoreType.DMA((266,)),
            pltpu.SemaphoreType.DMA((32,)),
        ],
        compiler_params=pltpu.CompilerParams(
            collective_id=0, has_side_effects=True, vmem_limit_bytes=62 * 2**20
        ),
    )(tiles, flips, tokens, cotangent, params, lengths, *weights)


SCATTER_ORDER = (
    ("P", 1), ("A", 1), ("B", 1), ("P", 0), ("R",), ("A", 0), ("B", 0), ("BR", 0, 0), ("S1", 1), ("BR", 0, 1),
    ("BR", 0, 2), ("BR", 0, 3), ("P", 2), ("A", 2), ("B", 2), ("S1", 0), ("X", 0), ("P", 3), ("A", 3),
    ("B", 3), ("BR", 1, 0), ("BR", 1, 1), ("T1", 0), ("S1", 2), ("BR", 1, 2), ("BR", 1, 3), ("X", 1),
    ("S1", 3), ("S2", 0), ("T2", 0), ("S2", 2), ("P", 4), ("S3", 0), ("B", 4), ("S2", 3), ("A", 4), ("T1", 1),
    ("P", 5), ("B", 5), ("A", 5), ("S3", 2), ("T3", 0), ("S1", 4), ("T2", 1), ("S3", 3), ("S2", 1), ("L", 0),
    ("S1", 5), ("L", 2), ("S2", 4), ("L", 3), ("S3", 1), ("T3", 1), ("N1",), ("S2", 5), ("S3", 4), ("L", 1),
    ("N2",), ("S3", 5), ("L", 4), ("N3",), ("L", 5),
)


def add_rows(dst, src, rows, cols):
    def step(g, carry):
        at = pl.ds(pl.multiple_of(g * 16, 16), 16)
        dst[at, cols] = (dst[at, cols].astype(F32) + src[at, cols].astype(F32)).astype(dst.dtype)
        return carry

    lax.fori_loop(0, rows // 16, step, 0)


def peers(me):
    x, y, z, c = me
    here, there = z * 4 + y, x * 2 + c
    plane, line = [], []
    for k in range(1, 16):
        at = (here + k) % 16
        plane.append(device(x, at % 4, at // 4, c))
    for k in range(1, 8):
        at = (there + k) % 8
        line.append(device(at // 2, y, z, at % 2))
    return here, there, plane, line


FEATS = 256


def scatter_kernel(
    tiles, flips, made, back, toks, wall_a, wall_b, tokens, gains,
    grad_a, grad_b, tok_out, norm_out, square_out,
    v_act, v_made, v_back, v_wall_a, v_wall_b, part_a, part_b, stage,
    r1_a, r1_b, r2_a, r2_b, t1_a, t1_b, t2_a, t2_b, sum_a, sum_b,
    own, core, x1, x2, norm1, norm2, square1, square2, shown, cotangent,
    send, recv, keep, load,
):
    me = x, y, z, c = place()
    xlo = x % 2
    wires = Wires(me, send, recv)
    parts, grads = (part_a, part_b), (grad_a, grad_b)
    r1, r2 = (r1_a, r1_b), (r2_a, r2_b)
    t1, t2, sums = (t1_a, t1_b), (t2_a, t2_b), (sum_a, sum_b)
    late = []
    here, there, plane, line = peers(me)

    def fetch(src, dst, sem):
        for side in range(2):
            for g in range(4):
                at = g * 256 + (c if side == 0 else 1 - c) * TOK
                pltpu.make_async_copy(
                    src.at[pl.ds(at, TOK)], dst.at[pl.ds(side * 512 + g * TOK, TOK)], load.at[sem]
                ).start()

    def fetched(dst, sem):
        pltpu.make_async_copy(dst, dst, load.at[sem]).wait()

    def wall_copy(i, f):
        wall, buf = ((wall_a, v_wall_a), (wall_b, v_wall_b))[i]
        return pltpu.make_async_copy(
            wall.at[pl.ds(f * FEATS, FEATS)], buf.at[f % 2], load.at[4 + 2 * i + f % 2]
        )

    own_rows = pl.ds(pl.multiple_of((xlo * 4 + x // 2 * 2 + c) * TOK, TOK), TOK)
    pltpu.make_async_copy(toks.at[pl.ds(1, 1), own_rows], cotangent, load.at[3]).start()
    fetch(toks.at[1], v_act, 0)
    fetch(made, v_made, 1)
    fetch(back, v_back, 2)
    for i in (1, 0):
        for f in range(2):
            wall_copy(i, f).start()

    barrier = pltpu.get_barrier_semaphore()
    for to in plane + line:
        pl.semaphore_signal(barrier, inc=1, device_id=to, device_id_type=MESH)
    pl.semaphore_wait(barrier, 22)
    axes = (("z+", "z-", "y+", "y-"), ("y+", "y-", "z+", "z-"))

    def spots(half):
        return (z, y) if half == 0 else (y, z)

    def piece(half, chunk, spot, start, size):
        i, c0, cn = chunk
        cols = pl.ds(c0, cn)
        if half == 0:
            return parts[i].at[0, spot, pl.ds(start, size), :, cols]
        return parts[i].at[1, pl.ds(start, size), spot, :, cols]

    state = {}

    def product(n):
        i, c0, cn = CHUNKS[n]
        right = (v_back, v_made)[i]

        def step(f, carry):
            feats = pl.ds(pl.multiple_of(f * 512, 512), 512)
            got = lax.dot_general(
                v_act[:, feats], right[:, pl.ds(c0, cn)], ROWS_DIMS, preferred_element_type=F32
            )
            at = pl.ds(f % 2 * 2, 2)
            parts[i][f // 2, at, :, :, pl.ds(c0, cn)] = got.astype(BF).reshape(2, 4, ROWS, cn)
            return carry

        lax.fori_loop(0, D // 512, step, 0)

    def branch(k, blocks):
        i = 1 - k
        left, buf = (v_back, v_made)[i], (v_wall_a, v_wall_b)[i]
        for f in blocks:
            wall_copy(i, f).wait()
            feats = pl.ds(f * FEATS, FEATS)
            for side in range(2):
                got = lax.dot_general(
                    left[pl.ds(side * 512, 512), :], buf[f % 2], COLS_DIMS, preferred_element_type=F32
                )
                got = got.astype(BF).reshape(2, 2, TOK, FEATS)
                if side == 0:
                    own[k, :, :, :, feats] = got
                else:
                    stage[:, :, :, feats] = got
            if f + 2 < D // FEATS:
                wall_copy(i, f + 2).start()

    def cross(k):
        state["c", k] = wires.push(stage, core.at[k], "c")

    def stage0(n, half):
        chunk = i, c0, cn = CHUNKS[n]
        p, q = spots(half)
        up, down = axes[half][:2]
        cols = pl.ds(c0, cn)
        state["a", n, half, 0] = wires.push(
            piece(half, chunk, (p + 2) % 4, 0, 2), r1[i].at[half, 0, :, :, cols], up
        )
        state["a", n, half, 1] = wires.push(
            piece(half, chunk, (p + 2) % 4, 2, 2), r1[i].at[half, 1, :, :, cols], down
        )

    def stage0b(n, half):
        chunk = i, c0, cn = CHUNKS[n]
        p, q = spots(half)
        up, down = axes[half][:2]
        cols = pl.ds(c0, cn)
        state["b", n, half, 0] = wires.push(
            piece(half, chunk, (p + 1) % 4, 2, 2), r2[i].at[half, 0, pl.ds(2, 2), :, cols], up
        )
        state["b", n, half, 1] = wires.push(
            piece(half, chunk, (p + 3) % 4, 0, 2), r2[i].at[half, 1, pl.ds(0, 2), :, cols], down
        )

    def stage1(n, half):
        chunk = i, c0, cn = CHUNKS[n]
        cols = pl.ds(c0, cn)
        p, q = spots(half)
        for d in range(2):
            state["a", n, half, d].wait_recv()
            spot = (p + 1) % 4 if d == 0 else (p + 3) % 4
            for m in range(2):
                block = 2 * d + m
                mine = parts[i].at[0, spot, block] if half == 0 else parts[i].at[1, block, spot]
                add_rows(mine, r1[i].at[half, d, m], ROWS, cols)
            state["s", n, half, d] = wires.push(
                piece(half, chunk, spot, 2 * d, 2), r2[i].at[half, d, pl.ds(2 * d, 2), :, cols], axes[half][d]
            )

    def kept(i, half, p, q):
        return parts[i].at[0, p, q] if half == 0 else parts[i].at[1, q, p]

    def stage2(n, half):
        i, c0, cn = CHUNKS[n]
        cols = pl.ds(c0, cn)
        p, q = spots(half)
        up, down = axes[half][2:]
        for d in range(2):
            state["b", n, half, d].wait_recv()
            state["s", n, half, d].wait_recv()

        def step(g, carry):
            at = pl.ds(pl.multiple_of((g % 4) * 16, 16), 16)
            m = g // 4
            mine = kept(i, half, p, m)
            total = (
                mine[at, cols].astype(F32)
                + r2[i][half, 0, m, at, cols].astype(F32)
                + r2[i][half, 1, m, at, cols].astype(F32)
            )
            mine[at, cols] = total.astype(BF)
            return carry

        lax.fori_loop(0, 16, step, 0)
        lo, hi = pl.ds(0, ROWS // 2), pl.ds(ROWS // 2, ROWS // 2)
        far = kept(i, half, p, (q + 2) % 4)
        state["t", n, half, 0] = wires.push(far.at[lo, cols], t1[i].at[half, 0, :, cols], up)
        state["t", n, half, 1] = wires.push(far.at[hi, cols], t1[i].at[half, 1, :, cols], down)
        state["u", n, half, 0] = wires.push(
            kept(i, half, p, (q + 1) % 4).at[hi, cols], t2[i].at[half, 0, hi, cols], up
        )
        state["u", n, half, 1] = wires.push(
            kept(i, half, p, (q + 3) % 4).at[lo, cols], t2[i].at[half, 1, lo, cols], down
        )

    def stage3(n, half):
        i, c0, cn = CHUNKS[n]
        cols = pl.ds(c0, cn)
        p, q = spots(half)
        for d in range(2):
            state["t", n, half, d].wait_recv()
            rows = pl.ds(d * (ROWS // 2), ROWS // 2)
            mine = kept(i, half, p, (q + 1) % 4 if d == 0 else (q + 3) % 4).at[rows]
            add_rows(mine, t1[i].at[half, d], ROWS // 2, cols)
            state["v", n, half, d] = wires.push(
                mine.at[:, cols], t2[i].at[half, d, rows, cols], axes[half][2 + d]
            )

    def stage4(n, half):
        i, c0, cn = CHUNKS[n]
        cols = pl.ds(c0, cn)
        p, q = spots(half)
        for d in range(2):
            state["u", n, half, d].wait_recv()
            state["v", n, half, d].wait_recv()
        mine = kept(i, half, p, q)

        def step(g, carry):
            at = pl.ds(pl.multiple_of(g * 16, 16), 16)
            total = (
                mine[at, cols].astype(F32)
                + t2[i][half, 0, at, cols].astype(F32)
                + t2[i][half, 1, at, cols].astype(F32)
            )
            sums[i][half, at, cols] = total
            squares = total * total
            for m in range(cn // 128):
                part = squares[:, m * 128 : m * 128 + 128]
                carry = carry + part[:8] + part[8:]
            return carry

        return lax.fori_loop(0, ROWS // 16, step, jnp.zeros((8, 128), F32))

    def stage5(n):
        i, c0, cn = CHUNKS[n]
        cols = pl.ds(c0, cn)
        state["g", n] = wires.push(sums[i].at[1 - xlo, :, cols], grads[i].at[xlo, :, cols], "p")
        copy = pltpu.make_async_copy(sums[i].at[xlo, :, cols], grads[i].at[xlo, :, cols], keep.at[n])
        copy.start()
        late.append(copy)

    half_tok = TOK // 2

    def tokens1(k):
        state["c", k].wait_recv()

        def step(g, carry):
            at = pl.ds(pl.multiple_of((g % 8) * 16, 16), 16)
            s = g // 8
            own[k, s // 2, s % 2, at, :] = (
                own[k, s // 2, s % 2, at, :].astype(F32) + core[k, s // 2, s % 2, at, :].astype(F32)
            ).astype(BF)
            return carry

        lax.fori_loop(0, 32, step, 0)

        def spot(s, d, far):
            rows = pl.ds((d if far else 1 - d) * half_tok, half_tok)
            return own.at[k, s % 2, s // 2, rows]

        for d, name in enumerate(("x+", "x-")):
            state["x1", k, d] = wires.push(spot((x + 2) % 4, d, True), x1.at[k, d], name)
        for d, name in enumerate(("x+", "x-")):
            to = (x + 1) % 4 if d == 0 else (x + 3) % 4
            rows = pl.ds((1 - d) * half_tok, half_tok)
            state["x2", k, d] = wires.push(spot(to, d, False), x2.at[k, d, rows], name)

    def tokens2(k):
        for d, name in enumerate(("x+", "x-")):
            state["x1", k, d].wait_recv()
            to = (x + 1) % 4 if d == 0 else (x + 3) % 4
            rows = pl.ds(d * half_tok, half_tok)
            mine = own.at[k, to % 2, to // 2, rows]
            add_rows(mine, x1.at[k, d], half_tok, pl.ds(0, D))
            state["x3", k, d] = wires.push(mine, x2.at[k, d, rows], name)

    def tokens3(k):
        for d in range(2):
            state["x2", k, d].wait_recv()
            state["x3", k, d].wait_recv()

        def total(at):
            return (
                own[k, xlo, x // 2, at, :].astype(F32)
                + x2[k, 0, at, :].astype(F32)
                + x2[k, 1, at, :].astype(F32)
            )

        def result(g, carry):
            at = pl.ds(pl.multiple_of(g * 16, 16), 16)
            stage_tiles(shown, tokens[at, :].astype(F32) + total(at), at)
            return carry

        def gradient(g, carry):
            at = pl.ds(pl.multiple_of(g * 16, 16), 16)
            inputs = tokens[at, :].astype(F32)
            centered = inputs - jnp.mean(inputs, -1, keepdims=True)
            variance = jnp.mean(centered * centered, -1, keepdims=True)
            deviation = lax.rsqrt(variance + NORM_EPSILON)
            standard = centered * deviation
            d_normed = total(at)
            d_standard = d_normed * gains[0:1, :]
            gradient_rows = cotangent[0, at, :].astype(F32) + deviation * (
                d_standard
                - jnp.mean(d_standard, -1, keepdims=True)
                - standard * jnp.mean(d_standard * standard, -1, keepdims=True)
            )
            stage_tiles(shown, gradient_rows, at)
            return (
                carry[0] + jnp.sum(d_normed * standard, 0, keepdims=True),
                carry[1] + jnp.sum(d_normed, 0, keepdims=True),
            )

        if k == 0:
            lax.fori_loop(0, TOK // 16, result, 0)
        else:
            zero = jnp.zeros((1, D), F32)
            gain_sum, shift_sum = lax.fori_loop(0, TOK // 16, gradient, (zero, zero))
            norm1[here, 0:1, :] = gain_sum
            norm1[here, 1:2, :] = shift_sum

        def show(cols, value):
            tok_out[k, :, cols] = value.astype(BF)

        reorder(shown, 1, tiles, flips, show)

    def small1(slots):
        return [wires.push(slots.at[here], slots.at[here], to) for to in plane]

    def small2(copies, slots, after):
        for copy in copies:
            copy.wait_recv()
        total = slots[0]
        for k in range(1, 16):
            total = total + slots[k]
        after[there] = total
        return [wires.push(after.at[there], after.at[there], to) for to in line]

    def small3(copies, after):
        for copy in copies:
            copy.wait_recv()
        total = after[0]
        for k in range(1, 8):
            total = total + after[k]
        return total

    def both(step, n):
        for half in range(2):
            step(n, half)

    squares = [jnp.zeros((8, 128), F32)]

    def last(n):
        for half in range(2):
            squares[0] = squares[0] + stage4(n, half)
        stage5(n)

    fetched(v_act, 0)
    fetched(v_made, 1)
    fetched(cotangent, 3)
    waiting = [True]
    norm_copies = [None]

    def next_product(n):
        if CHUNKS[n][0] == 0 and waiting[0]:
            waiting[0] = False
            fetched(v_act, 0)
            fetched(v_back, 2)
        product(n)

    def some_branch(k, j):
        if k == 1 and j == 0:
            if waiting[0]:
                fetched(v_back, 2)
                waiting[0] = False
                fetched(v_act, 0)
            state["c", 0].wait_send()
            wires.open = [copy for copy in wires.open if copy is not state["c", 0]]
        branch(k, range(2 * j, 2 * j + 2))

    def norm_step(number):
        if number == 1:
            norm_copies[0] = small1(norm1)
        elif number == 2:
            norm_copies[0] = small2(norm_copies[0], norm1, norm2)
        else:
            stage_tiles(shown, small3(norm_copies[0], norm2), pl.ds(0, 2))

            def show_norm(cols, value):
                norm_out[:, cols] = value

            reorder(shown, 1, tiles, flips, show_norm, 8)

    steps = {
        "P": next_product,
        "R": lambda: fetch(toks.at[0], v_act, 0),
        "A": lambda n: both(stage0, n),
        "B": lambda n: both(stage0b, n),
        "S1": lambda n: both(stage1, n),
        "S2": lambda n: both(stage2, n),
        "S3": lambda n: both(stage3, n),
        "L": last,
        "BR": some_branch,
        "X": cross,
        "T1": tokens1,
        "T2": tokens2,
        "T3": tokens3,
        "N1": lambda: norm_step(1),
        "N2": lambda: norm_step(2),
        "N3": lambda: norm_step(3),
    }
    for name, *at in SCATTER_ORDER:
        if (name, *at) == SCATTER_ORDER[-1]:
            wires.close(140)
        steps[name](*at)
    square1[here] = squares[0]
    square_copies = small1(square1)
    square_copies = small2(square_copies, square1, square2)
    square_out[...] = small3(square_copies, square2)
    for n in range(len(CHUNKS)):
        state["g", n].wait_recv()
    wires.close()
    for copy in late:
        copy.wait()


def scatter_all(tiles, flips, made, back, toks, wall_a, wall_b, tokens, gains):
    any_ = pl.BlockSpec(memory_space=pl.ANY)
    vmem = pl.BlockSpec(memory_space=pltpu.VMEM)

    def both(*shape, dtype=BF):
        return [pltpu.VMEM(shape + (CA,), dtype), pltpu.VMEM(shape + (CB,), dtype)]

    return pl.pallas_call(
        scatter_kernel,
        out_shape=(
            jax.ShapeDtypeStruct((2, ROWS, CA), F32),
            jax.ShapeDtypeStruct((2, ROWS, CB), F32),
            jax.ShapeDtypeStruct((2, TOK, D), BF),
            jax.ShapeDtypeStruct((8, D), F32),
            jax.ShapeDtypeStruct((8, 128), F32),
        ),
        in_specs=[pl.BlockSpec(memory_space=pltpu.SMEM), vmem] + [any_] * 5 + [vmem] * 2,
        out_specs=(any_, any_, vmem, vmem, vmem),
        scratch_shapes=[
            pltpu.VMEM((GROUP, D), BF),
            pltpu.VMEM((GROUP, CB), BF),
            pltpu.VMEM((GROUP, CA), BF),
            pltpu.VMEM((2, FEATS, CA), BF),
            pltpu.VMEM((2, FEATS, CB), BF),
            *both(2, 4, 4, ROWS),
            pltpu.VMEM((2, 2, TOK, D), BF),
            *both(2, 2, 2, ROWS),
            *both(2, 2, 4, ROWS),
            *both(2, 2, ROWS // 2),
            *both(2, 2, ROWS),
            *both(2, ROWS, dtype=F32),
            pltpu.VMEM((2, 2, 2, TOK, D), BF),
            pltpu.VMEM((2, 2, 2, TOK, D), BF),
            pltpu.VMEM((2, 2, TOK // 2, D), BF),
            pltpu.VMEM((2, 2, TOK, D), BF),
            pltpu.VMEM((16, 2, D), F32),
            pltpu.VMEM((8, 2, D), F32),
            pltpu.VMEM((16, 8, 128), F32),
            pltpu.VMEM((8, 8, 128), F32),
            pltpu.VMEM((D // 128, TOK, 128), F32),
            pltpu.VMEM((1, TOK, D), BF),
            pltpu.SemaphoreType.DMA((224,)),
            pltpu.SemaphoreType.DMA((224,)),
            pltpu.SemaphoreType.DMA((8,)),
            pltpu.SemaphoreType.DMA((8,)),
        ],
        compiler_params=pltpu.CompilerParams(
            collective_id=1, has_side_effects=True, vmem_limit_bytes=62 * 2**20
        ),
    )(tiles, flips, made, back, toks, wall_a, wall_b, tokens, gains)


def halves(item):
    high = item.astype(BF)
    return high, (item - high.astype(F32)).astype(BF)


def near_product(left, right, dims):
    (a, a_low), (b, b_low) = left, right
    axis = 0 if dims == (((1,), (0,)), ((), ())) else 1
    return lax.dot_general(
        jnp.concatenate([a, a, a_low], 1),
        jnp.concatenate([b, b_low, b], axis),
        dims,
        preferred_element_type=F32,
    )


def update_kernel(tok, squares, norm_raw, norm_params, norm_moment1, norm_moment2, grad_a, grad_b, *refs):
    ins, refs = refs[:20], refs[20:]
    out, input_grad, grad_norm, norm_grads, norm_first, norm_second, norm_new = refs[:7]
    outs, v_ins, v_outs, came, left = refs[7:27], refs[27:47], refs[47:67], refs[67], refs[68]
    weights, firsts, seconds, bases = v_ins[0:5], v_ins[5:10], v_ins[10:15], v_ins[15:20]
    grads, firsts_new, seconds_new, weights_new = v_outs[0:5], v_outs[5:10], v_outs[10:15], v_outs[15:20]
    parts = (grad_a, grad_b)
    order = (2, 0, 3, 4, 1)
    arriving = {}
    for i in order:
        for k in range(4):
            n = 5 * k + i
            arriving[i, k] = pltpu.make_async_copy(ins[n], v_ins[n], came.at[n])
            arriving[i, k].start()
    out[...] = tok[0]
    input_grad[...] = tok[1]
    leaving = []
    left_lanes = lax.broadcasted_iota(jnp.int32, (1, 128), 1) < 64

    def whole(item):
        return jnp.sum(jnp.sum(item, 0, keepdims=True), 1, keepdims=True)

    raw = norm_raw[0:2, :]
    length = jnp.sqrt(whole(squares[...]) + whole(raw * raw))
    clip = jnp.minimum(1.0, CLIP_LIMIT / length)
    grad_norm[...] = length
    norm_grads[...] = clip * raw
    norm_first[...], norm_second[...], norm_new[...] = adam_plain(
        norm_params[...], clip * raw, norm_moment1[...], norm_moment2[...], NORM_RATE
    )

    def fetch(piece, side):
        i, half, column = piece
        tile = parts[i][half, :, pl.ds(column // 128 * 128, 128)]
        return tile if column // 64 % 2 == side else pltpu.roll(tile, 64, 1)

    tables = pieces()
    for i in order:
        table = tables[i]
        for k in range(4):
            arriving[i, k].wait()
        blocks = range(WIDTHS[i] // 128)
        for group in (blocks[at : at + 4] for at in range(0, len(blocks), 4)):
            bases_of = [halves(bases[i][block]) for block in group]
            clipped = []
            for block in group:
                one, two = table[2 * block], table[2 * block + 1]
                if two == one[:2] + (one[2] + 64,) and one[2] % 128 == 0:
                    grad = parts[one[0]][one[1], :, pl.ds(one[2], 128)]
                else:
                    grad = jnp.where(left_lanes, fetch(one, 0), fetch(two, 1))
                clipped.append(clip * grad)
            turned = [
                near_product(halves(grad), basis, (((1,), (0,)), ((), ())))
                for grad, basis in zip(clipped, bases_of)
            ]
            ratios = []
            for block, grad, item in zip(group, clipped, turned):
                cols = pl.ds(block * 128, 128)
                first = BETA_ONE * firsts[i][:, cols] + (1.0 - BETA_ONE) * item
                second = BETA_TWO * seconds[i][:, cols] + (1.0 - BETA_TWO) * item * item
                grads[i][:, cols] = grad
                firsts_new[i][:, cols] = first
                seconds_new[i][:, cols] = second
                ratios.append(
                    first
                    * (1.0 / (1.0 - BETA_ONE**STEP))
                    / (jnp.sqrt(second * (1.0 / (1.0 - BETA_TWO**STEP))) + ADAM_EPS)
                )
            turned_back = [
                near_product(halves(ratio), basis, COLS_DIMS) for ratio, basis in zip(ratios, bases_of)
            ]
            for block, item in zip(group, turned_back):
                cols = pl.ds(block * 128, 128)
                weight = weights[i][:, cols]
                weights_new[i][:, cols] = weight - RATE_LIST[i] * (item + WEIGHT_DECAY * weight)
        for k in range(4):
            n = 5 * k + i
            copy = pltpu.make_async_copy(v_outs[n], outs[n], left.at[n])
            copy.start()
            leaving.append(copy)
    for copy in leaving:
        copy.wait()


def update(tok, squares, norm, grad_a, grad_b, weights, firsts, seconds, bases):
    vmem = pl.BlockSpec(memory_space=pltpu.VMEM)
    any_ = pl.BlockSpec(memory_space=pl.ANY)
    shapes = [jax.ShapeDtypeStruct((ROWS, width), F32) for width in WIDTHS]
    small = [jax.ShapeDtypeStruct((TOK, D), BF)] * 2
    small += [jax.ShapeDtypeStruct((1, 1), F32)] + [jax.ShapeDtypeStruct((2, D), F32)] * 4
    state = (*weights, *firsts, *seconds, *bases)
    return pl.pallas_call(
        update_kernel,
        out_shape=tuple(small + shapes * 4),
        in_specs=[vmem] * 8 + [any_] * 20,
        out_specs=(vmem,) * 7 + (any_,) * 20,
        scratch_shapes=[pltpu.VMEM(item.shape, F32) for item in state]
        + [pltpu.VMEM(item.shape, F32) for item in shapes * 4]
        + [pltpu.SemaphoreType.DMA((20,))] * 2,
        compiler_params=pltpu.CompilerParams(vmem_limit_bytes=56 * 2**20),
    )(tok, squares, *norm, grad_a, grad_b, *state)


def adam_plain(param, grad, first, second, rate):
    first_new = BETA_ONE * first + (1.0 - BETA_ONE) * grad
    second_new = BETA_TWO * second + (1.0 - BETA_TWO) * grad * grad
    ratio = (
        first_new
        / (1.0 - BETA_ONE**STEP)
        / (jnp.sqrt(second_new / (1.0 - BETA_TWO**STEP)) + ADAM_EPS)
    )
    return (first_new, second_new, param - rate * ratio)


def body(
    tokens,
    cotangent,
    doc_lengths,
    row_owner,
    norm_params,
    norm_moment1,
    norm_moment2,
    qkv_weight,
    out_weight,
    gate_weight,
    up_weight,
    down_weight,
    qkv_moment1,
    out_moment1,
    gate_moment1,
    up_moment1,
    down_moment1,
    qkv_moment2,
    out_moment2,
    gate_moment2,
    up_moment2,
    down_moment2,
    qkv_basis,
    out_basis,
    gate_basis,
    up_basis,
    down_basis,
):
    blocks = jnp.arange(32, dtype=jnp.int32)
    inverse = jnp.sum((row_owner[None, :] == blocks[:, None]) * blocks[None, :], 1)
    tiles, flips = places(jnp.stack([inverse, row_owner]))
    weights = (qkv_weight, out_weight, gate_weight, up_weight, down_weight)
    wall_a, wall_b, toks, made, back, tokens_stored, params_stored = gather_all(
        tiles, flips, tokens, cotangent, norm_params, doc_lengths, weights
    )
    grad_a, grad_b, tok_out, norm_raw, squares = scatter_all(
        tiles, flips, made, back, toks, wall_a, wall_b, tokens_stored, params_stored
    )
    firsts = (qkv_moment1, out_moment1, gate_moment1, up_moment1, down_moment1)
    seconds = (qkv_moment2, out_moment2, gate_moment2, up_moment2, down_moment2)
    bases = (qkv_basis, out_basis, gate_basis, up_basis, down_basis)
    norm = (norm_raw, norm_params, norm_moment1, norm_moment2)
    out, input_grad, grad_norm, *rest = update(
        tok_out, squares, norm, grad_a, grad_b, weights, firsts, seconds, bases
    )
    return (out, input_grad, grad_norm[0, 0], *rest)


def solution(mesh):
    tok, weight, whole = P(("dp", "mp"), None), P("dp", "mp"), P()
    in_specs = (tok, tok, P("dp", None)) + (whole,) * 4 + (weight,) * 15 + (P("mp", None, None),) * 5
    out_specs = (tok, tok) + (whole,) * 5 + (weight,) * 20
    return jax.shard_map(body, mesh=mesh, in_specs=in_specs, out_specs=out_specs, check_vma=False)
```
